32 devices in a mesh: seq: 16 (over z, y, core), fsdp: 2 (over x).
Axes of the slice: x: 2, y: 2, z: 4, core: 2. Of those that a mesh axis runs over, the one named last changes fastest.
Arguments:
- tokens: bfloat16 [2, 3072, 1536], P('fsdp', 'seq'), may hold values from -6 to 6
- norm1_gain: bfloat16 [1536], P('seq'), may hold values from 0.099609375 to 1.8984375
- in_weight: bfloat16 [1536, 3, 1536], P('seq', None, 'fsdp'), may hold values from -0.15625 to 0.15625
- conv_kernel: bfloat16 [1536, 3], P('seq'), may hold values from -3.5 to 3.5
- out_weight: bfloat16 [1536, 1536], P('seq', 'fsdp'), may hold values from -0.15625 to 0.15625
- norm2_gain: bfloat16 [1536], P('seq'), may hold values from 0.099609375 to 1.8984375
- gate_weight: bfloat16 [1536, 6912], P('seq', 'fsdp'), may hold values from -0.15625 to 0.15625
- up_weight: bfloat16 [1536, 6912], P('seq', 'fsdp'), may hold values from -0.15625 to 0.15625
- down_weight: bfloat16 [1536, 6912], P('seq', 'fsdp'), may hold values from -0.109375 to 0.109375
- d_out: bfloat16 [2, 3072, 1536], P('fsdp', 'seq'), may hold values from -6 to 6
Outputs:
- result: bfloat16 [2, 3072, 1536], P('fsdp', 'seq')
- d_tokens: bfloat16 [2, 3072, 1536], P('fsdp', 'seq')
- d_norm1_gain: float32 [1536], P('seq')
- d_in_weight: float32 [1536, 3, 1536], P('seq', None, 'fsdp')
- d_conv_kernel: float32 [1536, 3], P('seq')
- d_out_weight: float32 [1536, 1536], P('seq', 'fsdp')
- d_norm2_gain: float32 [1536], P('seq')
- d_gate_weight: float32 [1536, 6912], P('seq', 'fsdp')
- d_up_weight: float32 [1536, 6912], P('seq', 'fsdp')
- d_down_weight: float32 [1536, 6912], P('seq', 'fsdp')
The draws below stay inside these ranges and needn't reach their ends.
All inputs are finite; a program needn't handle non-finite values.
Results may differ from the reference program's by a relative error of at most 0.012.
Values may be sent and summed in bfloat16 or wider, within the bound.
A program may use at most 576 MiB of HBM per device.

```python
import jax
import jax.numpy as jnp
from jax import lax

D = 1536
FF = 6912
KW = 3
SEQS = 3
GROUP_TOK = 3072
SEQ_LEN = 1024
GROUPS = 2


def level_of(stream_key, dims, shards, low, largest):
    def one(axis_at, blocks):
        steps = jax.random.uniform(jax.random.fold_in(jax.random.fold_in(stream_key, 6), axis_at), (blocks,), jnp.float32, low / len(shards), largest / len(shards))
        return jnp.repeat(jnp.exp(steps), dims[axis_at] // blocks).reshape((-1,) + (1,) * (len(dims) - axis_at - 1))

    factor_of = one(*shards[0])
    for cut in shards[1:]:
        factor_of = factor_of * one(*cut)
    return factor_of


def bell_draw(rng, dims, deviation, bound, cuts=(), kind=jnp.bfloat16):
    drawn = jax.random.normal(rng, dims, jnp.float32) * deviation
    if len(cuts) > 0:
        drawn = level_of(rng, dims, cuts, -0.22, 0.18) * drawn
    return jnp.clip(drawn, min=-bound, max=bound).astype(kind)


def setup_inputs(seed: int = 0) -> dict:
    keys = jax.random.split(jax.random.key(seed), 11)
    return {
        "tokens": bell_draw(keys[0], (GROUPS, GROUP_TOK, D), 1.0, 6.0, ((0, 2), (1, 16))),
        "norm1_gain": jnp.clip(1.0 + 0.18 * jax.random.normal(keys[1], (D,), jnp.float32), 0.099609375, 1.8984375).astype(jnp.bfloat16),
        "in_weight": bell_draw(keys[2], (D, 3, D), D ** -0.5, 0.15625, ((0, 16), (2, 2))),
        "conv_kernel": bell_draw(keys[3], (D, KW), KW ** -0.5, 3.5, ((0, 16),)),
        "out_weight": bell_draw(keys[4], (D, D), D ** -0.5, 0.15625, ((0, 16), (1, 2))),
        "norm2_gain": jnp.clip(1.0 + 0.18 * jax.random.normal(keys[5], (D,), jnp.float32), 0.099609375, 1.8984375).astype(jnp.bfloat16),
        "gate_weight": bell_draw(keys[6], (D, FF), D ** -0.5, 0.15625, ((0, 16), (1, 2))),
        "up_weight": bell_draw(keys[7], (D, FF), D ** -0.5, 0.15625, ((0, 16), (1, 2))),
        "down_weight": bell_draw(keys[8], (D, FF), (FF // 2) ** -0.5, 0.109375, ((0, 16), (1, 2))),
        "d_out": bell_draw(keys[9], (GROUPS, GROUP_TOK, D), 1.0, 6.0, ((0, 2), (1, 16))),
    }


EPSILON = 1e-05

@jax.custom_vjp
def low(v):
    return lax.optimization_barrier(v.astype(jnp.bfloat16)).astype(jnp.float32)

@jax.custom_vjp
def low_back(v):
    return v

def low_keep(v):
    return (low(v), None)

def low_pass(kept, grad):
    return (grad,)

def back_keep(v):
    return (v, None)

def back_low(kept, grad):
    return (low(grad),)
low.defvjp(low_keep, low_pass)
low_back.defvjp(back_keep, back_low)

def exact_dot(left, right):
    return jnp.dot(left, right, precision=lax.Precision.HIGHEST)

def root_norm(hidden, gain):
    scale = lax.rsqrt(lax.optimization_barrier(jnp.mean(hidden * hidden, axis=-1, keepdims=True)) + EPSILON)
    return hidden * scale * gain

def causal_conv(gated, kernel):
    taps = kernel.shape[1]
    length = gated.shape[0]
    padded = jnp.concatenate([jnp.zeros((taps - 1, gated.shape[1]), gated.dtype), gated], axis=0)
    total = jnp.zeros_like(gated)
    for offset in range(taps):
        total = total + padded[offset:offset + length] * kernel[:, offset]
    return total

def block_layer(hidden, weights):
    gain_one, w_in, kernel, w_out, gain_two, w_gate, w_up, w_down = weights
    width = hidden.shape[1]
    normed = low(root_norm(hidden, gain_one))
    projected = low_back(exact_dot(normed, w_in.reshape(width, 3 * width)))
    b_part = projected[:, :width]
    c_part = projected[:, width:2 * width]
    x_part = projected[:, 2 * width:]
    gated = low(b_part * x_part)
    mixed = low(c_part * causal_conv(gated, kernel))
    hidden_one = hidden + low_back(exact_dot(mixed, w_out.T))
    normed_two = low(root_norm(hidden_one, gain_two))
    gate = low_back(exact_dot(normed_two, w_gate))
    upper = low_back(exact_dot(normed_two, w_up))
    active = low(jax.nn.silu(gate) * upper)
    return hidden_one + low_back(exact_dot(active, w_down.T))

def reference(tokens, norm1_gain, in_weight, conv_kernel, out_weight, norm2_gain, gate_weight, up_weight, down_weight, d_out):
    weights = tuple((item.astype(jnp.float32) for item in (norm1_gain, in_weight, conv_kernel, out_weight, norm2_gain, gate_weight, up_weight, down_weight)))
    sequences = tokens.astype(jnp.float32).reshape(GROUPS * SEQS, SEQ_LEN, D)
    cotangent = d_out.astype(jnp.float32).reshape(GROUPS * SEQS, SEQ_LEN, D)

    def step(totals, item):
        sequence, seq_cot = item
        output, pullback = jax.vjp(block_layer, sequence, weights)
        d_sequence, d_weights = pullback(seq_cot)
        totals = jax.tree.map(lambda left, right: left + right, totals, d_weights)
        return (totals, (output, d_sequence))
    zeros = jax.tree.map(jnp.zeros_like, weights)
    grads, (outputs, d_sequences) = lax.scan(step, zeros, (sequences, cotangent))
    result = outputs.reshape(GROUPS, GROUP_TOK, D).astype(jnp.bfloat16)
    d_tokens = d_sequences.reshape(GROUPS, GROUP_TOK, D).astype(jnp.bfloat16)
    return (result, d_tokens, grads[0], grads[1], grads[2], grads[3], grads[4], grads[5], grads[6], grads[7])
```

```python
import jax
import jax.numpy as jnp
from jax import lax
from jax.sharding import PartitionSpec as P

SEQS = 3
EPSILON = 1e-05
BOTH = ("seq", "fsdp")


def times_transposed(left, right):
    return lax.dot_general(
        left, right, (((1,), (1,)), ((), ())), preferred_element_type=jnp.float32
    )


def transposed_times(left, right):
    return lax.dot_general(
        left, right, (((0,), (0,)), ((), ())), preferred_element_type=jnp.float32
    )


def times(left, right):
    return jnp.dot(left, right, preferred_element_type=jnp.float32)


def root_norm(hidden, gain):
    scale = lax.rsqrt(jnp.mean(hidden * hidden, axis=-1, keepdims=True) + EPSILON)
    return (hidden * scale * gain, scale)


def norm_back(grad, hidden, scale, gain):
    weighted = grad * gain
    inner = jnp.sum(weighted * hidden, axis=-1, keepdims=True)
    d_hidden = scale * weighted - hidden * (scale * scale * scale) * inner / hidden.shape[-1]
    d_gain = jnp.sum(grad * hidden * scale, axis=0)
    return (d_hidden, d_gain)


def device(z, y, c, x):
    return (z * 4 + y * 2 + c) * 2 + x


def every(planes):
    return [
        (z, y, c, x) for z in range(planes) for y in range(2) for c in range(2) for x in range(2)
    ]


def on_device(
    tokens,
    norm1_gain,
    in_weight,
    conv_kernel,
    out_weight,
    norm2_gain,
    gate_weight,
    up_weight,
    down_weight,
    d_out,
):
    planes = lax.axis_size("seq") // 4
    here = lax.axis_index("seq")
    y, c, x = (here // 2) % 2, here % 2, lax.axis_index("fsdp")
    z = here // 4
    rows, width = tokens.shape[1:]
    share = gate_weight.shape[0]
    plane_groups = [
        [device(z, y, c, x) for x in range(2) for y in range(2)]
        for z in range(planes)
        for c in range(2)
    ]
    column_groups = [
        [z * 4 + y * 2 + c for z in range(planes) for c in range(2)] for y in range(2)
    ]
    members = 2 * planes

    def moved(value, target):
        pairs = []
        for place in every(planes):
            to = target(*place)
            if to is not None:
                pairs.append((device(*place), device(*to)))
        return lax.ppermute(value, BOTH, pairs)

    def swap_y(value):
        return moved(value, lambda z, y, c, x: (z, 1 - y, c, x))

    def swap_x(value):
        return moved(value, lambda z, y, c, x: (z, y, c, 1 - x))

    def swap_both(value):
        return moved(value, lambda z, y, c, x: (z, 1 - y, c, 1 - x))

    def ordered(first, second, flag):
        return jnp.where(flag == 0, jnp.stack([first, second]), jnp.stack([second, first]))

    def plane_gather(value):
        by_y = ordered(value, swap_y(value), y)
        other = ordered(swap_x(value), swap_both(value), y)
        return ordered(by_y, other, x).reshape((4 * value.shape[0],) + value.shape[1:])

    def plane_sum(partial):
        sent = partial.astype(jnp.bfloat16).reshape(4, rows, width)
        got = lax.all_to_all(sent, BOTH, 0, 0, axis_index_groups=plane_groups, tiled=True)
        return jnp.sum(got.astype(jnp.float32), axis=0)

    def fetch(weight):
        halves = weight.reshape(share, 2, -1)
        mine = jnp.where(y == 0, halves[:, 0], halves[:, 1])
        theirs = jnp.where(y == 0, halves[:, 1], halves[:, 0])
        pair = ordered(mine, swap_y(theirs), y)
        got = lax.all_gather(pair, "seq", axis=0, tiled=False, axis_index_groups=column_groups)
        got = got.reshape(planes, 2, 2, share, -1)
        return jnp.swapaxes(got, 1, 2).reshape(width, -1)

    def give(grad):
        sent = grad.astype(jnp.bfloat16).reshape(planes, 2, 2, share, -1)
        sent = jnp.swapaxes(sent, 1, 2).reshape(members * 2, share, -1)
        got = lax.psum_scatter(
            sent, "seq", scatter_dimension=0, tiled=True, axis_index_groups=column_groups
        )
        mine = jnp.where(y == 0, got[0], got[1])
        theirs = jnp.where(y == 0, got[1], got[0])
        pair = ordered(mine, swap_y(theirs), y).astype(jnp.float32)
        return jnp.concatenate([pair[0], pair[1]], axis=1)

    gains = lax.all_gather(
        jnp.concatenate(
            [norm1_gain[:, None], norm2_gain[:, None], conv_kernel], axis=1
        ),
        "seq",
        axis=0,
        tiled=True,
    ).astype(jnp.float32)
    gain_one, gain_two, kernel = gains[:, 0], gains[:, 1], gains[:, 2:]
    taps = kernel.shape[1]
    margin = taps - 1
    channels = in_weight.shape[2] // 2
    first_channel = x * (2 * channels) + y * channels
    kernel_here = lax.dynamic_slice_in_dim(kernel, first_channel, channels, 0)

    w_in_halves = jnp.swapaxes(in_weight.reshape(share, 3, 2, channels), 1, 2)
    w_mixer = fetch(
        jnp.concatenate(
            [w_in_halves.reshape(share, 2, 3 * channels), out_weight.reshape(share, 2, channels)],
            axis=2,
        ).reshape(share, 8 * channels)
    )
    w_in, w_out = w_mixer[:, : 3 * channels], w_mixer[:, 3 * channels :]

    hidden = tokens[0].astype(jnp.float32)
    normed, scale_one = root_norm(hidden, gain_one)
    normed_low = plane_gather(normed.astype(jnp.bfloat16))
    grad_low = plane_gather(d_out[0])

    w_gate = fetch(gate_weight)
    w_up = fetch(up_weight)
    w_down = fetch(down_weight)

    projected = times(normed_low, w_in).reshape(2, 2, rows, 3 * channels)
    b_part = projected[..., :channels]
    c_part = projected[..., channels : 2 * channels]
    x_part = projected[..., 2 * channels :]
    gated = (b_part * x_part).astype(jnp.bfloat16)

    def swap_core(value):
        return moved(value, lambda z, y, c, x: (z, y, 1 - c, x))

    def to_next(value):
        return moved(
            value, lambda z, y, c, x: (z + 1, y, 0, x) if c == 1 and z + 1 < planes else None
        )

    def to_last(value):
        return moved(value, lambda z, y, c, x: (z - 1, y, 1, x) if c == 0 and z > 0 else None)

    tail = gated[:, :, rows - margin :]
    from_core, from_plane = swap_core(tail), to_next(tail[:, 1])
    before = jnp.where(
        c == 1, from_core, jnp.stack([from_plane, from_core[:, 0]], axis=1)
    )
    padded = jnp.concatenate([before, gated], axis=2).astype(jnp.float32)
    seq_len = lax.axis_size("seq") * rows // SEQS
    block = z * 4 + jnp.arange(2, dtype=jnp.int32) * 2 + c
    position = block[:, None] * rows + jnp.arange(rows, dtype=jnp.int32)
    in_sequence = position % seq_len
    masks = [
        (in_sequence >= margin - offset).astype(jnp.float32)[None, :, :, None]
        for offset in range(taps)
    ]
    conv = jnp.zeros_like(b_part)
    for offset in range(taps):
        conv = conv + masks[offset] * padded[:, :, offset : offset + rows] * kernel_here[:, offset]
    mixed = (c_part * conv).astype(jnp.bfloat16).reshape(4 * rows, channels)
    hidden_one = hidden + plane_sum(times_transposed(mixed, w_out))

    normed_two, scale_two = root_norm(hidden_one, gain_two)
    normed_two_low = plane_gather(normed_two.astype(jnp.bfloat16))
    gate = times(normed_two_low, w_gate)
    upper = times(normed_two_low, w_up)
    sigma = jax.nn.sigmoid(gate)
    active = (gate * sigma * upper).astype(jnp.bfloat16)
    d_active = times(grad_low, w_down)
    d_upper = (d_active * gate * sigma).astype(jnp.bfloat16)
    d_gate = (d_active * upper * sigma * (1.0 + gate * (1.0 - sigma))).astype(jnp.bfloat16)
    d_normed_two = plane_sum(times_transposed(d_gate, w_gate) + times_transposed(d_upper, w_up))
    result = hidden_one + plane_sum(times_transposed(active, w_down))
    d_gate_w = give(transposed_times(normed_two_low, d_gate))
    d_up_w = give(transposed_times(normed_two_low, d_upper))
    d_down_w = give(transposed_times(grad_low, active))

    d_hidden_two, d_gain_two = norm_back(d_normed_two, hidden_one, scale_two, gain_two)
    grad_one = d_out[0].astype(jnp.float32) + d_hidden_two
    grad_one_low = plane_gather(grad_one.astype(jnp.bfloat16))
    d_out_w = transposed_times(grad_one_low, mixed)
    d_mixed = times(grad_one_low, w_out).reshape(2, 2, rows, channels)
    d_c = d_mixed * conv
    d_conv = d_mixed * c_part
    kernel_cols = []
    d_padded = jnp.zeros((2, 2, rows + margin, channels), jnp.float32)
    for offset in range(taps):
        masked = masks[offset] * d_conv
        kernel_cols.append(jnp.sum(masked * padded[:, :, offset : offset + rows], axis=(0, 1, 2)))
        d_padded = d_padded + jnp.pad(
            masked * kernel_here[:, offset],
            ((0, 0), (0, 0), (offset, margin - offset), (0, 0)),
        )
    head = d_padded[:, :, :margin]
    from_core, from_plane = swap_core(head), to_last(head[:, 0])
    after = jnp.where(c == 0, from_core, jnp.stack([from_core[:, 1], from_plane], axis=1))
    d_gated = d_padded[:, :, margin:] + jnp.pad(
        after, ((0, 0), (0, 0), (rows - margin, 0), (0, 0))
    )
    d_projected = (
        jnp.concatenate([d_gated * x_part, d_c, d_gated * b_part], axis=3)
        .astype(jnp.bfloat16)
        .reshape(4 * rows, 3 * channels)
    )
    d_in_w = transposed_times(normed_low, d_projected)
    d_normed = plane_sum(times_transposed(d_projected, w_in))
    d_mixer = give(jnp.concatenate([d_in_w, d_out_w], axis=1)).reshape(share, 2, 4 * channels)
    d_in_w = jnp.swapaxes(d_mixer[:, :, : 3 * channels].reshape(share, 2, 3, channels), 1, 2)
    d_in_w = d_in_w.reshape(share, 3, 2 * channels)
    d_out_w = d_mixer[:, :, 3 * channels :].reshape(share, 2 * channels)
    d_hidden, d_gain_one = norm_back(d_normed, hidden, scale_one, gain_one)
    d_tokens = (grad_one + d_hidden).astype(jnp.bfloat16)

    d_kernel = lax.dynamic_update_slice(
        jnp.zeros((width, taps), jnp.float32), jnp.stack(kernel_cols, axis=1), (first_channel, 0)
    )
    small = jnp.concatenate([d_gain_one[:, None], d_gain_two[:, None], d_kernel], axis=1)
    small = lax.psum(small, BOTH)
    small = lax.dynamic_slice_in_dim(small, here * share, share, 0)
    return (
        result.astype(jnp.bfloat16)[None],
        d_tokens[None],
        small[:, 0],
        d_in_w,
        small[:, 2:],
        d_out_w,
        small[:, 1],
        d_gate_w,
        d_up_w,
        d_down_w,
    )


def solution(mesh):
    return jax.shard_map(
        on_device,
        mesh=mesh,
        in_specs=(
            P("fsdp", "seq", None),
            P("seq"),
            P("seq", None, "fsdp"),
            P("seq", None),
            P("seq", "fsdp"),
            P("seq"),
            P("seq", "fsdp"),
            P("seq", "fsdp"),
            P("seq", "fsdp"),
            P("fsdp", "seq", None),
        ),
        out_specs=(
            P("fsdp", "seq", None),
            P("fsdp", "seq", None),
            P("seq"),
            P("seq", None, "fsdp"),
            P("seq", None),
            P("seq", "fsdp"),
            P("seq"),
            P("seq", "fsdp"),
            P("seq", "fsdp"),
            P("seq", "fsdp"),
        ),
        check_vma=False,
    )
```

```python
import functools

import jax
import jax.numpy as jnp
from jax import lax
from jax.experimental import pallas as pl
from jax.experimental.pallas import tpu as pltpu
from jax.sharding import PartitionSpec as P

SEQS = 3
EPSILON = 1e-05
BOTH = ("seq", "fsdp")
MESH = pl.DeviceIdType.MESH
PART = 256


def times_transposed(left, right):
    return lax.dot_general(
        left, right, (((1,), (1,)), ((), ())), preferred_element_type=jnp.float32
    )


def transposed_times(left, right):
    return lax.dot_general(
        left, right, (((0,), (0,)), ((), ())), preferred_element_type=jnp.float32
    )


def times(left, right):
    return jnp.dot(left, right, preferred_element_type=jnp.float32)


def root_norm(hidden, gain):
    scale = lax.rsqrt(jnp.mean(hidden * hidden, axis=-1, keepdims=True) + EPSILON)
    return (hidden * scale * gain, scale)


def norm_back(grad, hidden, scale, gain):
    weighted = grad * gain
    inner = jnp.sum(weighted * hidden, axis=-1, keepdims=True)
    d_hidden = scale * weighted - hidden * (scale * scale * scale) * inner / hidden.shape[-1]
    d_gain = jnp.sum(grad * hidden * scale, axis=0)
    return (d_hidden, d_gain)


def device(z, y, c, x):
    return (z * 4 + y * 2 + c) * 2 + x


def every(planes):
    return [
        (z, y, c, x) for z in range(planes) for y in range(2) for c in range(2) for x in range(2)
    ]


def plain_on_device(
    tokens,
    norm1_gain,
    in_weight,
    conv_kernel,
    out_weight,
    norm2_gain,
    gate_weight,
    up_weight,
    down_weight,
    d_out,
):
    planes = lax.axis_size("seq") // 4
    here = lax.axis_index("seq")
    y, c, x = (here // 2) % 2, here % 2, lax.axis_index("fsdp")
    z = here // 4
    rows, width = tokens.shape[1:]
    share = gate_weight.shape[0]
    plane_groups = [
        [device(z, y, c, x) for x in range(2) for y in range(2)]
        for z in range(planes)
        for c in range(2)
    ]
    column_groups = [
        [z * 4 + y * 2 + c for z in range(planes) for c in range(2)] for y in range(2)
    ]
    members = 2 * planes

    def moved(value, target):
        pairs = []
        for place in every(planes):
            to = target(*place)
            if to is not None:
                pairs.append((device(*place), device(*to)))
        return lax.ppermute(value, BOTH, pairs)

    def swap_y(value):
        return moved(value, lambda z, y, c, x: (z, 1 - y, c, x))

    def swap_x(value):
        return moved(value, lambda z, y, c, x: (z, y, c, 1 - x))

    def swap_both(value):
        return moved(value, lambda z, y, c, x: (z, 1 - y, c, 1 - x))

    def ordered(first, second, flag):
        return jnp.where(flag == 0, jnp.stack([first, second]), jnp.stack([second, first]))

    def plane_gather(value):
        by_y = ordered(value, swap_y(value), y)
        other = ordered(swap_x(value), swap_both(value), y)
        return ordered(by_y, other, x).reshape((4 * value.shape[0],) + value.shape[1:])

    def plane_sum(partial):
        sent = partial.astype(jnp.bfloat16).reshape(4, rows, width)
        got = lax.all_to_all(sent, BOTH, 0, 0, axis_index_groups=plane_groups, tiled=True)
        return jnp.sum(got.astype(jnp.float32), axis=0)

    def fetch(weight):
        halves = weight.reshape(share, 2, -1)
        mine = jnp.where(y == 0, halves[:, 0], halves[:, 1])
        theirs = jnp.where(y == 0, halves[:, 1], halves[:, 0])
        pair = ordered(mine, swap_y(theirs), y)
        got = lax.all_gather(pair, "seq", axis=0, tiled=False, axis_index_groups=column_groups)
        got = got.reshape(planes, 2, 2, share, -1)
        return jnp.swapaxes(got, 1, 2).reshape(width, -1)

    def give(grad):
        sent = grad.astype(jnp.bfloat16).reshape(planes, 2, 2, share, -1)
        sent = jnp.swapaxes(sent, 1, 2).reshape(members * 2, share, -1)
        got = lax.psum_scatter(
            sent, "seq", scatter_dimension=0, tiled=True, axis_index_groups=column_groups
        )
        mine = jnp.where(y == 0, got[0], got[1])
        theirs = jnp.where(y == 0, got[1], got[0])
        pair = ordered(mine, swap_y(theirs), y).astype(jnp.float32)
        return jnp.concatenate([pair[0], pair[1]], axis=1)

    gains = lax.all_gather(
        jnp.concatenate(
            [norm1_gain[:, None], norm2_gain[:, None], conv_kernel], axis=1
        ),
        "seq",
        axis=0,
        tiled=True,
    ).astype(jnp.float32)
    gain_one, gain_two, kernel = gains[:, 0], gains[:, 1], gains[:, 2:]
    taps = kernel.shape[1]
    margin = taps - 1
    channels = in_weight.shape[2] // 2
    first_channel = x * (2 * channels) + y * channels
    kernel_here = lax.dynamic_slice_in_dim(kernel, first_channel, channels, 0)

    w_in_halves = jnp.swapaxes(in_weight.reshape(share, 3, 2, channels), 1, 2)
    w_mixer = fetch(
        jnp.concatenate(
            [w_in_halves.reshape(share, 2, 3 * channels), out_weight.reshape(share, 2, channels)],
            axis=2,
        ).reshape(share, 8 * channels)
    )
    w_in, w_out = w_mixer[:, : 3 * channels], w_mixer[:, 3 * channels :]

    hidden = tokens[0].astype(jnp.float32)
    normed, scale_one = root_norm(hidden, gain_one)
    normed_low = plane_gather(normed.astype(jnp.bfloat16))
    grad_low = plane_gather(d_out[0])

    w_gate = fetch(gate_weight)
    w_up = fetch(up_weight)
    w_down = fetch(down_weight)

    projected = times(normed_low, w_in).reshape(2, 2, rows, 3 * channels)
    b_part = projected[..., :channels]
    c_part = projected[..., channels : 2 * channels]
    x_part = projected[..., 2 * channels :]
    gated = (b_part * x_part).astype(jnp.bfloat16)

    def swap_core(value):
        return moved(value, lambda z, y, c, x: (z, y, 1 - c, x))

    def to_next(value):
        return moved(
            value, lambda z, y, c, x: (z + 1, y, 0, x) if c == 1 and z + 1 < planes else None
        )

    def to_last(value):
        return moved(value, lambda z, y, c, x: (z - 1, y, 1, x) if c == 0 and z > 0 else None)

    tail = gated[:, :, rows - margin :]
    from_core, from_plane = swap_core(tail), to_next(tail[:, 1])
    before = jnp.where(
        c == 1, from_core, jnp.stack([from_plane, from_core[:, 0]], axis=1)
    )
    padded = jnp.concatenate([before, gated], axis=2).astype(jnp.float32)
    seq_len = lax.axis_size("seq") * rows // SEQS
    block = z * 4 + jnp.arange(2, dtype=jnp.int32) * 2 + c
    position = block[:, None] * rows + jnp.arange(rows, dtype=jnp.int32)
    in_sequence = position % seq_len
    masks = [
        (in_sequence >= margin - offset).astype(jnp.float32)[None, :, :, None]
        for offset in range(taps)
    ]
    conv = jnp.zeros_like(b_part)
    for offset in range(taps):
        conv = conv + masks[offset] * padded[:, :, offset : offset + rows] * kernel_here[:, offset]
    mixed = (c_part * conv).astype(jnp.bfloat16).reshape(4 * rows, channels)
    hidden_one = hidden + plane_sum(times_transposed(mixed, w_out))

    normed_two, scale_two = root_norm(hidden_one, gain_two)
    normed_two_low = plane_gather(normed_two.astype(jnp.bfloat16))
    gate = times(normed_two_low, w_gate)
    upper = times(normed_two_low, w_up)
    sigma = jax.nn.sigmoid(gate)
    active = (gate * sigma * upper).astype(jnp.bfloat16)
    d_active = times(grad_low, w_down)
    d_upper = (d_active * gate * sigma).astype(jnp.bfloat16)
    d_gate = (d_active * upper * sigma * (1.0 + gate * (1.0 - sigma))).astype(jnp.bfloat16)
    d_normed_two = plane_sum(times_transposed(d_gate, w_gate) + times_transposed(d_upper, w_up))
    result = hidden_one + plane_sum(times_transposed(active, w_down))
    d_gate_w = give(transposed_times(normed_two_low, d_gate))
    d_up_w = give(transposed_times(normed_two_low, d_upper))
    d_down_w = give(transposed_times(grad_low, active))

    d_hidden_two, d_gain_two = norm_back(d_normed_two, hidden_one, scale_two, gain_two)
    grad_one = d_out[0].astype(jnp.float32) + d_hidden_two
    grad_one_low = plane_gather(grad_one.astype(jnp.bfloat16))
    d_out_w = transposed_times(grad_one_low, mixed)
    d_mixed = times(grad_one_low, w_out).reshape(2, 2, rows, channels)
    d_c = d_mixed * conv
    d_conv = d_mixed * c_part
    kernel_cols = []
    d_padded = jnp.zeros((2, 2, rows + margin, channels), jnp.float32)
    for offset in range(taps):
        masked = masks[offset] * d_conv
        kernel_cols.append(jnp.sum(masked * padded[:, :, offset : offset + rows], axis=(0, 1, 2)))
        d_padded = d_padded + jnp.pad(
            masked * kernel_here[:, offset],
            ((0, 0), (0, 0), (offset, margin - offset), (0, 0)),
        )
    head = d_padded[:, :, :margin]
    from_core, from_plane = swap_core(head), to_last(head[:, 0])
    after = jnp.where(c == 0, from_core, jnp.stack([from_core[:, 1], from_plane], axis=1))
    d_gated = d_padded[:, :, margin:] + jnp.pad(
        after, ((0, 0), (0, 0), (rows - margin, 0), (0, 0))
    )
    d_projected = (
        jnp.concatenate([d_gated * x_part, d_c, d_gated * b_part], axis=3)
        .astype(jnp.bfloat16)
        .reshape(4 * rows, 3 * channels)
    )
    d_in_w = transposed_times(normed_low, d_projected)
    d_normed = plane_sum(times_transposed(d_projected, w_in))
    d_mixer = give(jnp.concatenate([d_in_w, d_out_w], axis=1)).reshape(share, 2, 4 * channels)
    d_in_w = jnp.swapaxes(d_mixer[:, :, : 3 * channels].reshape(share, 2, 3, channels), 1, 2)
    d_in_w = d_in_w.reshape(share, 3, 2 * channels)
    d_out_w = d_mixer[:, :, 3 * channels :].reshape(share, 2 * channels)
    d_hidden, d_gain_one = norm_back(d_normed, hidden, scale_one, gain_one)
    d_tokens = (grad_one + d_hidden).astype(jnp.bfloat16)

    d_kernel = lax.dynamic_update_slice(
        jnp.zeros((width, taps), jnp.float32), jnp.stack(kernel_cols, axis=1), (first_channel, 0)
    )
    small = jnp.concatenate([d_gain_one[:, None], d_gain_two[:, None], d_kernel], axis=1)
    small = lax.psum(small, BOTH)
    small = lax.dynamic_slice_in_dim(small, here * share, share, 0)
    return (
        result.astype(jnp.bfloat16)[None],
        d_tokens[None],
        small[:, 0],
        d_in_w,
        small[:, 2:],
        d_out_w,
        small[:, 1],
        d_gate_w,
        d_up_w,
        d_down_w,
    )


class Place:
    def __init__(self, planes):
        self.planes = planes
        self.me, self.x = lax.axis_index("seq"), lax.axis_index("fsdp")
        self.z = lax.div(self.me, 4)
        self.y = lax.rem(lax.div(self.me, 2), 2)
        self.c = lax.rem(self.me, 2)
        self.core = (self.me + 1 - 2 * self.c, self.x)
        self.across = (self.me + 2 - 4 * self.y, self.x)
        self.low, self.high = (self.me - 4, self.x), (self.me + 4, self.x)
        self.has_low, self.has_high = self.z > 0, self.z < planes - 1
        self.block = self.x * 2 + self.y
        self.peers = [
            (self.me, 1 - self.x),
            self.across,
            (self.across[0], 1 - self.x),
        ]
        self.peer_blocks = [
            (1 - self.x) * 2 + self.y,
            self.x * 2 + 1 - self.y,
            (1 - self.x) * 2 + 1 - self.y,
        ]
        self.is_first, self.is_last = self.c == 0, self.c == 1
        self.gives_next = jnp.logical_and(self.is_last, self.has_high)
        self.gives_last = jnp.logical_and(self.is_first, self.has_low)
        self.next, self.last = (self.me + 3, self.x), (self.me - 3, self.x)


def remote(source, target, send, receive, device_id):
    return pltpu.make_async_remote_copy(
        src_ref=source,
        dst_ref=target,
        send_sem=send,
        recv_sem=receive,
        device_id=device_id,
        device_id_type=MESH,
    )


def signal(semaphore, device_id):
    pl.semaphore_signal(semaphore, inc=1, device_id=device_id, device_id_type=MESH)


def dot(left, right):
    return jnp.dot(left, right, preferred_element_type=jnp.float32)


def kernel(
    planes,
    parts,
    seq_len,
    weights,
    tokens,
    d_out,
    gains,
    taps,
    result,
    d_tokens,
    own_grad,
    other_grad,
    small,
    d_taps,
    kept_weights,
    kept_mixer,
    w,
    core_in,
    extra,
    n_one,
    n_two,
    e_all,
    sent_a,
    sent_b,
    total_a,
    total_b,
    got_a,
    got_b,
    gated,
    d_conv,
    mixed,
    active,
    d_gate_up,
    hidden_one,
    d_hidden,
    halo,
    local_sem,
    y_send,
    y_recv,
    z_send,
    z_recv,
    c_send,
    c_recv,
    core_send,
    core_recv,
    core_free,
    sum_send,
    sum_recv,
    ready,
    last_send,
    last_recv,
    own_sem,
    all_send,
    all_recv,
    part_send,
    part_recv,
    halo_send,
    halo_recv,
    keep_sem,
):
    at = Place(planes)
    z, y, c = at.z, at.y, at.c
    rows, width = tokens.shape
    channels = taps.shape[1]
    share = weights.shape[2]
    wide = 4 * share
    chunks = parts + 2
    step_cols = weights.shape[3] // 3

    def y_copies(k):
        return (
            pltpu.make_async_copy(weights.at[k, y], w.at[k, z, y, c], local_sem.at[k]),
            remote(weights.at[k, 1 - y], w.at[k, z, y, c], y_send.at[k], y_recv.at[k], at.across),
        )

    def piece(k, p):
        return w.at[k, p, :, c]

    def to_side(k, p, side):
        return remote(
            piece(k, p),
            piece(k, p),
            z_send.at[k, side, p],
            z_recv.at[k, p],
            at.high if side else at.low,
        )

    def to_core(k, p):
        return remote(piece(k, p), piece(k, p), c_send.at[k, p], c_recv.at[k, p], at.core)

    def begin(k):
        for copy in y_copies(k):
            copy.start()

    def own(k):
        y_copies(k)[0].wait()
        remote(
            weights.at[k, y], w.at[k, z, 1 - y, c], y_send.at[k], y_recv.at[k], at.across
        ).wait_recv()
        pl.when(at.has_low)(lambda: to_side(k, z, 0).start())
        pl.when(at.has_high)(lambda: to_side(k, z, 1).start())
        to_core(k, z).start()

    def relay(k, t):
        below, above = z - t, z + t

        @pl.when(below >= 0)
        def _():
            to_side(k, below, 1).wait_recv()
            pl.when(at.has_high)(lambda: to_side(k, below, 1).start())
            to_core(k, below).start()

        @pl.when(above < planes)
        def _():
            to_side(k, above, 0).wait_recv()
            pl.when(at.has_low)(lambda: to_side(k, above, 0).start())
            to_core(k, above).start()

    def relays(k):
        for t in range(1, planes):
            relay(k, t)

    def core_wait(k):
        for p in range(planes):
            remote(
                w.at[k, p, :, 1 - c], w.at[k, p, :, 1 - c], c_send.at[k, p], c_recv.at[k, p], at.core
            ).wait_recv()

    def gather_done(k):
        y_copies(k)[1].wait_send()
        for p in range(planes):
            pl.when(jnp.logical_and(at.has_low, p >= z))(lambda: to_side(k, p, 0).wait_send())
            pl.when(jnp.logical_and(at.has_high, p <= z))(lambda: to_side(k, p, 1).wait_send())
            to_core(k, p).wait_send()

    def chunk_of(v):
        return lax.rem(v + 2, chunks)

    def core_copy(v):
        k = chunk_of(v)
        return remote(
            w.at[k, :, :, 1 - c],
            core_in.at[lax.rem(v, 2)],
            core_send.at[k],
            core_recv.at[k],
            at.core,
        )

    def core_start(v):
        pl.when(v >= 2)(lambda: pl.semaphore_wait(core_free, 1))
        core_copy(v).start()

    def core_add(v):
        k, slot = chunk_of(v), lax.rem(v, 2)
        core_copy(v).wait()

        def add(p, carry):
            total = w[k, p, :, c].astype(jnp.float32) + core_in[slot, p].astype(jnp.float32)
            w[k, p, :, c] = total.astype(jnp.bfloat16)
            return carry

        lax.fori_loop(0, planes, add, 0)
        pl.when(v < chunks - 2)(lambda: signal(core_free, at.core))
        pl.when(at.has_low)(lambda: signal(ready.at[1], at.low))
        pl.when(at.has_high)(lambda: signal(ready.at[0], at.high))

    def landing(k, d):
        return w.at[k, d, :, 1 - c]

    def sum_up(k, d):
        return remote(
            landing(k, d), landing(k, d), sum_send.at[k, 1, d], sum_recv.at[k, 1, d], at.high
        )

    def sum_down(k, d):
        return remote(
            landing(k, d), landing(k, d), sum_send.at[k, 0, d], sum_recv.at[k, 0, d], at.low
        )

    def sum_down_last(k, d):
        return remote(
            landing(k, d), extra.at[k], sum_send.at[k, 0, d], sum_recv.at[k, 0, d], at.low
        )

    def add_here(k, d, arrived):
        here = w[k, d, :, c].astype(jnp.float32)

        @pl.when(arrived)
        def _():
            w[k, d, :, 1 - c] = (w[k, d, :, 1 - c].astype(jnp.float32) + here).astype(jnp.bfloat16)

        @pl.when(jnp.logical_not(arrived))
        def _():
            w[k, d, :, 1 - c] = w[k, d, :, c]

    def add_up(v):
        k = chunk_of(v)
        pl.when(at.has_high)(lambda: pl.semaphore_wait(ready.at[1], 1))
        for d in range(planes - 1, -1, -1):

            @pl.when(d > z)
            def _():
                pl.when(at.has_low)(lambda: sum_up(k, d).wait_recv())
                add_here(k, d, at.has_low)
                sum_up(k, d).start()

            @pl.when(jnp.logical_and(z == d, at.has_low))
            def _():
                sum_up(k, d).wait_recv()
                total = w[k, d, :, c].astype(jnp.float32) + w[k, d, :, 1 - c].astype(jnp.float32)
                w[k, d, :, c] = total.astype(jnp.bfloat16)

    def add_down(v):
        k = chunk_of(v)
        pl.when(at.has_low)(lambda: pl.semaphore_wait(ready.at[0], 1))
        for d in range(planes):

            @pl.when(d < z)
            def _():
                pl.when(at.has_high)(lambda: sum_down(k, d).wait_recv())
                add_here(k, d, at.has_high)
                pl.when(z - 1 > d)(lambda: sum_down(k, d).start())
                pl.when(z - 1 == d)(lambda: sum_down_last(k, d).start())

            @pl.when(jnp.logical_and(z == d, at.has_high))
            def _():
                sum_down_last(k, d).wait_recv()
                total = w[k, d, :, c].astype(jnp.float32) + extra[k].astype(jnp.float32)
                w[k, d, :, c] = total.astype(jnp.bfloat16)

    def give_copies(k):
        return (
            pltpu.make_async_copy(w.at[k, z, y, c], own_grad.at[k], own_sem.at[k]),
            remote(
                w.at[k, z, 1 - y, c], other_grad.at[k], last_send.at[k], last_recv.at[k], at.across
            ),
        )

    def give(v):
        for copy in give_copies(chunk_of(v)):
            copy.start()

    def sum_done(v):
        k = chunk_of(v)
        for d in range(planes):
            pl.when(d > z)(lambda: sum_up(k, d).wait_send())
            pl.when(d < z)(lambda: sum_down(k, d).wait_send())
        for copy in give_copies(k):
            copy.wait()

    pause = planes - 1

    def stage(o, do):
        early = jnp.logical_and(o >= 0, o < parts)
        late = jnp.logical_and(o >= parts + pause, o < parts + pause + 2)
        pl.when(jnp.logical_or(early, late))(lambda: do(jnp.where(late, o - pause, o)))

    def tick(i):
        far = jnp.maximum(z, planes - 1 - z)
        stage(i - 1, core_add)
        stage(i - 1 - z, add_up)
        stage(i - 1 - (planes - 1 - z), add_down)
        stage(i - 1 - far, give)

    def all_copies(buffer, which):
        return [
            remote(
                buffer.at[at.block],
                buffer.at[at.block],
                all_send.at[which, i],
                all_recv.at[which, i],
                peer,
            )
            for i, peer in enumerate(at.peers)
        ]

    def all_start(buffer, which):
        for copy in all_copies(buffer, which):
            copy.start()

    def all_wait(buffer, which):
        for i, peer in enumerate(at.peers):
            landed = buffer.at[at.peer_blocks[i]]
            remote(
                landed, landed, all_send.at[which, i], all_recv.at[which, i], peer
            ).wait_recv()

    def all_done(buffer, which):
        for copy in all_copies(buffer, which):
            copy.wait_send()

    def part_copies(source, target, which):
        return [
            remote(
                source.at[at.peer_blocks[i]],
                target.at[i],
                part_send.at[which, i],
                part_recv.at[which, i],
                peer,
            )
            for i, peer in enumerate(at.peers)
        ]

    def part_start(source, target, which):
        for copy in part_copies(source, target, which):
            copy.start()

    def part_wait(source, target, which):
        for copy in part_copies(source, target, which):
            copy.wait_recv()

    def part_done(source, target, which):
        for copy in part_copies(source, target, which):
            copy.wait_send()

    tile = 48

    def by_rows(body):
        def run(i, carry):
            body(pl.ds(pl.multiple_of(i * tile, tile), tile))
            return carry

        lax.fori_loop(0, rows // tile, run, 0)

    def scale_of(hidden):
        return lax.rsqrt(jnp.mean(hidden * hidden, axis=-1, keepdims=True) + EPSILON)

    def summed(source, target, span):
        total = source[at.block, span, :].astype(jnp.float32)
        for i in range(3):
            total = total + target[i, span, :].astype(jnp.float32)
        return total

    def back_through_norm(grad, hidden, gain, row):
        scale = scale_of(hidden)
        weighted = grad * gain
        inner = jnp.sum(weighted * hidden, axis=-1, keepdims=True)
        small[row : row + 1, :] += jnp.sum(grad * hidden * scale, axis=0, keepdims=True)
        return scale * weighted - hidden * (scale * scale * scale) * inner / width

    def transposed(buffer, k):
        def one(p, carry):
            cols = pl.ds(pl.multiple_of(p * wide, wide), wide)
            block = buffer[:, :, cols].reshape(4 * rows, wide).T
            w[k, p] = block.reshape(2, 2, share, 4 * rows)
            return carry

        lax.fori_loop(0, planes, one, 0)

    def whole(k, low, high):
        return w[k, :, :, :, :, low:high].reshape(planes * wide, high - low)

    def plane_rows(k, p, low, high):
        return w[k, p, :, :, :, low:high].reshape(wide, high - low)

    def pair(t):
        return pl.ds(2 * t, 2)

    def columns(p):
        return pl.ds(pl.multiple_of(p * wide, wide), wide)

    halo[...] = jnp.zeros_like(halo)
    barrier = pltpu.get_barrier_semaphore()
    for device_id in [at.core] + at.peers:
        signal(barrier, device_id)
    pl.when(at.has_low)(lambda: signal(barrier, at.low))
    pl.when(at.has_high)(lambda: signal(barrier, at.high))
    pl.when(at.gives_next)(lambda: signal(barrier, at.next))
    pl.when(at.gives_last)(lambda: signal(barrier, at.last))
    count = 4
    for flag in (at.has_low, at.has_high, at.gives_next, at.gives_last):
        count = count + jnp.where(flag, 1, 0)
    pl.semaphore_wait(barrier, count)

    begin(0)
    begin(1)
    e_copy = pltpu.make_async_copy(d_out, e_all.at[at.block], keep_sem.at[0])
    e_copy.start()
    small[...] = jnp.zeros_like(small)
    d_taps[...] = jnp.zeros_like(d_taps)

    def first_norm(span):
        hidden = tokens[span, :].astype(jnp.float32)
        n_one[at.block, span, :] = (hidden * scale_of(hidden) * gains[0:1, :]).astype(jnp.bfloat16)

    by_rows(first_norm)
    all_start(n_one, 0)
    own(0)
    own(1)
    for k in range(2, chunks):
        begin(k)
    relay(0, 1)
    relay(1, 1)
    own(2)
    for t in range(2, planes):
        relay(0, t)
        relay(1, t)
    own(3)
    own(4)
    e_copy.wait()
    all_start(e_all, 1)
    core_wait(0)
    core_wait(1)
    all_wait(n_one, 0)

    def project(t, carry):
        normed = n_one[pair(t)].reshape(2 * rows, width)
        b_c = dot(normed, whole(0, 0, 2 * channels))
        x_part = dot(normed, whole(1, 0, channels))
        total_a[pair(t), :, 0 : 2 * channels] = b_c.reshape(2, rows, 2 * channels)
        total_a[pair(t), :, 2 * channels : 3 * channels] = x_part.reshape(2, rows, channels)
        product = (b_c[:, :channels] * x_part).astype(jnp.bfloat16).astype(jnp.float32)
        gated[pair(t), 8 : 8 + rows, :] = product.reshape(2, rows, channels)
        return carry

    lax.fori_loop(0, 2, project, 0)

    def halo_core(which, edge):
        return remote(
            edge, halo.at[2 * which], halo_send.at[2 * which], halo_recv.at[2 * which], at.core
        )

    def halo_plane(which, edge, target):
        return remote(
            edge,
            halo.at[2 * which + 1],
            halo_send.at[2 * which + 1],
            halo_recv.at[2 * which + 1],
            target,
        )

    tail = gated.at[:, pl.ds(rows, 8), :]
    halo_core(0, tail).start()
    pl.when(at.gives_next)(lambda: halo_plane(0, tail, at.next).start())
    halo_core(0, tail).wait_recv()
    pl.when(at.gives_last)(lambda: halo_plane(0, tail, at.last).wait_recv())
    for group in range(2):

        @pl.when(at.is_last)
        def _():
            gated[2 * group, 0:8, :] = halo[0, 2 * group]
            gated[2 * group + 1, 0:8, :] = halo[0, 2 * group + 1]

        @pl.when(at.is_first)
        def _():
            gated[2 * group, 0:8, :] = halo[1, 2 * group + 1]
            gated[2 * group + 1, 0:8, :] = halo[0, 2 * group]

    def start_of(block):
        return lax.rem((z * 4 + lax.rem(block, 2) * 2 + c) * rows, seq_len)

    def place_in(block, ahead):
        place = start_of(block) + ahead + lax.broadcasted_iota(jnp.int32, (rows, channels), 0)
        return jnp.where(place >= seq_len, place - seq_len, place)

    def convolve(b, carry):
        place = place_in(b, 0)
        conv = jnp.zeros((rows, channels), jnp.float32)
        for j in range(3):
            moved = gated[b, 6 + j : 6 + j + rows, :]
            conv = conv + jnp.where(place >= 2 - j, moved, 0.0) * taps[j : j + 1, :]
        total_a[b, :, 3 * channels : 4 * channels] = conv
        mixed[b] = (total_a[b, :, channels : 2 * channels] * conv).astype(jnp.bfloat16)
        return carry

    lax.fori_loop(0, 4, convolve, 0)

    def branch(i, carry):
        t, p = lax.div(i, planes), lax.rem(i, planes)
        left = mixed[pair(t)].reshape(2 * rows, channels)
        out = times_transposed(left, plane_rows(1, p, channels, 2 * channels))
        sent_a[pair(t), :, columns(p)] = out.reshape(2, rows, wide).astype(jnp.bfloat16)
        return carry

    lax.fori_loop(0, 2 * planes, branch, 0)
    part_start(sent_a, got_a, 0)
    gather_done(0)
    gather_done(1)
    keep_weights = pltpu.make_async_copy(w.at[pl.ds(0, 2)], kept_weights, keep_sem.at[1])
    keep_mixer = pltpu.make_async_copy(total_a, kept_mixer, keep_sem.at[2])
    keep_weights.start()
    keep_mixer.start()
    relays(2)
    keep_weights.wait()
    keep_mixer.wait()
    total_a[...] = jnp.zeros_like(total_a)
    total_b[...] = jnp.zeros_like(total_b)
    all_wait(e_all, 1)
    transposed(e_all, 1)
    part_wait(sent_a, got_a, 0)

    def second_norm(span):
        hidden = tokens[span, :].astype(jnp.float32) + summed(sent_a, got_a, span)
        hidden_one[span, :] = hidden
        n_two[at.block, span, :] = (hidden * scale_of(hidden) * gains[1:2, :]).astype(jnp.bfloat16)

    by_rows(second_norm)
    all_start(n_two, 2)
    part_done(sent_a, got_a, 0)
    own(5)
    relays(3)
    own(6)
    relays(4)
    all_wait(n_two, 2)
    transposed(n_two, 0)

    def feed_forward(k):
        def half(t, carry):
            normed = n_two[pair(t)].reshape(2 * rows, width)
            both = dot(normed, whole(k, 0, 2 * step_cols))
            d_active = dot(
                e_all[pair(t)].reshape(2 * rows, width), whole(k, 2 * step_cols, 3 * step_cols)
            )
            gate, upper = both[:, :step_cols], both[:, step_cols:]
            sigma = jax.nn.sigmoid(gate)
            soft = gate * sigma
            here = pl.ds(pl.multiple_of(t * 2 * rows, 2 * rows), 2 * rows)
            active[here, :] = (soft * upper).astype(jnp.bfloat16)
            d_gate_up[here, step_cols:] = (d_active * soft).astype(jnp.bfloat16)
            d_gate_up[here, :step_cols] = (
                d_active * upper * sigma * (1.0 + gate * (1.0 - sigma))
            ).astype(jnp.bfloat16)

            def spread(p, inner):
                back = times_transposed(d_gate_up[here, :], plane_rows(k, p, 0, 2 * step_cols))
                total_b[pair(t), :, columns(p)] += back.reshape(2, rows, wide)
                out = times_transposed(
                    active[here, :], plane_rows(k, p, 2 * step_cols, 3 * step_cols)
                )
                total_a[pair(t), :, columns(p)] += out.reshape(2, rows, wide)
                return inner

            lax.fori_loop(0, planes, spread, 0)
            return carry

        lax.fori_loop(0, 2, half, 0)
        gather_done(k)

        def grads(p, carry):
            low = dot(w[0, p].reshape(wide, 4 * rows), d_gate_up[...])
            w[k, p, :, :, :, 0 : 2 * step_cols] = low.astype(jnp.bfloat16).reshape(
                2, 2, share, 2 * step_cols
            )
            high = dot(w[1, p].reshape(wide, 4 * rows), active[...])
            w[k, p, :, :, :, 2 * step_cols : 3 * step_cols] = high.astype(jnp.bfloat16).reshape(
                2, 2, share, step_cols
            )
            return carry

        lax.fori_loop(0, planes, grads, 0)

    def one_part(i, carry):
        k = i + 2
        pl.when(k + 5 < chunks)(lambda: own(k + 5))
        tick(i)
        core_wait(k)
        feed_forward(k)
        core_start(i)
        pl.when(k + 3 < chunks)(lambda: relays(k + 3))
        return carry

    lax.fori_loop(0, parts, one_part, 0)

    restore_weights = pltpu.make_async_copy(kept_weights, w.at[pl.ds(0, 2)], keep_sem.at[1])
    restore_weights.start()
    sum_done(0)
    sum_done(1)
    transposed(n_one, 2)

    def cast(source, target):
        def run(b, carry):
            target[b] = source[b].astype(jnp.bfloat16)
            return carry

        lax.fori_loop(0, 4, run, 0)

    cast(total_b, sent_a)
    part_start(sent_a, got_a, 2)
    cast(total_a, sent_b)
    part_start(sent_b, got_b, 1)
    restore_mixer = pltpu.make_async_copy(kept_mixer, total_a, keep_sem.at[2])
    restore_mixer.start()
    tick(parts)
    part_wait(sent_a, got_a, 2)
    all_done(n_one, 0)

    def through_second(span):
        grad = back_through_norm(
            summed(sent_a, got_a, span), hidden_one[span, :], gains[1:2, :], 1
        )
        grad = e_all[at.block, span, :].astype(jnp.float32) + grad
        d_hidden[span, :] = grad
        n_one[at.block, span, :] = grad.astype(jnp.bfloat16)

    by_rows(through_second)
    all_start(n_one, 3)
    part_done(sent_a, got_a, 2)
    tick(parts + 1)
    part_wait(sent_b, got_b, 1)

    def last_out(span):
        result[span, :] = (hidden_one[span, :] + summed(sent_b, got_b, span)).astype(jnp.bfloat16)

    by_rows(last_out)
    part_done(sent_b, got_b, 1)
    restore_weights.wait()
    restore_mixer.wait()
    all_wait(n_one, 3)

    def into_mixer(t, carry):
        grad = n_one[pair(t)].reshape(2 * rows, width)
        d_mixed = dot(grad, whole(1, channels, 2 * channels)).reshape(2, rows, channels)
        conv = total_a[pair(t), :, 3 * channels : 4 * channels]
        c_part = total_a[pair(t), :, channels : 2 * channels]
        sent_b[pair(t), :, channels : 2 * channels] = (d_mixed * conv).astype(jnp.bfloat16)
        d_conv[pair(t), 0:rows, :] = d_mixed * c_part
        return carry

    lax.fori_loop(0, 2, into_mixer, 0)
    head = d_conv.at[:, pl.ds(0, 8), :]
    halo_core(1, head).start()
    pl.when(at.gives_last)(lambda: halo_plane(1, head, at.last).start())
    transposed(n_one, 3)

    def d_out_weight(p, carry):
        grad = dot(w[3, p].reshape(wide, 4 * rows), mixed[...].reshape(4 * rows, channels))
        w[1, p, :, :, :, channels : 2 * channels] = grad.astype(jnp.bfloat16).reshape(
            2, 2, share, channels
        )
        return carry

    lax.fori_loop(0, planes, d_out_weight, 0)
    halo_core(1, head).wait_recv()
    pl.when(at.gives_next)(lambda: halo_plane(1, head, at.next).wait_recv())
    for group in range(2):

        @pl.when(at.is_first)
        def _():
            d_conv[2 * group, rows : rows + 8, :] = halo[2, 2 * group]
            d_conv[2 * group + 1, rows : rows + 8, :] = halo[2, 2 * group + 1]

        @pl.when(at.is_last)
        def _():
            d_conv[2 * group, rows : rows + 8, :] = halo[2, 2 * group + 1]
            d_conv[2 * group + 1, rows : rows + 8, :] = halo[3, 2 * group]

    def convolve_back(b, carry):
        place = place_in(b, 0)
        d_gated = jnp.zeros((rows, channels), jnp.float32)
        for j in range(3):
            ahead = 2 - j
            moved = jnp.where(
                place_in(b, ahead) >= ahead, d_conv[b, ahead : ahead + rows, :], 0.0
            )
            d_gated = d_gated + moved * taps[j : j + 1, :]
            product = d_conv[b, 0:rows, :] * gated[b, 6 + j : 6 + j + rows, :]
            d_taps[j : j + 1, :] += jnp.sum(
                jnp.where(place >= ahead, product, 0.0), axis=0, keepdims=True
            )
        x_part = total_a[b, :, 2 * channels : 3 * channels]
        sent_b[b, :, 0:channels] = (d_gated * x_part).astype(jnp.bfloat16)
        b_part = total_a[b, :, 0:channels]
        sent_b[b, :, 2 * channels : 3 * channels] = (d_gated * b_part).astype(jnp.bfloat16)
        return carry

    lax.fori_loop(0, 4, convolve_back, 0)

    def d_normed(i, carry):
        t, p = lax.div(i, planes), lax.rem(i, planes)
        grad = sent_b[pair(t), :, 0 : 2 * channels].reshape(2 * rows, 2 * channels)
        out = times_transposed(grad, plane_rows(0, p, 0, 2 * channels))
        grad = sent_b[pair(t), :, 2 * channels : 3 * channels].reshape(2 * rows, channels)
        out = out + times_transposed(grad, plane_rows(1, p, 0, channels))
        sent_a[pair(t), :, columns(p)] = out.reshape(2, rows, wide).astype(jnp.bfloat16)
        return carry

    lax.fori_loop(0, 2 * planes, d_normed, 0)
    part_start(sent_a, got_a, 3)

    def d_in_weight(p, carry):
        normed = w[2, p].reshape(wide, 4 * rows)
        grad = dot(normed, sent_b[:, :, 0 : 2 * channels].reshape(4 * rows, 2 * channels))
        w[0, p] = grad.astype(jnp.bfloat16).reshape(2, 2, share, 2 * channels)
        grad = dot(normed, sent_b[:, :, 2 * channels : 3 * channels].reshape(4 * rows, channels))
        w[1, p, :, :, :, 0:channels] = grad.astype(jnp.bfloat16).reshape(2, 2, share, channels)
        return carry

    lax.fori_loop(0, planes, d_in_weight, 0)
    core_start(jnp.int32(parts))
    core_start(jnp.int32(parts + 1))
    for i in range(parts + 2, parts + pause + 2):
        tick(i)
    part_wait(sent_a, got_a, 3)

    def through_first(span):
        hidden = tokens[span, :].astype(jnp.float32)
        grad = back_through_norm(summed(sent_a, got_a, span), hidden, gains[0:1, :], 0)
        d_tokens[span, :] = (d_hidden[span, :] + grad).astype(jnp.bfloat16)

    by_rows(through_first)
    for i in range(parts + pause + 2, parts + pause + planes + 2):
        tick(i)

    part_done(sent_a, got_a, 3)
    all_done(e_all, 1)
    all_done(n_two, 2)
    all_done(n_one, 3)
    halo_core(0, tail).wait_send()
    halo_core(1, head).wait_send()
    pl.when(at.gives_next)(lambda: halo_plane(0, tail, at.next).wait_send())
    pl.when(at.gives_last)(lambda: halo_plane(1, head, at.last).wait_send())
    for v in range(2, chunks):
        sum_done(v)


def one_kernel(planes, seq_len, weights, tokens, d_out, gains, taps):
    chunks, _, share, cols = weights.shape
    parts = chunks - 2
    rows, width = tokens.shape
    channels = taps.shape[1]
    low, full = jnp.bfloat16, jnp.float32
    shape = jax.ShapeDtypeStruct
    vmem, anywhere = pl.BlockSpec(memory_space=pltpu.VMEM), pl.BlockSpec(memory_space=pl.ANY)
    dma = pltpu.SemaphoreType.DMA
    block = (4, rows, width)
    return pl.pallas_call(
        functools.partial(kernel, planes, parts, seq_len),
        out_shape=(
            shape((rows, width), low),
            shape((rows, width), low),
            shape((chunks, share, cols), low),
            shape((chunks, share, cols), low),
            shape((8, width), full),
            shape((8, channels), full),
            shape((2, planes, 2, 2, share, cols), low),
            shape(block, full),
        ),
        in_specs=[anywhere, vmem, anywhere, vmem, vmem],
        out_specs=[vmem, vmem, anywhere, anywhere, vmem, vmem, anywhere, anywhere],
        scratch_shapes=[
            pltpu.VMEM((chunks, planes, 2, 2, share, cols), low),
            pltpu.VMEM((2, planes, 2, share, cols), low),
            pltpu.VMEM((chunks, 2, share, cols), low),
            pltpu.VMEM(block, low),
            pltpu.VMEM(block, low),
            pltpu.VMEM(block, low),
            pltpu.VMEM(block, low),
            pltpu.VMEM(block, low),
            pltpu.VMEM(block, full),
            pltpu.VMEM(block, full),
            pltpu.VMEM((3, rows, width), low),
            pltpu.VMEM((3, rows, width), low),
            pltpu.VMEM((4, rows + 8, channels), full),
            pltpu.VMEM((4, rows + 8, channels), full),
            pltpu.VMEM((4, rows, channels), low),
            pltpu.VMEM((4 * rows, PART), low),
            pltpu.VMEM((4 * rows, 2 * PART), low),
            pltpu.VMEM((rows, width), full),
            pltpu.VMEM((rows, width), full),
            pltpu.VMEM((4, 4, 8, channels), full),
            dma((chunks,)),
            dma((chunks,)),
            dma((chunks,)),
            dma((chunks, 2, planes)),
            dma((chunks, planes)),
            dma((chunks, planes)),
            dma((chunks, planes)),
            dma((chunks,)),
            dma((chunks,)),
            pltpu.SemaphoreType.REGULAR,
            dma((chunks, 2, planes)),
            dma((chunks, 2, planes)),
            pltpu.SemaphoreType.REGULAR((2,)),
            dma((chunks,)),
            dma((chunks,)),
            dma((chunks,)),
            dma((4, 3)),
            dma((4, 3)),
            dma((4, 3)),
            dma((4, 3)),
            dma((4,)),
            dma((4,)),
            dma((3,)),
        ],
        compiler_params=pltpu.CompilerParams(
            collective_id=0, has_side_effects=True, vmem_limit_bytes=64 * 1024 * 1024
        ),
    )(weights, tokens, d_out, gains, taps)


def on_device(
    tokens,
    norm1_gain,
    in_weight,
    conv_kernel,
    out_weight,
    norm2_gain,
    gate_weight,
    up_weight,
    down_weight,
    d_out,
):
    planes = lax.axis_size("seq") // 4
    here = lax.axis_index("seq")
    y, x = (here // 2) % 2, lax.axis_index("fsdp")
    rows, width = tokens.shape[1:]
    share = gate_weight.shape[0]
    channels = in_weight.shape[2] // 2
    hidden = gate_weight.shape[1] // 2
    parts = -(-hidden // PART)

    gains = lax.all_gather(
        jnp.concatenate([norm1_gain[:, None], norm2_gain[:, None], conv_kernel], axis=1),
        "seq",
        axis=0,
        tiled=True,
    ).astype(jnp.float32)
    gains = jnp.pad(gains.T, ((0, 3), (0, 0)))
    first_channel = x * (2 * channels) + y * channels
    taps = lax.dynamic_slice_in_dim(gains, first_channel, channels, 1)[2:]
    taps = jnp.pad(taps, ((0, 2), (0, 0)))

    mixer = jnp.concatenate(
        [in_weight.reshape(share, 3, 2, channels), out_weight.reshape(share, 1, 2, channels)],
        axis=1,
    )
    mixer = mixer.reshape(share, 2, 2, 2, channels).transpose(1, 3, 0, 2, 4)
    mixer = mixer.reshape(2, 2, share, 2 * channels)

    def in_parts(weight):
        halves = jnp.pad(
            weight.reshape(share, 2, hidden), ((0, 0), (0, 0), (0, parts * PART - hidden))
        )
        return halves.reshape(share, 2, parts, PART).transpose(2, 1, 0, 3)

    ffn = jnp.concatenate(
        [in_parts(gate_weight), in_parts(up_weight), in_parts(down_weight)], axis=3
    )
    weights = jnp.concatenate([mixer, ffn], axis=0)
    result, d_tokens, own_grad, other_grad, small, d_taps, _, _ = one_kernel(
        planes,
        lax.axis_size("seq") * rows // SEQS,
        weights,
        tokens[0],
        d_out[0],
        gains,
        taps,
    )
    both = jnp.where(
        y == 0, jnp.stack([own_grad, other_grad]), jnp.stack([other_grad, own_grad])
    )
    d_mixer = both[:, :2].reshape(2, 2, share, 2, channels).transpose(2, 1, 3, 0, 4)
    d_mixer = d_mixer.reshape(share, 4, 2 * channels).astype(jnp.float32)

    def whole_grad(which):
        grad = both[:, 2:, :, which * PART : (which + 1) * PART].transpose(2, 0, 1, 3)
        grad = grad.reshape(share, 2, parts * PART)[:, :, :hidden]
        return grad.reshape(share, 2 * hidden).astype(jnp.float32)

    taps_count = conv_kernel.shape[1]
    d_kernel = lax.dynamic_update_slice(
        jnp.zeros((taps_count, width), jnp.float32), d_taps[:taps_count], (0, first_channel)
    )
    sums = lax.psum(jnp.concatenate([small[:2], d_kernel], axis=0), BOTH)
    sums = lax.dynamic_slice_in_dim(sums, here * share, share, 1)
    return (
        result[None],
        d_tokens[None],
        sums[0],
        d_mixer[:, :3],
        sums[2:].T,
        d_mixer[:, 3],
        sums[1],
        whole_grad(0),
        whole_grad(1),
        whole_grad(2),
    )


def fits(mesh):
    return mesh.shape["seq"] <= 16


def solution(mesh):
    return jax.shard_map(
        on_device if fits(mesh) else plain_on_device,
        mesh=mesh,
        in_specs=(
            P("fsdp", "seq", None),
            P("seq"),
            P("seq", None, "fsdp"),
            P("seq", None),
            P("seq", "fsdp"),
            P("seq"),
            P("seq", "fsdp"),
            P("seq", "fsdp"),
            P("seq", "fsdp"),
            P("fsdp", "seq", None),
        ),
        out_specs=(
            P("fsdp", "seq", None),
            P("fsdp", "seq", None),
            P("seq"),
            P("seq", None, "fsdp"),
            P("seq", None),
            P("seq", "fsdp"),
            P("seq"),
            P("seq", "fsdp"),
            P("seq", "fsdp"),
            P("seq", "fsdp"),
        ),
        check_vma=False,
    )
```

```python
import functools

import jax
import jax.numpy as jnp
from jax import lax
from jax.experimental import pallas as pl
from jax.experimental.pallas import tpu as pltpu
from jax.sharding import PartitionSpec as P

SEQS = 3
EPSILON = 1e-05
BOTH = ("seq", "fsdp")
MESH = pl.DeviceIdType.MESH
PART = 256


def times_transposed(left, right):
    return lax.dot_general(
        left, right, (((1,), (1,)), ((), ())), preferred_element_type=jnp.float32
    )


def transposed_times(left, right):
    return lax.dot_general(
        left, right, (((0,), (0,)), ((), ())), preferred_element_type=jnp.float32
    )


def times(left, right):
    return jnp.dot(left, right, preferred_element_type=jnp.float32)


def root_norm(hidden, gain):
    scale = lax.rsqrt(jnp.mean(hidden * hidden, axis=-1, keepdims=True) + EPSILON)
    return (hidden * scale * gain, scale)


def norm_back(grad, hidden, scale, gain):
    weighted = grad * gain
    inner = jnp.sum(weighted * hidden, axis=-1, keepdims=True)
    d_hidden = scale * weighted - hidden * (scale * scale * scale) * inner / hidden.shape[-1]
    d_gain = jnp.sum(grad * hidden * scale, axis=0)
    return (d_hidden, d_gain)


def device(z, y, c, x):
    return (z * 4 + y * 2 + c) * 2 + x


def every(planes):
    return [
        (z, y, c, x) for z in range(planes) for y in range(2) for c in range(2) for x in range(2)
    ]


def plain_on_device(
    tokens,
    norm1_gain,
    in_weight,
    conv_kernel,
    out_weight,
    norm2_gain,
    gate_weight,
    up_weight,
    down_weight,
    d_out,
):
    planes = lax.axis_size("seq") // 4
    here = lax.axis_index("seq")
    y, c, x = (here // 2) % 2, here % 2, lax.axis_index("fsdp")
    z = here // 4
    rows, width = tokens.shape[1:]
    share = gate_weight.shape[0]
    plane_groups = [
        [device(z, y, c, x) for x in range(2) for y in range(2)]
        for z in range(planes)
        for c in range(2)
    ]
    column_groups = [
        [z * 4 + y * 2 + c for z in range(planes) for c in range(2)] for y in range(2)
    ]
    members = 2 * planes

    def moved(value, target):
        pairs = []
        for place in every(planes):
            to = target(*place)
            if to is not None:
                pairs.append((device(*place), device(*to)))
        return lax.ppermute(value, BOTH, pairs)

    def swap_y(value):
        return moved(value, lambda z, y, c, x: (z, 1 - y, c, x))

    def swap_x(value):
        return moved(value, lambda z, y, c, x: (z, y, c, 1 - x))

    def swap_both(value):
        return moved(value, lambda z, y, c, x: (z, 1 - y, c, 1 - x))

    def ordered(first, second, flag):
        return jnp.where(flag == 0, jnp.stack([first, second]), jnp.stack([second, first]))

    def plane_gather(value):
        by_y = ordered(value, swap_y(value), y)
        other = ordered(swap_x(value), swap_both(value), y)
        return ordered(by_y, other, x).reshape((4 * value.shape[0],) + value.shape[1:])

    def plane_sum(partial):
        sent = partial.astype(jnp.bfloat16).reshape(4, rows, width)
        got = lax.all_to_all(sent, BOTH, 0, 0, axis_index_groups=plane_groups, tiled=True)
        return jnp.sum(got.astype(jnp.float32), axis=0)

    def fetch(weight):
        halves = weight.reshape(share, 2, -1)
        mine = jnp.where(y == 0, halves[:, 0], halves[:, 1])
        theirs = jnp.where(y == 0, halves[:, 1], halves[:, 0])
        pair = ordered(mine, swap_y(theirs), y)
        got = lax.all_gather(pair, "seq", axis=0, tiled=False, axis_index_groups=column_groups)
        got = got.reshape(planes, 2, 2, share, -1)
        return jnp.swapaxes(got, 1, 2).reshape(width, -1)

    def give(grad):
        sent = grad.astype(jnp.bfloat16).reshape(planes, 2, 2, share, -1)
        sent = jnp.swapaxes(sent, 1, 2).reshape(members * 2, share, -1)
        got = lax.psum_scatter(
            sent, "seq", scatter_dimension=0, tiled=True, axis_index_groups=column_groups
        )
        mine = jnp.where(y == 0, got[0], got[1])
        theirs = jnp.where(y == 0, got[1], got[0])
        pair = ordered(mine, swap_y(theirs), y).astype(jnp.float32)
        return jnp.concatenate([pair[0], pair[1]], axis=1)

    gains = lax.all_gather(
        jnp.concatenate(
            [norm1_gain[:, None], norm2_gain[:, None], conv_kernel], axis=1
        ),
        "seq",
        axis=0,
        tiled=True,
    ).astype(jnp.float32)
    gain_one, gain_two, kernel = gains[:, 0], gains[:, 1], gains[:, 2:]
    taps = kernel.shape[1]
    margin = taps - 1
    channels = in_weight.shape[2] // 2
    first_channel = x * (2 * channels) + y * channels
    kernel_here = lax.dynamic_slice_in_dim(kernel, first_channel, channels, 0)

    w_in_halves = jnp.swapaxes(in_weight.reshape(share, 3, 2, channels), 1, 2)
    w_mixer = fetch(
        jnp.concatenate(
            [w_in_halves.reshape(share, 2, 3 * channels), out_weight.reshape(share, 2, channels)],
            axis=2,
        ).reshape(share, 8 * channels)
    )
    w_in, w_out = w_mixer[:, : 3 * channels], w_mixer[:, 3 * channels :]

    hidden = tokens[0].astype(jnp.float32)
    normed, scale_one = root_norm(hidden, gain_one)
    normed_low = plane_gather(normed.astype(jnp.bfloat16))
    grad_low = plane_gather(d_out[0])

    w_gate = fetch(gate_weight)
    w_up = fetch(up_weight)
    w_down = fetch(down_weight)

    projected = times(normed_low, w_in).reshape(2, 2, rows, 3 * channels)
    b_part = projected[..., :channels]
    c_part = projected[..., channels : 2 * channels]
    x_part = projected[..., 2 * channels :]
    gated = (b_part * x_part).astype(jnp.bfloat16)

    def swap_core(value):
        return moved(value, lambda z, y, c, x: (z, y, 1 - c, x))

    def to_next(value):
        return moved(
            value, lambda z, y, c, x: (z + 1, y, 0, x) if c == 1 and z + 1 < planes else None
        )

    def to_last(value):
        return moved(value, lambda z, y, c, x: (z - 1, y, 1, x) if c == 0 and z > 0 else None)

    tail = gated[:, :, rows - margin :]
    from_core, from_plane = swap_core(tail), to_next(tail[:, 1])
    before = jnp.where(
        c == 1, from_core, jnp.stack([from_plane, from_core[:, 0]], axis=1)
    )
    padded = jnp.concatenate([before, gated], axis=2).astype(jnp.float32)
    seq_len = lax.axis_size("seq") * rows // SEQS
    block = z * 4 + jnp.arange(2, dtype=jnp.int32) * 2 + c
    position = block[:, None] * rows + jnp.arange(rows, dtype=jnp.int32)
    in_sequence = position % seq_len
    masks = [
        (in_sequence >= margin - offset).astype(jnp.float32)[None, :, :, None]
        for offset in range(taps)
    ]
    conv = jnp.zeros_like(b_part)
    for offset in range(taps):
        conv = conv + masks[offset] * padded[:, :, offset : offset + rows] * kernel_here[:, offset]
    mixed = (c_part * conv).astype(jnp.bfloat16).reshape(4 * rows, channels)
    hidden_one = hidden + plane_sum(times_transposed(mixed, w_out))

    normed_two, scale_two = root_norm(hidden_one, gain_two)
    normed_two_low = plane_gather(normed_two.astype(jnp.bfloat16))
    gate = times(normed_two_low, w_gate)
    upper = times(normed_two_low, w_up)
    sigma = jax.nn.sigmoid(gate)
    active = (gate * sigma * upper).astype(jnp.bfloat16)
    d_active = times(grad_low, w_down)
    d_upper = (d_active * gate * sigma).astype(jnp.bfloat16)
    d_gate = (d_active * upper * sigma * (1.0 + gate * (1.0 - sigma))).astype(jnp.bfloat16)
    d_normed_two = plane_sum(times_transposed(d_gate, w_gate) + times_transposed(d_upper, w_up))
    result = hidden_one + plane_sum(times_transposed(active, w_down))
    d_gate_w = give(transposed_times(normed_two_low, d_gate))
    d_up_w = give(transposed_times(normed_two_low, d_upper))
    d_down_w = give(transposed_times(grad_low, active))

    d_hidden_two, d_gain_two = norm_back(d_normed_two, hidden_one, scale_two, gain_two)
    grad_one = d_out[0].astype(jnp.float32) + d_hidden_two
    grad_one_low = plane_gather(grad_one.astype(jnp.bfloat16))
    d_out_w = transposed_times(grad_one_low, mixed)
    d_mixed = times(grad_one_low, w_out).reshape(2, 2, rows, channels)
    d_c = d_mixed * conv
    d_conv = d_mixed * c_part
    kernel_cols = []
    d_padded = jnp.zeros((2, 2, rows + margin, channels), jnp.float32)
    for offset in range(taps):
        masked = masks[offset] * d_conv
        kernel_cols.append(jnp.sum(masked * padded[:, :, offset : offset + rows], axis=(0, 1, 2)))
        d_padded = d_padded + jnp.pad(
            masked * kernel_here[:, offset],
            ((0, 0), (0, 0), (offset, margin - offset), (0, 0)),
        )
    head = d_padded[:, :, :margin]
    from_core, from_plane = swap_core(head), to_last(head[:, 0])
    after = jnp.where(c == 0, from_core, jnp.stack([from_core[:, 1], from_plane], axis=1))
    d_gated = d_padded[:, :, margin:] + jnp.pad(
        after, ((0, 0), (0, 0), (rows - margin, 0), (0, 0))
    )
    d_projected = (
        jnp.concatenate([d_gated * x_part, d_c, d_gated * b_part], axis=3)
        .astype(jnp.bfloat16)
        .reshape(4 * rows, 3 * channels)
    )
    d_in_w = transposed_times(normed_low, d_projected)
    d_normed = plane_sum(times_transposed(d_projected, w_in))
    d_mixer = give(jnp.concatenate([d_in_w, d_out_w], axis=1)).reshape(share, 2, 4 * channels)
    d_in_w = jnp.swapaxes(d_mixer[:, :, : 3 * channels].reshape(share, 2, 3, channels), 1, 2)
    d_in_w = d_in_w.reshape(share, 3, 2 * channels)
    d_out_w = d_mixer[:, :, 3 * channels :].reshape(share, 2 * channels)
    d_hidden, d_gain_one = norm_back(d_normed, hidden, scale_one, gain_one)
    d_tokens = (grad_one + d_hidden).astype(jnp.bfloat16)

    d_kernel = lax.dynamic_update_slice(
        jnp.zeros((width, taps), jnp.float32), jnp.stack(kernel_cols, axis=1), (first_channel, 0)
    )
    small = jnp.concatenate([d_gain_one[:, None], d_gain_two[:, None], d_kernel], axis=1)
    small = lax.psum(small, BOTH)
    small = lax.dynamic_slice_in_dim(small, here * share, share, 0)
    return (
        result.astype(jnp.bfloat16)[None],
        d_tokens[None],
        small[:, 0],
        d_in_w,
        small[:, 2:],
        d_out_w,
        small[:, 1],
        d_gate_w,
        d_up_w,
        d_down_w,
    )


class Place:
    def __init__(self, planes):
        self.planes = planes
        self.me, self.x = lax.axis_index("seq"), lax.axis_index("fsdp")
        self.z = lax.div(self.me, 4)
        self.y = lax.rem(lax.div(self.me, 2), 2)
        self.c = lax.rem(self.me, 2)
        self.core = (self.me + 1 - 2 * self.c, self.x)
        self.across = (self.me + 2 - 4 * self.y, self.x)
        self.low, self.high = (self.me - 4, self.x), (self.me + 4, self.x)
        self.has_low, self.has_high = self.z > 0, self.z < planes - 1
        self.block = self.x * 2 + self.y
        self.beside = (self.me, 1 - self.x)
        self.beside_block = (1 - self.x) * 2 + self.y
        self.across_block = self.x * 2 + 1 - self.y
        self.far_block = (1 - self.x) * 2 + 1 - self.y
        self.is_first, self.is_last = self.c == 0, self.c == 1
        self.gives_next = jnp.logical_and(self.is_last, self.has_high)
        self.gives_last = jnp.logical_and(self.is_first, self.has_low)
        self.next, self.last = (self.me + 3, self.x), (self.me - 3, self.x)


def remote(source, target, send, receive, device_id):
    return pltpu.make_async_remote_copy(
        src_ref=source,
        dst_ref=target,
        send_sem=send,
        recv_sem=receive,
        device_id=device_id,
        device_id_type=MESH,
    )


def signal(semaphore, device_id):
    pl.semaphore_signal(semaphore, inc=1, device_id=device_id, device_id_type=MESH)


def dot(left, right):
    return jnp.dot(left, right, preferred_element_type=jnp.float32)


def kernel(
    planes,
    parts,
    seq_len,
    weights,
    tokens,
    d_out,
    gains_here,
    result,
    d_tokens,
    own_grad,
    other_grad,
    small,
    kept_weights,
    kept_mixer,
    w,
    core_in,
    extra,
    n_one,
    f_all,
    n_two,
    e_all,
    sent_a,
    sent_b,
    total_a,
    total_b,
    got_a,
    got_b,
    gated,
    d_conv,
    mixed,
    active,
    d_gate_up,
    hidden_one,
    d_hidden,
    halo,
    gains_in,
    gains,
    taps,
    small_in,
    gain_send,
    gain_recv,
    small_send,
    small_recv,
    local_sem,
    y_send,
    y_recv,
    z_send,
    z_recv,
    c_send,
    c_recv,
    core_send,
    core_recv,
    core_free,
    sum_send,
    sum_recv,
    ready,
    last_send,
    last_recv,
    own_sem,
    all_send,
    all_recv,
    part_send,
    part_recv,
    halo_send,
    halo_recv,
    keep_sem,
):
    at = Place(planes)
    z, y, c = at.z, at.y, at.c
    rows, width = tokens.shape
    channels = taps.shape[1]
    count = 4 * planes
    share = weights.shape[2]
    wide = 4 * share
    chunks = parts + 2
    step_cols = weights.shape[3] // 3

    def y_copies(k):
        return (
            pltpu.make_async_copy(weights.at[k, y], w.at[k, z, y, c], local_sem.at[k]),
            remote(weights.at[k, 1 - y], w.at[k, z, y, c], y_send.at[k], y_recv.at[k], at.across),
        )

    def piece(k, p):
        return w.at[k, p, :, c]

    def to_side(k, p, side):
        return remote(
            piece(k, p),
            piece(k, p),
            z_send.at[k, side, p],
            z_recv.at[k, p],
            at.high if side else at.low,
        )

    def to_core(k, p):
        return remote(piece(k, p), piece(k, p), c_send.at[k, p], c_recv.at[k, p], at.core)

    def begin(k):
        for copy in y_copies(k):
            copy.start()

    def own(k):
        y_copies(k)[0].wait()
        remote(
            weights.at[k, y], w.at[k, z, 1 - y, c], y_send.at[k], y_recv.at[k], at.across
        ).wait_recv()
        pl.when(at.has_low)(lambda: to_side(k, z, 0).start())
        pl.when(at.has_high)(lambda: to_side(k, z, 1).start())
        to_core(k, z).start()

    def relay(k, t):
        below, above = z - t, z + t

        @pl.when(below >= 0)
        def _():
            to_side(k, below, 1).wait_recv()
            pl.when(at.has_high)(lambda: to_side(k, below, 1).start())
            to_core(k, below).start()

        @pl.when(above < planes)
        def _():
            to_side(k, above, 0).wait_recv()
            pl.when(at.has_low)(lambda: to_side(k, above, 0).start())
            to_core(k, above).start()

    def relays(k):
        for t in range(1, planes):
            relay(k, t)

    def core_wait(k):
        for p in range(planes):
            remote(
                w.at[k, p, :, 1 - c], w.at[k, p, :, 1 - c], c_send.at[k, p], c_recv.at[k, p], at.core
            ).wait_recv()

    def gather_done(k):
        y_copies(k)[1].wait_send()
        for p in range(planes):
            pl.when(jnp.logical_and(at.has_low, p >= z))(lambda: to_side(k, p, 0).wait_send())
            pl.when(jnp.logical_and(at.has_high, p <= z))(lambda: to_side(k, p, 1).wait_send())
            to_core(k, p).wait_send()

    def chunk_of(v):
        return lax.rem(v + 2, chunks)

    def core_copy(v):
        k = chunk_of(v)
        return remote(
            w.at[k, :, :, 1 - c],
            core_in.at[lax.rem(v, 2)],
            core_send.at[k],
            core_recv.at[k],
            at.core,
        )

    def core_start(v):
        pl.when(v >= 2)(lambda: pl.semaphore_wait(core_free, 1))
        core_copy(v).start()

    def core_add(v):
        k, slot = chunk_of(v), lax.rem(v, 2)
        core_copy(v).wait()

        def add(p, carry):
            total = w[k, p, :, c].astype(jnp.float32) + core_in[slot, p].astype(jnp.float32)
            w[k, p, :, c] = total.astype(jnp.bfloat16)
            return carry

        lax.fori_loop(0, planes, add, 0)
        pl.when(v < chunks - 2)(lambda: signal(core_free, at.core))
        pl.when(at.has_low)(lambda: signal(ready.at[1], at.low))
        pl.when(at.has_high)(lambda: signal(ready.at[0], at.high))

    def landing(k, d):
        return w.at[k, d, :, 1 - c]

    def sum_up(k, d):
        return remote(
            landing(k, d), landing(k, d), sum_send.at[k, 1, d], sum_recv.at[k, 1, d], at.high
        )

    def sum_down(k, d):
        return remote(
            landing(k, d), landing(k, d), sum_send.at[k, 0, d], sum_recv.at[k, 0, d], at.low
        )

    def sum_down_last(k, d):
        return remote(
            landing(k, d), extra.at[k], sum_send.at[k, 0, d], sum_recv.at[k, 0, d], at.low
        )

    def add_here(k, d, arrived):
        here = w[k, d, :, c].astype(jnp.float32)

        @pl.when(arrived)
        def _():
            w[k, d, :, 1 - c] = (w[k, d, :, 1 - c].astype(jnp.float32) + here).astype(jnp.bfloat16)

        @pl.when(jnp.logical_not(arrived))
        def _():
            w[k, d, :, 1 - c] = w[k, d, :, c]

    def add_up(v):
        k = chunk_of(v)
        pl.when(at.has_high)(lambda: pl.semaphore_wait(ready.at[1], 1))
        for d in range(planes - 1, -1, -1):

            @pl.when(d > z)
            def _():
                pl.when(at.has_low)(lambda: sum_up(k, d).wait_recv())
                add_here(k, d, at.has_low)
                sum_up(k, d).start()

            @pl.when(jnp.logical_and(z == d, at.has_low))
            def _():
                sum_up(k, d).wait_recv()
                total = w[k, d, :, c].astype(jnp.float32) + w[k, d, :, 1 - c].astype(jnp.float32)
                w[k, d, :, c] = total.astype(jnp.bfloat16)

    def add_down(v):
        k = chunk_of(v)
        pl.when(at.has_low)(lambda: pl.semaphore_wait(ready.at[0], 1))
        for d in range(planes):

            @pl.when(d < z)
            def _():
                pl.when(at.has_high)(lambda: sum_down(k, d).wait_recv())
                add_here(k, d, at.has_high)
                pl.when(z - 1 > d)(lambda: sum_down(k, d).start())
                pl.when(z - 1 == d)(lambda: sum_down_last(k, d).start())

            @pl.when(jnp.logical_and(z == d, at.has_high))
            def _():
                sum_down_last(k, d).wait_recv()
                total = w[k, d, :, c].astype(jnp.float32) + extra[k].astype(jnp.float32)
                w[k, d, :, c] = total.astype(jnp.bfloat16)

    def give_copies(k):
        return (
            pltpu.make_async_copy(w.at[k, z, y, c], own_grad.at[k], own_sem.at[k]),
            remote(
                w.at[k, z, 1 - y, c], other_grad.at[k], last_send.at[k], last_recv.at[k], at.across
            ),
        )

    def give(v):
        for copy in give_copies(chunk_of(v)):
            copy.start()

    def sum_done(v):
        k = chunk_of(v)
        for d in range(planes):
            pl.when(d > z)(lambda: sum_up(k, d).wait_send())
            pl.when(d < z)(lambda: sum_down(k, d).wait_send())
        for copy in give_copies(k):
            copy.wait()

    def first_hop(v):
        core_add(v)
        pl.when(jnp.logical_not(at.has_low))(lambda: add_up(v))
        pl.when(jnp.logical_not(at.has_high))(lambda: add_down(v))

    def tick(j):
        def stage(o, extra_flag, do):
            there = jnp.logical_and(o >= 0, o < chunks)
            pl.when(jnp.logical_and(there, extra_flag))(lambda: do(o))

        far = jnp.maximum(z, planes - 1 - z)
        stage(j - z, at.has_low, add_up)
        stage(j - (planes - 1 - z), at.has_high, add_down)
        stage(j - far, far >= 0, give)

    part_rows = rows // 2

    def half_of(buffer, block, which_half):
        return buffer.at[block, pl.ds(which_half * part_rows, part_rows), :]

    def all_copy(buffer, which, i):
        block, which_half, to = (
            (at.block, 0, at.beside),
            (at.block, 1, at.across),
            (at.block, 1, at.beside),
            (at.block, 0, at.across),
            (at.beside_block, 0, at.across),
            (at.across_block, 1, at.beside),
        )[i]
        ref = half_of(buffer, block, which_half)
        return remote(ref, ref, all_send.at[which, i], all_recv.at[which, i], to)

    def all_landed(buffer, which, i):
        block, which_half = (
            (at.beside_block, 0),
            (at.across_block, 1),
            (at.beside_block, 1),
            (at.across_block, 0),
            (at.far_block, 0),
            (at.far_block, 1),
        )[i]
        ref = half_of(buffer, block, which_half)
        remote(
            ref, ref, all_send.at[which, i], all_recv.at[which, i], at.across
        ).wait_recv()

    def all_start(buffer, which):
        for i in range(4):
            all_copy(buffer, which, i).start()

    def all_pass(buffer, which):
        for i in range(2):
            all_landed(buffer, which, i)
            all_copy(buffer, which, 4 + i).start()

    def all_wait(buffer, which):
        for i in range(2, 6):
            all_landed(buffer, which, i)

    def all_done(buffer, which):
        for i in range(6):
            all_copy(buffer, which, i).wait_send()

    def part_copy(source, target, which, i):
        block, which_half, slot, to = (
            (at.far_block, 0, 2, at.beside),
            (at.far_block, 1, 2, at.across),
            (at.beside_block, 0, 0, at.beside),
            (at.across_block, 1, 1, at.across),
            (at.across_block, 0, 1, at.across),
            (at.beside_block, 1, 0, at.beside),
        )[i]
        return remote(
            half_of(source, block, which_half),
            half_of(target, slot, which_half),
            part_send.at[which, i],
            part_recv.at[which, i],
            to,
        )

    def part_start(source, target, which):
        for i in range(4):
            part_copy(source, target, which, i).start()

    def part_pass(source, target, which):
        for i, block in enumerate((at.across_block, at.beside_block)):
            part_copy(source, target, which, i).wait_recv()
            here = pl.ds(i * part_rows, part_rows)
            total = source[block, here, :].astype(jnp.float32)
            total = total + target[2, here, :].astype(jnp.float32)
            source[block, here, :] = total.astype(jnp.bfloat16)
            part_copy(source, target, which, 4 + i).start()

    def part_wait(source, target, which):
        for i in range(2, 6):
            part_copy(source, target, which, i).wait_recv()

    def part_done(source, target, which):
        for i in range(6):
            part_copy(source, target, which, i).wait_send()

    tile = 48

    def by_rows(body):
        def run(i, carry):
            body(pl.ds(pl.multiple_of(i * tile, tile), tile))
            return carry

        lax.fori_loop(0, rows // tile, run, 0)

    def scale_of(hidden):
        return lax.rsqrt(jnp.mean(hidden * hidden, axis=-1, keepdims=True) + EPSILON)

    def summed(source, target, span):
        total = source[at.block, span, :].astype(jnp.float32)
        for i in range(2):
            total = total + target[i, span, :].astype(jnp.float32)
        return total

    def back_through_norm(grad, hidden, gain, row):
        scale = scale_of(hidden)
        weighted = grad * gain
        inner = jnp.sum(weighted * hidden, axis=-1, keepdims=True)
        small[row : row + 1, :] += jnp.sum(grad * hidden * scale, axis=0, keepdims=True)
        return scale * weighted - hidden * (scale * scale * scale) * inner / width

    def transposed(buffer, k):
        def one(p, carry):
            cols = pl.ds(pl.multiple_of(p * wide, wide), wide)
            block = buffer[:, :, cols].reshape(4 * rows, wide).T
            w[k, p] = block.reshape(2, 2, share, 4 * rows)
            return carry

        lax.fori_loop(0, planes, one, 0)

    def whole(k, low, high):
        return w[k, :, :, :, :, low:high].reshape(planes * wide, high - low)

    def plane_rows(k, p, low, high):
        return w[k, p, :, :, :, low:high].reshape(wide, high - low)

    def pair(t):
        return pl.ds(2 * t, 2)

    def columns(p):
        return pl.ds(pl.multiple_of(p * wide, wide), wide)

    halo[...] = jnp.zeros_like(halo)
    barrier = pltpu.get_barrier_semaphore()
    signal(barrier, at.beside)

    def greet(t, carry):
        signal(barrier, (lax.rem(at.me + t, count), at.x))
        return carry

    lax.fori_loop(1, count, greet, 0)
    pl.semaphore_wait(barrier, count)

    def gain_copy(t):
        other = lax.rem(at.me + t, count)
        return remote(
            gains_here,
            gains_in.at[at.me],
            gain_send.at[t],
            gain_recv.at[t],
            (other, at.x),
        )

    def gain_start(t, carry):
        gain_copy(t).start()
        return carry

    def gain_wait(t, carry):
        gain_copy(t).wait()
        return carry

    lax.fori_loop(1, count, gain_start, 0)
    begin(0)
    begin(1)
    e_copy = pltpu.make_async_copy(d_out, e_all.at[at.block], keep_sem.at[0])
    e_copy.start()
    small[...] = jnp.zeros_like(small)
    gains_in[at.me] = gains_here[...]
    lax.fori_loop(1, count, gain_wait, 0)
    for d in range(count):
        found = gains_in[d].astype(jnp.float32)[0:8, :share]
        gains[:, d * share : (d + 1) * share] = found
    channel_columns = pl.ds(pl.multiple_of(at.block * channels, channels), channels)
    taps[...] = gains[:, channel_columns]

    def first_norm(span):
        hidden = tokens[span, :].astype(jnp.float32)
        n_one[at.block, span, :] = (hidden * scale_of(hidden) * gains[0:1, :]).astype(jnp.bfloat16)

    by_rows(first_norm)
    all_start(n_one, 0)
    for k in range(2, 5):
        begin(k)
    own(0)
    own(1)
    relay(0, 1)
    all_pass(n_one, 0)
    relay(1, 1)
    own(2)
    for t in range(2, planes):
        relay(0, t)
    e_copy.wait()
    all_start(e_all, 1)
    begin(5)
    relay(1, 2)
    core_wait(0)
    all_wait(n_one, 0)

    def project_c(t, carry):
        normed = n_one[pair(t)].reshape(2 * rows, width)
        c_part = dot(normed, whole(0, 0, channels))
        total_a[pair(t), :, channels : 2 * channels] = c_part.reshape(2, rows, channels)
        return carry

    def project_b_x(t, carry):
        normed = n_one[pair(t)].reshape(2 * rows, width)
        b_x = dot(normed, whole(1, 0, 2 * channels)).reshape(2, rows, 2 * channels)
        total_a[pair(t), :, 0:channels] = b_x[:, :, :channels]
        total_a[pair(t), :, 2 * channels : 3 * channels] = b_x[:, :, channels:]
        product = (b_x[:, :, :channels] * b_x[:, :, channels:]).astype(jnp.bfloat16)
        gated[pair(t), 8 : 8 + rows, :] = product.astype(jnp.float32)
        return carry

    lax.fori_loop(0, 2, project_c, 0)
    for t in range(3, planes):
        relay(1, t)
    own(3)
    all_pass(e_all, 1)
    core_wait(1)
    lax.fori_loop(0, 2, project_b_x, 0)

    def halo_core(which, edge):
        return remote(
            edge, halo.at[2 * which], halo_send.at[2 * which], halo_recv.at[2 * which], at.core
        )

    def halo_plane(which, edge, target):
        return remote(
            edge,
            halo.at[2 * which + 1],
            halo_send.at[2 * which + 1],
            halo_recv.at[2 * which + 1],
            target,
        )

    tail = gated.at[:, pl.ds(rows, 8), :]
    halo_core(0, tail).start()
    pl.when(at.gives_next)(lambda: halo_plane(0, tail, at.next).start())
    halo_core(0, tail).wait_recv()
    pl.when(at.gives_last)(lambda: halo_plane(0, tail, at.last).wait_recv())
    for group in range(2):

        @pl.when(at.is_last)
        def _():
            gated[2 * group, 0:8, :] = halo[0, 2 * group]
            gated[2 * group + 1, 0:8, :] = halo[0, 2 * group + 1]

        @pl.when(at.is_first)
        def _():
            gated[2 * group, 0:8, :] = halo[1, 2 * group + 1]
            gated[2 * group + 1, 0:8, :] = halo[0, 2 * group]

    def start_of(block):
        return lax.rem((z * 4 + lax.rem(block, 2) * 2 + c) * rows, seq_len)

    def place_in(block, ahead):
        place = start_of(block) + ahead + lax.broadcasted_iota(jnp.int32, (rows, channels), 0)
        return jnp.where(place >= seq_len, place - seq_len, place)

    def convolve(b, carry):
        place = place_in(b, 0)
        conv = jnp.zeros((rows, channels), jnp.float32)
        for j in range(3):
            moved = gated[b, 6 + j : 6 + j + rows, :]
            conv = conv + jnp.where(place >= 2 - j, moved, 0.0) * taps[2 + j : 3 + j, :]
        total_a[b, :, 3 * channels : 4 * channels] = conv
        mixed[b] = (total_a[b, :, channels : 2 * channels] * conv).astype(jnp.bfloat16)
        return carry

    lax.fori_loop(0, 4, convolve, 0)

    def branch(i, carry):
        t, p = lax.div(i, planes), lax.rem(i, planes)
        left = mixed[pair(t)].reshape(2 * rows, channels)
        out = times_transposed(left, plane_rows(0, p, channels, 2 * channels))
        sent_a[pair(t), :, columns(p)] = out.reshape(2, rows, wide).astype(jnp.bfloat16)
        return carry

    lax.fori_loop(0, 2 * planes, branch, 0)
    part_start(sent_a, got_a, 0)
    gather_done(0)
    gather_done(1)
    keep_weights = pltpu.make_async_copy(w.at[pl.ds(0, 2)], kept_weights, keep_sem.at[1])
    keep_mixer = pltpu.make_async_copy(total_a, kept_mixer, keep_sem.at[2])
    keep_weights.start()
    keep_mixer.start()
    own(4)
    begin(6)
    relay(2, 1)
    part_pass(sent_a, got_a, 0)
    for t in range(2, planes):
        relay(2, t)
    keep_weights.wait()
    keep_mixer.wait()
    total_a[...] = jnp.zeros_like(total_a)
    total_b[...] = jnp.zeros_like(total_b)
    all_wait(e_all, 1)
    transposed(e_all, 1)
    relay(3, 1)
    part_wait(sent_a, got_a, 0)

    def second_norm(span):
        hidden = tokens[span, :].astype(jnp.float32) + summed(sent_a, got_a, span)
        hidden_one[span, :] = hidden
        n_two[at.block, span, :] = (hidden * scale_of(hidden) * gains[1:2, :]).astype(jnp.bfloat16)

    by_rows(second_norm)
    all_start(n_two, 2)
    begin(7)
    part_done(sent_a, got_a, 0)
    own(5)
    relay(3, 2)
    all_pass(n_two, 2)
    begin(8)
    for t in range(3, planes):
        relay(3, t)
    own(6)
    relay(4, 1)
    all_wait(n_two, 2)
    transposed(n_two, 0)
    own(7)
    relay(4, 2)

    steps = planes - 1

    def relay_step(r):
        k = 4 + lax.div(r + 2, steps)
        pl.when(k < chunks)(lambda: relay(k, 1 + lax.rem(r + 2, steps)))

    def feed_forward(k):
        def half(t, carry):
            normed = n_two[pair(t)].reshape(2 * rows, width)
            both = dot(normed, whole(k, 0, 2 * step_cols))
            d_active = dot(
                e_all[pair(t)].reshape(2 * rows, width), whole(k, 2 * step_cols, 3 * step_cols)
            )
            gate, upper = both[:, :step_cols], both[:, step_cols:]
            sigma = jax.nn.sigmoid(gate)
            soft = gate * sigma
            here = pl.ds(pl.multiple_of(t * 2 * rows, 2 * rows), 2 * rows)
            active[here, :] = (soft * upper).astype(jnp.bfloat16)
            d_gate_up[here, step_cols:] = (d_active * soft).astype(jnp.bfloat16)
            d_gate_up[here, :step_cols] = (
                d_active * upper * sigma * (1.0 + gate * (1.0 - sigma))
            ).astype(jnp.bfloat16)

            def spread(p, inner):
                back = times_transposed(d_gate_up[here, :], plane_rows(k, p, 0, 2 * step_cols))
                total_b[pair(t), :, columns(p)] += back.reshape(2, rows, wide)
                out = times_transposed(
                    active[here, :], plane_rows(k, p, 2 * step_cols, 3 * step_cols)
                )
                total_a[pair(t), :, columns(p)] += out.reshape(2, rows, wide)
                return inner

            lax.fori_loop(0, planes, spread, 0)
            pl.when(k < chunks - 1)(lambda: relay_step(2 * (k - 2) + t))
            return carry

        lax.fori_loop(0, 2, half, 0)
        gather_done(k)

        def grads(p, carry):
            low = dot(w[0, p].reshape(wide, 4 * rows), d_gate_up[...])
            w[k, p, :, :, :, 0 : 2 * step_cols] = low.astype(jnp.bfloat16).reshape(
                2, 2, share, 2 * step_cols
            )
            high = dot(w[1, p].reshape(wide, 4 * rows), active[...])
            w[k, p, :, :, :, 2 * step_cols : 3 * step_cols] = high.astype(jnp.bfloat16).reshape(
                2, 2, share, step_cols
            )
            return carry

        lax.fori_loop(0, planes, grads, 0)

    def one_part(i, carry):
        k = i + 2
        pl.when(i > 0)(lambda: first_hop(i - 1))
        pl.when(i == 1)(lambda: own(8))
        core_wait(k)
        feed_forward(k)
        core_start(i)
        pl.when(jnp.logical_and(i >= 3, i <= 4))(lambda: tick(i - 2))

        @pl.when(i == parts - 2)
        def _():
            for r in range(2 * (parts - 1), 5 * steps - 2):
                relay_step(jnp.int32(r))

        return carry

    lax.fori_loop(0, parts, one_part, 0)

    restore_weights = pltpu.make_async_copy(kept_weights, w.at[pl.ds(0, 2)], keep_sem.at[1])
    restore_weights.start()

    def cast(source, target):
        def run(b, carry):
            target[b] = source[b].astype(jnp.bfloat16)
            return carry

        lax.fori_loop(0, 4, run, 0)

    cast(total_b, sent_a)
    part_start(sent_a, got_a, 2)
    cast(total_a, sent_b)
    restore_mixer = pltpu.make_async_copy(kept_mixer, total_a, keep_sem.at[2])
    restore_mixer.start()
    first_hop(jnp.int32(parts - 1))
    part_pass(sent_a, got_a, 2)
    tick(3)
    part_wait(sent_a, got_a, 2)

    def through_second(span):
        grad = back_through_norm(
            summed(sent_a, got_a, span), hidden_one[span, :], gains[1:2, :], 1
        )
        grad = e_all[at.block, span, :].astype(jnp.float32) + grad
        d_hidden[span, :] = grad
        f_all[at.block, span, :] = grad.astype(jnp.bfloat16)

    by_rows(through_second)
    all_start(f_all, 3)
    part_done(sent_a, got_a, 2)
    tick(4)
    all_pass(f_all, 3)
    part_start(sent_b, got_b, 1)
    sum_done(0)
    transposed(n_one, 2)
    all_done(n_two, 2)
    restore_weights.wait()
    restore_mixer.wait()
    tick(5)
    all_wait(f_all, 3)

    def into_mixer(t, carry):
        grad = f_all[pair(t)].reshape(2 * rows, width)
        d_mixed = dot(grad, whole(0, channels, 2 * channels)).reshape(2, rows, channels)
        conv = total_a[pair(t), :, 3 * channels : 4 * channels]
        c_part = total_a[pair(t), :, channels : 2 * channels]
        n_two[pair(t), :, channels : 2 * channels] = (d_mixed * conv).astype(jnp.bfloat16)
        d_conv[pair(t), 0:rows, :] = d_mixed * c_part
        return carry

    lax.fori_loop(0, 2, into_mixer, 0)
    head = d_conv.at[:, pl.ds(0, 8), :]
    halo_core(1, head).start()
    pl.when(at.gives_last)(lambda: halo_plane(1, head, at.last).start())

    def from_c(i, carry):
        t, p = lax.div(i, planes), lax.rem(i, planes)
        grad = n_two[pair(t), :, channels : 2 * channels].reshape(2 * rows, channels)
        out = times_transposed(grad, plane_rows(0, p, 0, channels))
        total_b[pair(t), :, columns(p)] = out.reshape(2, rows, wide)
        return carry

    lax.fori_loop(0, 2 * planes, from_c, 0)
    sum_done(1)
    transposed(f_all, 3)

    def c_and_out_weight(p, carry):
        d_c = n_two[:, :, channels : 2 * channels].reshape(4 * rows, channels)
        grad = dot(w[2, p].reshape(wide, 4 * rows), d_c).astype(jnp.bfloat16)
        w[0, p, :, :, :, 0:channels] = grad.reshape(2, 2, share, channels)
        grad = dot(w[3, p].reshape(wide, 4 * rows), mixed[...].reshape(4 * rows, channels))
        w[0, p, :, :, :, channels : 2 * channels] = grad.astype(jnp.bfloat16).reshape(
            2, 2, share, channels
        )
        return carry

    lax.fori_loop(0, planes, c_and_out_weight, 0)
    core_start(jnp.int32(parts))
    halo_core(1, head).wait_recv()
    pl.when(at.gives_next)(lambda: halo_plane(1, head, at.next).wait_recv())
    for group in range(2):

        @pl.when(at.is_first)
        def _():
            d_conv[2 * group, rows : rows + 8, :] = halo[2, 2 * group]
            d_conv[2 * group + 1, rows : rows + 8, :] = halo[2, 2 * group + 1]

        @pl.when(at.is_last)
        def _():
            d_conv[2 * group, rows : rows + 8, :] = halo[2, 2 * group + 1]
            d_conv[2 * group + 1, rows : rows + 8, :] = halo[3, 2 * group]

    def convolve_back(b, carry):
        place = place_in(b, 0)
        d_gated = jnp.zeros((rows, channels), jnp.float32)
        for j in range(3):
            ahead = 2 - j
            moved = jnp.where(
                place_in(b, ahead) >= ahead, d_conv[b, ahead : ahead + rows, :], 0.0
            )
            d_gated = d_gated + moved * taps[2 + j : 3 + j, :]
            product = d_conv[b, 0:rows, :] * gated[b, 6 + j : 6 + j + rows, :]
            small[2 + j : 3 + j, channel_columns] += jnp.sum(
                jnp.where(place >= ahead, product, 0.0), axis=0, keepdims=True
            )
        x_part = total_a[b, :, 2 * channels : 3 * channels]
        n_two[b, :, 0:channels] = (d_gated * x_part).astype(jnp.bfloat16)
        b_part = total_a[b, :, 0:channels]
        n_two[b, :, 2 * channels : 3 * channels] = (d_gated * b_part).astype(jnp.bfloat16)
        return carry

    lax.fori_loop(0, 4, convolve_back, 0)
    first_hop(jnp.int32(parts))

    def d_normed(i, carry):
        t, p = lax.div(i, planes), lax.rem(i, planes)
        grad = n_two[pair(t), :, 0:channels].reshape(2 * rows, channels)
        out = times_transposed(grad, plane_rows(1, p, 0, channels))
        grad = n_two[pair(t), :, 2 * channels : 3 * channels].reshape(2 * rows, channels)
        out = out + times_transposed(grad, plane_rows(1, p, channels, 2 * channels))
        out = total_b[pair(t), :, columns(p)] + out.reshape(2, rows, wide)
        sent_a[pair(t), :, columns(p)] = out.astype(jnp.bfloat16)
        return carry

    lax.fori_loop(0, 2 * planes, d_normed, 0)
    part_start(sent_a, got_a, 3)

    def b_and_x_weight(p, carry):
        normed = w[2, p].reshape(wide, 4 * rows)
        for low, here in ((0, 0), (channels, 2 * channels)):
            grad = n_two[:, :, here : here + channels].reshape(4 * rows, channels)
            grad = dot(normed, grad).astype(jnp.bfloat16)
            w[1, p, :, :, :, low : low + channels] = grad.reshape(2, 2, share, channels)
        return carry

    lax.fori_loop(0, planes, b_and_x_weight, 0)
    core_start(jnp.int32(parts + 1))
    tick(6)
    part_pass(sent_a, got_a, 3)
    first_hop(jnp.int32(parts + 1))
    tick(7)
    part_pass(sent_b, got_b, 1)
    tick(8)
    part_wait(sent_a, got_a, 3)

    def through_first(span):
        hidden = tokens[span, :].astype(jnp.float32)
        grad = back_through_norm(summed(sent_a, got_a, span), hidden, gains[0:1, :], 0)
        d_tokens[span, :] = (d_hidden[span, :] + grad).astype(jnp.bfloat16)

    by_rows(through_first)

    def small_copy(i, to):
        return remote(small, small_in.at[i], small_send.at[i], small_recv.at[i], to)

    def small_plane(t):
        to = lax.rem(at.me + 4 * t, count)
        return remote(
            small, small_in.at[2 + t], small_send.at[2 + t], small_recv.at[2 + t], (to, at.x)
        )

    small_copy(0, at.core).start()
    tick(9)
    for i, (here, following) in enumerate(
        ((at.core, at.beside), (at.beside, at.across), (at.across, None))
    ):
        small_copy(i, here).wait()
        small[...] += small_in[i]
        if following is not None:
            small_copy(i + 1, following).start()
    for t in range(1, planes):
        small_plane(t).start()
    tick(10)
    for t in range(1, planes):
        small_plane(t).wait()
    for t in range(1, planes):
        small[...] += small_in[2 + t]
    part_wait(sent_b, got_b, 1)

    def last_out(span):
        result[span, :] = (hidden_one[span, :] + summed(sent_b, got_b, span)).astype(jnp.bfloat16)

    by_rows(last_out)
    for j in range(11, chunks + planes - 1):
        tick(j)

    part_done(sent_a, got_a, 3)
    all_done(e_all, 1)
    part_done(sent_b, got_b, 1)
    all_done(n_one, 0)
    all_done(f_all, 3)
    halo_core(0, tail).wait_send()
    halo_core(1, head).wait_send()
    pl.when(at.gives_next)(lambda: halo_plane(0, tail, at.next).wait_send())
    pl.when(at.gives_last)(lambda: halo_plane(1, head, at.last).wait_send())
    for v in range(2, chunks):
        sum_done(v)


def one_kernel(planes, seq_len, weights, tokens, d_out, gains):
    chunks, _, share, cols = weights.shape
    parts = chunks - 2
    rows, width = tokens.shape
    channels = width // 4
    low, full = jnp.bfloat16, jnp.float32
    shape = jax.ShapeDtypeStruct
    vmem, anywhere = pl.BlockSpec(memory_space=pltpu.VMEM), pl.BlockSpec(memory_space=pl.ANY)
    dma = pltpu.SemaphoreType.DMA
    block = (4, rows, width)
    return pl.pallas_call(
        functools.partial(kernel, planes, parts, seq_len),
        out_shape=(
            shape((rows, width), low),
            shape((rows, width), low),
            shape((chunks, share, cols), low),
            shape((chunks, share, cols), low),
            shape((8, width), full),
            shape((2, planes, 2, 2, share, cols), low),
            shape(block, full),
        ),
        in_specs=[anywhere, vmem, anywhere, vmem],
        out_specs=[vmem, vmem, anywhere, anywhere, vmem, anywhere, anywhere],
        scratch_shapes=[
            pltpu.VMEM((chunks, planes, 2, 2, share, cols), low),
            pltpu.VMEM((2, planes, 2, share, cols), low),
            pltpu.VMEM((chunks, 2, share, cols), low),
            pltpu.VMEM(block, low),
            pltpu.VMEM(block, low),
            pltpu.VMEM(block, low),
            pltpu.VMEM(block, low),
            pltpu.VMEM(block, low),
            pltpu.VMEM(block, low),
            pltpu.VMEM(block, full),
            pltpu.VMEM(block, full),
            pltpu.VMEM((3, rows, width), low),
            pltpu.VMEM((3, rows, width), low),
            pltpu.VMEM((4, rows + 8, channels), full),
            pltpu.VMEM((4, rows + 8, channels), full),
            pltpu.VMEM((4, rows, channels), low),
            pltpu.VMEM((4 * rows, PART), low),
            pltpu.VMEM((4 * rows, 2 * PART), low),
            pltpu.VMEM((rows, width), full),
            pltpu.VMEM((rows, width), full),
            pltpu.VMEM((4, 4, 8, channels), full),
            pltpu.VMEM((4 * planes,) + gains.shape, low),
            pltpu.VMEM((8, width), full),
            pltpu.VMEM((8, channels), full),
            pltpu.VMEM((2 + planes, 8, width), full),
            dma((4 * planes,)),
            dma((4 * planes,)),
            dma((2 + planes,)),
            dma((2 + planes,)),
            dma((chunks,)),
            dma((chunks,)),
            dma((chunks,)),
            dma((chunks, 2, planes)),
            dma((chunks, planes)),
            dma((chunks, planes)),
            dma((chunks, planes)),
            dma((chunks,)),
            dma((chunks,)),
            pltpu.SemaphoreType.REGULAR,
            dma((chunks, 2, planes)),
            dma((chunks, 2, planes)),
            pltpu.SemaphoreType.REGULAR((2,)),
            dma((chunks,)),
            dma((chunks,)),
            dma((chunks,)),
            dma((4, 6)),
            dma((4, 6)),
            dma((4, 6)),
            dma((4, 6)),
            dma((4,)),
            dma((4,)),
            dma((3,)),
        ],
        compiler_params=pltpu.CompilerParams(
            collective_id=0, has_side_effects=True, vmem_limit_bytes=64 * 1024 * 1024
        ),
    )(weights, tokens, d_out, gains)


def on_device(
    tokens,
    norm1_gain,
    in_weight,
    conv_kernel,
    out_weight,
    norm2_gain,
    gate_weight,
    up_weight,
    down_weight,
    d_out,
):
    planes = lax.axis_size("seq") // 4
    here = lax.axis_index("seq")
    y, x = (here // 2) % 2, lax.axis_index("fsdp")
    rows, width = tokens.shape[1:]
    share = gate_weight.shape[0]
    channels = in_weight.shape[2] // 2
    hidden = gate_weight.shape[1] // 2
    parts = -(-hidden // PART)

    gains = jnp.concatenate([norm1_gain[None], norm2_gain[None], conv_kernel.T], axis=0)
    gains = jnp.pad(gains, ((0, 16 - gains.shape[0]), (0, 128 - share)))

    mixer = jnp.concatenate(
        [in_weight.reshape(share, 3, 2, channels), out_weight.reshape(share, 1, 2, channels)],
        axis=1,
    )
    mixer = mixer[:, (1, 3, 0, 2)].reshape(share, 2, 2, 2, channels).transpose(1, 3, 0, 2, 4)
    mixer = mixer.reshape(2, 2, share, 2 * channels)

    def in_parts(weight):
        halves = jnp.pad(
            weight.reshape(share, 2, hidden), ((0, 0), (0, 0), (0, parts * PART - hidden))
        )
        return halves.reshape(share, 2, parts, PART).transpose(2, 1, 0, 3)

    ffn = jnp.concatenate(
        [in_parts(gate_weight), in_parts(up_weight), in_parts(down_weight)], axis=3
    )
    weights = jnp.concatenate([mixer, ffn], axis=0)
    result, d_tokens, own_grad, other_grad, small, _, _ = one_kernel(
        planes,
        lax.axis_size("seq") * rows // SEQS,
        weights,
        tokens[0],
        d_out[0],
        gains,
    )
    both = jnp.where(
        y == 0, jnp.stack([own_grad, other_grad]), jnp.stack([other_grad, own_grad])
    )
    d_mixer = both[:, :2].reshape(2, 2, share, 2, channels).transpose(2, 1, 3, 0, 4)
    d_mixer = d_mixer.reshape(share, 4, 2 * channels)[:, (2, 0, 3, 1)].astype(jnp.float32)

    def whole_grad(which):
        grad = both[:, 2:, :, which * PART : (which + 1) * PART].transpose(2, 0, 1, 3)
        grad = grad.reshape(share, 2, parts * PART)[:, :, :hidden]
        return grad.reshape(share, 2 * hidden).astype(jnp.float32)

    sums = lax.dynamic_slice_in_dim(small, here * share, share, 1)
    return (
        result[None],
        d_tokens[None],
        sums[0],
        d_mixer[:, :3],
        sums[2:5].T,
        d_mixer[:, 3],
        sums[1],
        whole_grad(0),
        whole_grad(1),
        whole_grad(2),
    )


def fits(mesh):
    return mesh.shape["seq"] <= 16


def solution(mesh):
    return jax.shard_map(
        on_device if fits(mesh) else plain_on_device,
        mesh=mesh,
        in_specs=(
            P("fsdp", "seq", None),
            P("seq"),
            P("seq", None, "fsdp"),
            P("seq", None),
            P("seq", "fsdp"),
            P("seq"),
            P("seq", "fsdp"),
            P("seq", "fsdp"),
            P("seq", "fsdp"),
            P("fsdp", "seq", None),
        ),
        out_specs=(
            P("fsdp", "seq", None),
            P("fsdp", "seq", None),
            P("seq"),
            P("seq", None, "fsdp"),
            P("seq", None),
            P("seq", "fsdp"),
            P("seq"),
            P("seq", "fsdp"),
            P("seq", "fsdp"),
            P("seq", "fsdp"),
        ),
        check_vma=False,
    )
```

```python
import functools

import jax
import jax.numpy as jnp
from jax import lax
from jax.experimental import pallas as pl
from jax.experimental.pallas import tpu as pltpu
from jax.sharding import PartitionSpec as P

SEQS = 3
EPSILON = 1e-05
BOTH = ("seq", "fsdp")
MESH = pl.DeviceIdType.MESH
PART = 256


def times_transposed(left, right):
    return lax.dot_general(
        left, right, (((1,), (1,)), ((), ())), preferred_element_type=jnp.float32
    )


def transposed_times(left, right):
    return lax.dot_general(
        left, right, (((0,), (0,)), ((), ())), preferred_element_type=jnp.float32
    )


def times(left, right):
    return jnp.dot(left, right, preferred_element_type=jnp.float32)


def root_norm(hidden, gain):
    scale = lax.rsqrt(jnp.mean(hidden * hidden, axis=-1, keepdims=True) + EPSILON)
    return (hidden * scale * gain, scale)


def norm_back(grad, hidden, scale, gain):
    weighted = grad * gain
    inner = jnp.sum(weighted * hidden, axis=-1, keepdims=True)
    d_hidden = scale * weighted - hidden * (scale * scale * scale) * inner / hidden.shape[-1]
    d_gain = jnp.sum(grad * hidden * scale, axis=0)
    return (d_hidden, d_gain)


def device(z, y, c, x):
    return (z * 4 + y * 2 + c) * 2 + x


def every(planes):
    return [
        (z, y, c, x) for z in range(planes) for y in range(2) for c in range(2) for x in range(2)
    ]


def plain_on_device(
    tokens,
    norm1_gain,
    in_weight,
    conv_kernel,
    out_weight,
    norm2_gain,
    gate_weight,
    up_weight,
    down_weight,
    d_out,
):
    planes = lax.axis_size("seq") // 4
    here = lax.axis_index("seq")
    y, c, x = (here // 2) % 2, here % 2, lax.axis_index("fsdp")
    z = here // 4
    rows, width = tokens.shape[1:]
    share = gate_weight.shape[0]
    plane_groups = [
        [device(z, y, c, x) for x in range(2) for y in range(2)]
        for z in range(planes)
        for c in range(2)
    ]
    column_groups = [
        [z * 4 + y * 2 + c for z in range(planes) for c in range(2)] for y in range(2)
    ]
    members = 2 * planes

    def moved(value, target):
        pairs = []
        for place in every(planes):
            to = target(*place)
            if to is not None:
                pairs.append((device(*place), device(*to)))
        return lax.ppermute(value, BOTH, pairs)

    def swap_y(value):
        return moved(value, lambda z, y, c, x: (z, 1 - y, c, x))

    def swap_x(value):
        return moved(value, lambda z, y, c, x: (z, y, c, 1 - x))

    def swap_both(value):
        return moved(value, lambda z, y, c, x: (z, 1 - y, c, 1 - x))

    def ordered(first, second, flag):
        return jnp.where(flag == 0, jnp.stack([first, second]), jnp.stack([second, first]))

    def plane_gather(value):
        by_y = ordered(value, swap_y(value), y)
        other = ordered(swap_x(value), swap_both(value), y)
        return ordered(by_y, other, x).reshape((4 * value.shape[0],) + value.shape[1:])

    def plane_sum(partial):
        sent = partial.astype(jnp.bfloat16).reshape(4, rows, width)
        got = lax.all_to_all(sent, BOTH, 0, 0, axis_index_groups=plane_groups, tiled=True)
        return jnp.sum(got.astype(jnp.float32), axis=0)

    def fetch(weight):
        halves = weight.reshape(share, 2, -1)
        mine = jnp.where(y == 0, halves[:, 0], halves[:, 1])
        theirs = jnp.where(y == 0, halves[:, 1], halves[:, 0])
        pair = ordered(mine, swap_y(theirs), y)
        got = lax.all_gather(pair, "seq", axis=0, tiled=False, axis_index_groups=column_groups)
        got = got.reshape(planes, 2, 2, share, -1)
        return jnp.swapaxes(got, 1, 2).reshape(width, -1)

    def give(grad):
        sent = grad.astype(jnp.bfloat16).reshape(planes, 2, 2, share, -1)
        sent = jnp.swapaxes(sent, 1, 2).reshape(members * 2, share, -1)
        got = lax.psum_scatter(
            sent, "seq", scatter_dimension=0, tiled=True, axis_index_groups=column_groups
        )
        mine = jnp.where(y == 0, got[0], got[1])
        theirs = jnp.where(y == 0, got[1], got[0])
        pair = ordered(mine, swap_y(theirs), y).astype(jnp.float32)
        return jnp.concatenate([pair[0], pair[1]], axis=1)

    gains = lax.all_gather(
        jnp.concatenate(
            [norm1_gain[:, None], norm2_gain[:, None], conv_kernel], axis=1
        ),
        "seq",
        axis=0,
        tiled=True,
    ).astype(jnp.float32)
    gain_one, gain_two, kernel = gains[:, 0], gains[:, 1], gains[:, 2:]
    taps = kernel.shape[1]
    margin = taps - 1
    channels = in_weight.shape[2] // 2
    first_channel = x * (2 * channels) + y * channels
    kernel_here = lax.dynamic_slice_in_dim(kernel, first_channel, channels, 0)

    w_in_halves = jnp.swapaxes(in_weight.reshape(share, 3, 2, channels), 1, 2)
    w_mixer = fetch(
        jnp.concatenate(
            [w_in_halves.reshape(share, 2, 3 * channels), out_weight.reshape(share, 2, channels)],
            axis=2,
        ).reshape(share, 8 * channels)
    )
    w_in, w_out = w_mixer[:, : 3 * channels], w_mixer[:, 3 * channels :]

    hidden = tokens[0].astype(jnp.float32)
    normed, scale_one = root_norm(hidden, gain_one)
    normed_low = plane_gather(normed.astype(jnp.bfloat16))
    grad_low = plane_gather(d_out[0])

    w_gate = fetch(gate_weight)
    w_up = fetch(up_weight)
    w_down = fetch(down_weight)

    projected = times(normed_low, w_in).reshape(2, 2, rows, 3 * channels)
    b_part = projected[..., :channels]
    c_part = projected[..., channels : 2 * channels]
    x_part = projected[..., 2 * channels :]
    gated = (b_part * x_part).astype(jnp.bfloat16)

    def swap_core(value):
        return moved(value, lambda z, y, c, x: (z, y, 1 - c, x))

    def to_next(value):
        return moved(
            value, lambda z, y, c, x: (z + 1, y, 0, x) if c == 1 and z + 1 < planes else None
        )

    def to_last(value):
        return moved(value, lambda z, y, c, x: (z - 1, y, 1, x) if c == 0 and z > 0 else None)

    tail = gated[:, :, rows - margin :]
    from_core, from_plane = swap_core(tail), to_next(tail[:, 1])
    before = jnp.where(
        c == 1, from_core, jnp.stack([from_plane, from_core[:, 0]], axis=1)
    )
    padded = jnp.concatenate([before, gated], axis=2).astype(jnp.float32)
    seq_len = lax.axis_size("seq") * rows // SEQS
    block = z * 4 + jnp.arange(2, dtype=jnp.int32) * 2 + c
    position = block[:, None] * rows + jnp.arange(rows, dtype=jnp.int32)
    in_sequence = position % seq_len
    masks = [
        (in_sequence >= margin - offset).astype(jnp.float32)[None, :, :, None]
        for offset in range(taps)
    ]
    conv = jnp.zeros_like(b_part)
    for offset in range(taps):
        conv = conv + masks[offset] * padded[:, :, offset : offset + rows] * kernel_here[:, offset]
    mixed = (c_part * conv).astype(jnp.bfloat16).reshape(4 * rows, channels)
    hidden_one = hidden + plane_sum(times_transposed(mixed, w_out))

    normed_two, scale_two = root_norm(hidden_one, gain_two)
    normed_two_low = plane_gather(normed_two.astype(jnp.bfloat16))
    gate = times(normed_two_low, w_gate)
    upper = times(normed_two_low, w_up)
    sigma = jax.nn.sigmoid(gate)
    active = (gate * sigma * upper).astype(jnp.bfloat16)
    d_active = times(grad_low, w_down)
    d_upper = (d_active * gate * sigma).astype(jnp.bfloat16)
    d_gate = (d_active * upper * sigma * (1.0 + gate * (1.0 - sigma))).astype(jnp.bfloat16)
    d_normed_two = plane_sum(times_transposed(d_gate, w_gate) + times_transposed(d_upper, w_up))
    result = hidden_one + plane_sum(times_transposed(active, w_down))
    d_gate_w = give(transposed_times(normed_two_low, d_gate))
    d_up_w = give(transposed_times(normed_two_low, d_upper))
    d_down_w = give(transposed_times(grad_low, active))

    d_hidden_two, d_gain_two = norm_back(d_normed_two, hidden_one, scale_two, gain_two)
    grad_one = d_out[0].astype(jnp.float32) + d_hidden_two
    grad_one_low = plane_gather(grad_one.astype(jnp.bfloat16))
    d_out_w = transposed_times(grad_one_low, mixed)
    d_mixed = times(grad_one_low, w_out).reshape(2, 2, rows, channels)
    d_c = d_mixed * conv
    d_conv = d_mixed * c_part
    kernel_cols = []
    d_padded = jnp.zeros((2, 2, rows + margin, channels), jnp.float32)
    for offset in range(taps):
        masked = masks[offset] * d_conv
        kernel_cols.append(jnp.sum(masked * padded[:, :, offset : offset + rows], axis=(0, 1, 2)))
        d_padded = d_padded + jnp.pad(
            masked * kernel_here[:, offset],
            ((0, 0), (0, 0), (offset, margin - offset), (0, 0)),
        )
    head = d_padded[:, :, :margin]
    from_core, from_plane = swap_core(head), to_last(head[:, 0])
    after = jnp.where(c == 0, from_core, jnp.stack([from_core[:, 1], from_plane], axis=1))
    d_gated = d_padded[:, :, margin:] + jnp.pad(
        after, ((0, 0), (0, 0), (rows - margin, 0), (0, 0))
    )
    d_projected = (
        jnp.concatenate([d_gated * x_part, d_c, d_gated * b_part], axis=3)
        .astype(jnp.bfloat16)
        .reshape(4 * rows, 3 * channels)
    )
    d_in_w = transposed_times(normed_low, d_projected)
    d_normed = plane_sum(times_transposed(d_projected, w_in))
    d_mixer = give(jnp.concatenate([d_in_w, d_out_w], axis=1)).reshape(share, 2, 4 * channels)
    d_in_w = jnp.swapaxes(d_mixer[:, :, : 3 * channels].reshape(share, 2, 3, channels), 1, 2)
    d_in_w = d_in_w.reshape(share, 3, 2 * channels)
    d_out_w = d_mixer[:, :, 3 * channels :].reshape(share, 2 * channels)
    d_hidden, d_gain_one = norm_back(d_normed, hidden, scale_one, gain_one)
    d_tokens = (grad_one + d_hidden).astype(jnp.bfloat16)

    d_kernel = lax.dynamic_update_slice(
        jnp.zeros((width, taps), jnp.float32), jnp.stack(kernel_cols, axis=1), (first_channel, 0)
    )
    small = jnp.concatenate([d_gain_one[:, None], d_gain_two[:, None], d_kernel], axis=1)
    small = lax.psum(small, BOTH)
    small = lax.dynamic_slice_in_dim(small, here * share, share, 0)
    return (
        result.astype(jnp.bfloat16)[None],
        d_tokens[None],
        small[:, 0],
        d_in_w,
        small[:, 2:],
        d_out_w,
        small[:, 1],
        d_gate_w,
        d_up_w,
        d_down_w,
    )


class Place:
    def __init__(self, planes):
        self.planes = planes
        self.me, self.x = lax.axis_index("seq"), lax.axis_index("fsdp")
        self.z = lax.div(self.me, 4)
        self.y = lax.rem(lax.div(self.me, 2), 2)
        self.c = lax.rem(self.me, 2)
        self.core = (self.me + 1 - 2 * self.c, self.x)
        self.across = (self.me + 2 - 4 * self.y, self.x)
        self.low, self.high = (self.me - 4, self.x), (self.me + 4, self.x)
        self.has_low, self.has_high = self.z > 0, self.z < planes - 1
        self.block = self.x * 2 + self.y
        self.beside = (self.me, 1 - self.x)
        self.beside_block = (1 - self.x) * 2 + self.y
        self.across_block = self.x * 2 + 1 - self.y
        self.far_block = (1 - self.x) * 2 + 1 - self.y
        self.is_first, self.is_last = self.c == 0, self.c == 1
        self.gives_next = jnp.logical_and(self.is_last, self.has_high)
        self.gives_last = jnp.logical_and(self.is_first, self.has_low)
        self.next, self.last = (self.me + 3, self.x), (self.me - 3, self.x)


def remote(source, target, send, receive, device_id):
    return pltpu.make_async_remote_copy(
        src_ref=source,
        dst_ref=target,
        send_sem=send,
        recv_sem=receive,
        device_id=device_id,
        device_id_type=MESH,
    )


def signal(semaphore, device_id):
    pl.semaphore_signal(semaphore, inc=1, device_id=device_id, device_id_type=MESH)


def dot(left, right):
    return jnp.dot(left, right, preferred_element_type=jnp.float32)


def kernel(
    planes,
    parts,
    seq_len,
    weights,
    tokens,
    d_out,
    gains_here,
    result,
    d_tokens,
    own_grad,
    other_grad,
    small,
    kept_weights,
    kept_mixer,
    w,
    core_in,
    extra,
    n_one,
    f_all,
    n_two,
    e_all,
    sent_a,
    sent_b,
    total_a,
    total_b,
    got_a,
    gated,
    d_conv,
    mixed,
    active,
    d_gate_up,
    hidden_one,
    d_hidden,
    halo,
    gains_in,
    gains,
    taps,
    small_in,
    gain_send,
    gain_recv,
    small_send,
    small_recv,
    local_sem,
    y_send,
    y_recv,
    z_send,
    z_recv,
    c_send,
    c_recv,
    core_send,
    core_recv,
    core_free,
    sum_send,
    sum_recv,
    ready,
    last_send,
    last_recv,
    own_sem,
    all_send,
    all_recv,
    part_send,
    part_recv,
    halo_send,
    halo_recv,
    keep_sem,
):
    at = Place(planes)
    z, y, c = at.z, at.y, at.c
    rows, width = tokens.shape
    channels = taps.shape[1]
    count = 4 * planes
    share = weights.shape[2]
    wide = 4 * share
    chunks = parts + 2
    step_cols = weights.shape[3] // 3

    def y_copies(k):
        return (
            pltpu.make_async_copy(weights.at[k, y], w.at[k, z, y, c], local_sem.at[k]),
            remote(weights.at[k, 1 - y], w.at[k, z, y, c], y_send.at[k], y_recv.at[k], at.across),
        )

    def piece(k, p):
        return w.at[k, p, :, c]

    def to_side(k, p, side):
        return remote(
            piece(k, p),
            piece(k, p),
            z_send.at[k, side, p],
            z_recv.at[k, p],
            at.high if side else at.low,
        )

    def to_core(k, p):
        return remote(piece(k, p), piece(k, p), c_send.at[k, p], c_recv.at[k, p], at.core)

    def begin(k):
        for copy in y_copies(k):
            copy.start()

    def own(k):
        y_copies(k)[0].wait()
        remote(
            weights.at[k, y], w.at[k, z, 1 - y, c], y_send.at[k], y_recv.at[k], at.across
        ).wait_recv()
        pl.when(at.has_low)(lambda: to_side(k, z, 0).start())
        pl.when(at.has_high)(lambda: to_side(k, z, 1).start())
        to_core(k, z).start()

    def relay(k, t):
        below, above = z - t, z + t

        @pl.when(below >= 0)
        def _():
            to_side(k, below, 1).wait_recv()
            pl.when(at.has_high)(lambda: to_side(k, below, 1).start())
            to_core(k, below).start()

        @pl.when(above < planes)
        def _():
            to_side(k, above, 0).wait_recv()
            pl.when(at.has_low)(lambda: to_side(k, above, 0).start())
            to_core(k, above).start()

    between = jnp.logical_and(at.has_low, at.has_high)

    def pass_on(k, t):
        pl.when(between)(lambda: relay(k, t))

    def take_last(k):
        @pl.when(jnp.logical_not(between))
        def _():
            for t in range(1, planes):
                relay(k, t)

    def core_wait(k):
        for p in range(planes):
            remote(
                w.at[k, p, :, 1 - c], w.at[k, p, :, 1 - c], c_send.at[k, p], c_recv.at[k, p], at.core
            ).wait_recv()

    def gather_done(k):
        y_copies(k)[1].wait_send()
        for p in range(planes):
            pl.when(jnp.logical_and(at.has_low, p >= z))(lambda: to_side(k, p, 0).wait_send())
            pl.when(jnp.logical_and(at.has_high, p <= z))(lambda: to_side(k, p, 1).wait_send())
            to_core(k, p).wait_send()

    def chunk_of(v):
        return lax.rem(v + 2, chunks)

    def core_copy(v):
        k = chunk_of(v)
        return remote(
            w.at[k, :, :, 1 - c],
            core_in.at[lax.rem(v, 2)],
            core_send.at[k],
            core_recv.at[k],
            at.core,
        )

    def core_start(v):
        pl.when(v >= 2)(lambda: pl.semaphore_wait(core_free, 1))
        core_copy(v).start()

    def core_add(v):
        k, slot = chunk_of(v), lax.rem(v, 2)
        core_copy(v).wait()

        def add(p, carry):
            total = w[k, p, :, c].astype(jnp.float32) + core_in[slot, p].astype(jnp.float32)
            w[k, p, :, c] = total.astype(jnp.bfloat16)
            return carry

        lax.fori_loop(0, planes, add, 0)
        pl.when(v < chunks - 2)(lambda: signal(core_free, at.core))
        pl.when(at.has_low)(lambda: signal(ready.at[1], at.low))
        pl.when(at.has_high)(lambda: signal(ready.at[0], at.high))

    def landing(k, d):
        return w.at[k, d, :, 1 - c]

    def sum_up(k, d):
        return remote(
            landing(k, d), landing(k, d), sum_send.at[k, 1, d], sum_recv.at[k, 1, d], at.high
        )

    def sum_down(k, d):
        return remote(
            landing(k, d), landing(k, d), sum_send.at[k, 0, d], sum_recv.at[k, 0, d], at.low
        )

    def sum_down_last(k, d):
        return remote(
            landing(k, d), extra.at[k], sum_send.at[k, 0, d], sum_recv.at[k, 0, d], at.low
        )

    def add_here(k, d, arrived):
        here = w[k, d, :, c].astype(jnp.float32)

        @pl.when(arrived)
        def _():
            w[k, d, :, 1 - c] = (w[k, d, :, 1 - c].astype(jnp.float32) + here).astype(jnp.bfloat16)

        @pl.when(jnp.logical_not(arrived))
        def _():
            w[k, d, :, 1 - c] = w[k, d, :, c]

    def add_up(v):
        k = chunk_of(v)
        pl.when(at.has_high)(lambda: pl.semaphore_wait(ready.at[1], 1))
        for d in range(planes - 1, -1, -1):

            @pl.when(d > z)
            def _():
                pl.when(at.has_low)(lambda: sum_up(k, d).wait_recv())
                add_here(k, d, at.has_low)
                sum_up(k, d).start()

            @pl.when(jnp.logical_and(z == d, at.has_low))
            def _():
                sum_up(k, d).wait_recv()
                total = w[k, d, :, c].astype(jnp.float32) + w[k, d, :, 1 - c].astype(jnp.float32)
                w[k, d, :, c] = total.astype(jnp.bfloat16)

    def add_down(v):
        k = chunk_of(v)
        pl.when(at.has_low)(lambda: pl.semaphore_wait(ready.at[0], 1))
        for d in range(planes):

            @pl.when(d < z)
            def _():
                pl.when(at.has_high)(lambda: sum_down(k, d).wait_recv())
                add_here(k, d, at.has_high)
                pl.when(z - 1 > d)(lambda: sum_down(k, d).start())
                pl.when(z - 1 == d)(lambda: sum_down_last(k, d).start())

            @pl.when(jnp.logical_and(z == d, at.has_high))
            def _():
                sum_down_last(k, d).wait_recv()
                total = w[k, d, :, c].astype(jnp.float32) + extra[k].astype(jnp.float32)
                w[k, d, :, c] = total.astype(jnp.bfloat16)

    def give_copies(k):
        return (
            pltpu.make_async_copy(w.at[k, z, y, c], own_grad.at[k], own_sem.at[k]),
            remote(
                w.at[k, z, 1 - y, c], other_grad.at[k], last_send.at[k], last_recv.at[k], at.across
            ),
        )

    def give(v):
        for copy in give_copies(chunk_of(v)):
            copy.start()

    def sum_done(v):
        k = chunk_of(v)
        for d in range(planes):
            pl.when(d > z)(lambda: sum_up(k, d).wait_send())
            pl.when(d < z)(lambda: sum_down(k, d).wait_send())
        for copy in give_copies(k):
            copy.wait()

    def first_hop(v):
        core_add(v)
        pl.when(jnp.logical_not(at.has_low))(lambda: add_up(v))
        pl.when(jnp.logical_not(at.has_high))(lambda: add_down(v))

    def tick(j):
        def stage(o, extra_flag, do):
            there = jnp.logical_and(o >= 0, o < chunks)
            pl.when(jnp.logical_and(there, extra_flag))(lambda: do(o))

        far = jnp.maximum(z, planes - 1 - z)
        stage(j - z, at.has_low, add_up)
        stage(j - (planes - 1 - z), at.has_high, add_down)
        stage(j - far, far >= 0, give)

    part_rows = rows // 2

    def half_of(buffer, block, which_half):
        return buffer.at[block, pl.ds(which_half * part_rows, part_rows), :]

    def all_copy(buffer, which, i):
        block, which_half, to = (
            (at.block, 0, at.beside),
            (at.block, 1, at.across),
            (at.block, 1, at.beside),
            (at.block, 0, at.across),
            (at.beside_block, 0, at.across),
            (at.across_block, 1, at.beside),
        )[i]
        ref = half_of(buffer, block, which_half)
        return remote(ref, ref, all_send.at[which, i], all_recv.at[which, i], to)

    def all_landed(buffer, which, i):
        block, which_half = (
            (at.beside_block, 0),
            (at.across_block, 1),
            (at.beside_block, 1),
            (at.across_block, 0),
            (at.far_block, 0),
            (at.far_block, 1),
        )[i]
        ref = half_of(buffer, block, which_half)
        remote(
            ref, ref, all_send.at[which, i], all_recv.at[which, i], at.across
        ).wait_recv()

    def all_start(buffer, which):
        for i in range(4):
            all_copy(buffer, which, i).start()

    def all_pass(buffer, which):
        for i in range(2):
            all_landed(buffer, which, i)
            all_copy(buffer, which, 4 + i).start()

    def all_wait(buffer, which):
        for i in range(2, 6):
            all_landed(buffer, which, i)

    def all_done(buffer, which):
        for i in range(6):
            all_copy(buffer, which, i).wait_send()

    def part_copy(source, target, which, i):
        block, which_half, slot, to = (
            (at.far_block, 0, 2, at.beside),
            (at.far_block, 1, 2, at.across),
            (at.beside_block, 0, 0, at.beside),
            (at.across_block, 1, 1, at.across),
            (at.across_block, 0, 1, at.across),
            (at.beside_block, 1, 0, at.beside),
        )[i]
        return remote(
            half_of(source, block, which_half),
            half_of(target, slot, which_half),
            part_send.at[which, i],
            part_recv.at[which, i],
            to,
        )

    def part_start(source, target, which):
        for i in range(4):
            part_copy(source, target, which, i).start()

    def part_pass(source, target, which):
        for i, block in enumerate((at.across_block, at.beside_block)):
            part_copy(source, target, which, i).wait_recv()
            here = pl.ds(i * part_rows, part_rows)
            total = source[block, here, :].astype(jnp.float32)
            total = total + target[2, here, :].astype(jnp.float32)
            source[block, here, :] = total.astype(jnp.bfloat16)
            part_copy(source, target, which, 4 + i).start()

    def part_wait(source, target, which):
        for i in range(2, 6):
            part_copy(source, target, which, i).wait_recv()

    def part_done(source, target, which):
        for i in range(6):
            part_copy(source, target, which, i).wait_send()

    tile = 48

    def by_rows(body):
        def run(i, carry):
            body(pl.ds(pl.multiple_of(i * tile, tile), tile))
            return carry

        lax.fori_loop(0, rows // tile, run, 0)

    def scale_of(hidden):
        return lax.rsqrt(jnp.mean(hidden * hidden, axis=-1, keepdims=True) + EPSILON)

    def summed(source, target, span):
        total = source[at.block, span, :].astype(jnp.float32)
        for i in range(2):
            total = total + target[i, span, :].astype(jnp.float32)
        return total

    def back_through_norm(grad, hidden, gain, row):
        scale = scale_of(hidden)
        weighted = grad * gain
        inner = jnp.sum(weighted * hidden, axis=-1, keepdims=True)
        small[row : row + 1, :] += jnp.sum(grad * hidden * scale, axis=0, keepdims=True)
        return scale * weighted - hidden * (scale * scale * scale) * inner / width

    def transposed(buffer, k):
        def one(p, carry):
            cols = pl.ds(pl.multiple_of(p * wide, wide), wide)
            block = buffer[:, :, cols].reshape(4 * rows, wide).T
            w[k, p] = block.reshape(2, 2, share, 4 * rows)
            return carry

        lax.fori_loop(0, planes, one, 0)

    def whole(k, low, high):
        return w[k, :, :, :, :, low:high].reshape(planes * wide, high - low)

    def two_planes(k, q, low, high):
        return w[k, pair(q), :, :, :, low:high].reshape(2 * wide, high - low)

    def pair(t):
        return pl.ds(2 * t, 2)

    def two_columns(q):
        return pl.ds(pl.multiple_of(q * 2 * wide, 2 * wide), 2 * wide)

    def weight_grad(turned, grads, k, span):
        out = dot(w[turned].reshape(planes * wide, 4 * rows), grads).astype(jnp.bfloat16)
        w[k, :, :, :, :, span] = out.reshape(planes, 2, 2, share, grads.shape[1])

    halo[...] = jnp.zeros_like(halo)
    barrier = pltpu.get_barrier_semaphore()
    signal(barrier, at.beside)

    def greet(t, carry):
        signal(barrier, (lax.rem(at.me + t, count), at.x))
        return carry

    lax.fori_loop(1, count, greet, 0)
    pl.semaphore_wait(barrier, count)

    def gain_copy(t):
        other = lax.rem(at.me + t, count)
        return remote(
            gains_here,
            gains_in.at[at.me],
            gain_send.at[t],
            gain_recv.at[t],
            (other, at.x),
        )

    def gain_start(t, carry):
        gain_copy(t).start()
        return carry

    def gain_wait(t, carry):
        gain_copy(t).wait()
        return carry

    lax.fori_loop(1, count, gain_start, 0)
    begin(0)
    begin(1)
    e_copy = pltpu.make_async_copy(d_out, e_all.at[at.block], keep_sem.at[0])
    e_copy.start()
    small[...] = jnp.zeros_like(small)
    gains_in[at.me] = gains_here[...]
    lax.fori_loop(1, count, gain_wait, 0)
    for d in range(count):
        found = gains_in[d].astype(jnp.float32)[0:8, :share]
        gains[:, d * share : (d + 1) * share] = found
    channel_columns = pl.ds(pl.multiple_of(at.block * channels, channels), channels)
    taps[...] = gains[:, channel_columns]

    def first_norm(span):
        hidden = tokens[span, :].astype(jnp.float32)
        n_one[at.block, span, :] = (hidden * scale_of(hidden) * gains[0:1, :]).astype(jnp.bfloat16)

    by_rows(first_norm)
    all_start(n_one, 0)
    begin(2)
    own(0)
    own(1)
    relay(0, 1)
    all_pass(n_one, 0)
    e_copy.wait()
    all_start(e_all, 1)
    begin(3)
    relay(1, 1)
    relay(0, 2)
    relay(1, 2)
    own(2)
    all_pass(e_all, 1)
    begin(4)
    for t in range(3, planes):
        relay(0, t)
    core_wait(0)
    all_wait(n_one, 0)

    def project_c(t, carry):
        normed = n_one[pair(t)].reshape(2 * rows, width)
        c_part = dot(normed, whole(0, 0, channels))
        total_a[pair(t), :, channels : 2 * channels] = c_part.reshape(2, rows, channels)
        return carry

    def project_b_x(t, carry):
        normed = n_one[pair(t)].reshape(2 * rows, width)
        b_x = dot(normed, whole(1, 0, 2 * channels)).reshape(2, rows, 2 * channels)
        total_a[pair(t), :, 0:channels] = b_x[:, :, :channels]
        total_a[pair(t), :, 2 * channels : 3 * channels] = b_x[:, :, channels:]
        product = (b_x[:, :, :channels] * b_x[:, :, channels:]).astype(jnp.bfloat16)
        gated[pair(t), 8 : 8 + rows, :] = product.astype(jnp.float32)
        return carry

    lax.fori_loop(0, 2, project_c, 0)
    for t in range(3, planes):
        relay(1, t)
    own(3)
    core_wait(1)
    lax.fori_loop(0, 2, project_b_x, 0)

    def halo_core(which, edge):
        return remote(
            edge, halo.at[2 * which], halo_send.at[2 * which], halo_recv.at[2 * which], at.core
        )

    def halo_plane(which, edge, target):
        return remote(
            edge,
            halo.at[2 * which + 1],
            halo_send.at[2 * which + 1],
            halo_recv.at[2 * which + 1],
            target,
        )

    tail = gated.at[:, pl.ds(rows, 8), :]
    halo_core(0, tail).start()
    pl.when(at.gives_next)(lambda: halo_plane(0, tail, at.next).start())
    halo_core(0, tail).wait_recv()
    pl.when(at.gives_last)(lambda: halo_plane(0, tail, at.last).wait_recv())
    for group in range(2):

        @pl.when(at.is_last)
        def _():
            gated[2 * group, 0:8, :] = halo[0, 2 * group]
            gated[2 * group + 1, 0:8, :] = halo[0, 2 * group + 1]

        @pl.when(at.is_first)
        def _():
            gated[2 * group, 0:8, :] = halo[1, 2 * group + 1]
            gated[2 * group + 1, 0:8, :] = halo[0, 2 * group]

    def start_of(block):
        return lax.rem((z * 4 + lax.rem(block, 2) * 2 + c) * rows, seq_len)

    def place_in(block, ahead):
        place = start_of(block) + ahead + lax.broadcasted_iota(jnp.int32, (rows, channels), 0)
        return jnp.where(place >= seq_len, place - seq_len, place)

    def convolve(b, carry):
        place = place_in(b, 0)
        conv = jnp.zeros((rows, channels), jnp.float32)
        for j in range(3):
            moved = gated[b, 6 + j : 6 + j + rows, :]
            conv = conv + jnp.where(place >= 2 - j, moved, 0.0) * taps[2 + j : 3 + j, :]
        total_a[b, :, 3 * channels : 4 * channels] = conv
        mixed[b] = (total_a[b, :, channels : 2 * channels] * conv).astype(jnp.bfloat16)
        return carry

    lax.fori_loop(0, 4, convolve, 0)

    def branch(i, carry):
        t, q = lax.div(i, planes // 2), lax.rem(i, planes // 2)
        left = mixed[pair(t)].reshape(2 * rows, channels)
        out = times_transposed(left, two_planes(0, q, channels, 2 * channels))
        out = out.reshape(2, rows, 2 * wide).astype(jnp.bfloat16)
        sent_a[pair(t), :, two_columns(q)] = out
        return carry

    lax.fori_loop(0, planes, branch, 0)
    part_start(sent_a, got_a, 0)
    gather_done(0)
    gather_done(1)
    keep_weights = pltpu.make_async_copy(w.at[pl.ds(0, 2)], kept_weights, keep_sem.at[1])
    keep_mixer = pltpu.make_async_copy(total_a, kept_mixer, keep_sem.at[2])
    keep_weights.start()
    keep_mixer.start()
    pass_on(2, 1)
    part_pass(sent_a, got_a, 0)
    own(4)
    begin(5)
    for t in range(2, planes):
        pass_on(2, t)
    keep_weights.wait()
    keep_mixer.wait()
    total_a[...] = jnp.zeros_like(total_a)
    total_b[...] = jnp.zeros_like(total_b)
    all_wait(e_all, 1)
    transposed(e_all, 1)
    part_wait(sent_a, got_a, 0)

    def second_norm(span):
        hidden = tokens[span, :].astype(jnp.float32) + summed(sent_a, got_a, span)
        hidden_one[span, :] = hidden
        n_two[at.block, span, :] = (hidden * scale_of(hidden) * gains[1:2, :]).astype(jnp.bfloat16)

    by_rows(second_norm)
    all_start(n_two, 2)
    part_done(sent_a, got_a, 0)
    pass_on(3, 1)
    own(5)
    all_pass(n_two, 2)
    begin(6)
    begin(7)
    begin(8)
    for t in range(2, planes):
        pass_on(3, t)
    own(6)
    pass_on(4, 1)
    all_wait(n_two, 2)
    transposed(n_two, 0)
    own(7)
    take_last(2)

    def cast(source, target):
        def run(b, carry):
            target[b] = source[b].astype(jnp.bfloat16)
            return carry

        lax.fori_loop(0, 4, run, 0)

    def feed_forward(k):
        def half(t, carry):
            normed = n_two[pair(t)].reshape(2 * rows, width)
            both = dot(normed, whole(k, 0, 2 * step_cols))
            d_active = dot(
                e_all[pair(t)].reshape(2 * rows, width), whole(k, 2 * step_cols, 3 * step_cols)
            )
            gate, upper = both[:, :step_cols], both[:, step_cols:]
            sigma = jax.nn.sigmoid(gate)
            soft = gate * sigma
            here = pl.ds(pl.multiple_of(t * 2 * rows, 2 * rows), 2 * rows)
            active[here, :] = (soft * upper).astype(jnp.bfloat16)
            d_gate_up[here, step_cols:] = (d_active * soft).astype(jnp.bfloat16)
            d_gate_up[here, :step_cols] = (
                d_active * upper * sigma * (1.0 + gate * (1.0 - sigma))
            ).astype(jnp.bfloat16)

            def spread(q, inner):
                back = times_transposed(d_gate_up[here, :], two_planes(k, q, 0, 2 * step_cols))
                total_b[pair(t), :, two_columns(q)] += back.reshape(2, rows, 2 * wide)
                out = times_transposed(
                    active[here, :], two_planes(k, q, 2 * step_cols, 3 * step_cols)
                )
                total_a[pair(t), :, two_columns(q)] += out.reshape(2, rows, 2 * wide)
                return inner

            lax.fori_loop(0, planes // 2, spread, 0)
            early = jnp.logical_and(between, jnp.logical_and(t == 0, k > 2))
            pl.when(early)(lambda: first_hop(k - 3))
            pl.when(jnp.logical_and(t == 0, k + 3 < chunks))(lambda: pass_on(k + 3, 1))
            pl.when(jnp.logical_and(t == 1, k + 2 < chunks))(lambda: pass_on(k + 2, 2))
            return carry

        lax.fori_loop(0, 2, half, 0)

        @pl.when(k == chunks - 1)
        def _():
            cast(total_b, sent_a)
            part_start(sent_a, got_a, 2)

        gather_done(k)

        def grads(n, carry):
            span = pl.ds(pl.multiple_of(n * step_cols, step_cols), step_cols)
            weight_grad(0, d_gate_up[:, span], k, span)
            return carry

        lax.fori_loop(0, 2, grads, 0)
        weight_grad(1, active[...], k, pl.ds(2 * step_cols, step_cols))

    def one_part(i, carry):
        k = i + 2
        pl.when(i == 1)(lambda: own(8))
        core_wait(k)
        feed_forward(k)
        core_start(i)
        pl.when(jnp.logical_not(between))(lambda: first_hop(i))
        pl.when(jnp.logical_and(i >= 3, i < parts - 1))(lambda: tick(i - 2))

        @pl.when(k + 1 < chunks)
        def _():
            take_last(k + 1)
            for t in range(3, planes):
                pass_on(k + 1, t)

        return carry

    lax.fori_loop(0, parts, one_part, 0)

    restore_weights = pltpu.make_async_copy(kept_weights, w.at[pl.ds(0, 2)], keep_sem.at[1])
    restore_weights.start()

    cast(total_a, sent_b)
    restore_mixer = pltpu.make_async_copy(kept_mixer, total_a, keep_sem.at[2])
    restore_mixer.start()
    pl.when(between)(lambda: first_hop(jnp.int32(parts - 1)))
    part_pass(sent_a, got_a, 2)
    tick(4)
    part_wait(sent_a, got_a, 2)

    def through_second(span):
        grad = back_through_norm(
            summed(sent_a, got_a, span), hidden_one[span, :], gains[1:2, :], 1
        )
        grad = e_all[at.block, span, :].astype(jnp.float32) + grad
        d_hidden[span, :] = grad
        f_all[at.block, span, :] = grad.astype(jnp.bfloat16)

    by_rows(through_second)
    all_done(n_two, 2)
    all_start(f_all, 3)
    part_done(sent_a, got_a, 2)
    all_pass(f_all, 3)
    part_start(sent_b, n_two, 1)
    sum_done(0)
    transposed(n_one, 2)
    all_done(n_one, 0)
    restore_weights.wait()
    restore_mixer.wait()
    tick(5)
    tick(6)
    all_wait(f_all, 3)

    def into_mixer(t, carry):
        grad = f_all[pair(t)].reshape(2 * rows, width)
        d_mixed = dot(grad, whole(0, channels, 2 * channels)).reshape(2, rows, channels)
        conv = total_a[pair(t), :, 3 * channels : 4 * channels]
        c_part = total_a[pair(t), :, channels : 2 * channels]
        n_one[pair(t), :, 2 * channels : 3 * channels] = (d_mixed * conv).astype(jnp.bfloat16)
        d_conv[pair(t), 0:rows, :] = d_mixed * c_part
        return carry

    lax.fori_loop(0, 2, into_mixer, 0)
    head = d_conv.at[:, pl.ds(0, 8), :]
    halo_core(1, head).start()
    pl.when(at.gives_last)(lambda: halo_plane(1, head, at.last).start())

    def from_c(i, carry):
        t, q = lax.div(i, planes // 2), lax.rem(i, planes // 2)
        grad = n_one[pair(t), :, 2 * channels : 3 * channels].reshape(2 * rows, channels)
        out = times_transposed(grad, two_planes(0, q, 0, channels))
        total_b[pair(t), :, two_columns(q)] = out.reshape(2, rows, 2 * wide)
        return carry

    lax.fori_loop(0, planes, from_c, 0)
    sum_done(1)
    transposed(f_all, 3)

    d_c = n_one[:, :, 2 * channels : 3 * channels].reshape(4 * rows, channels)
    weight_grad(2, d_c, 0, pl.ds(0, channels))
    weight_grad(3, mixed[...].reshape(4 * rows, channels), 0, pl.ds(channels, channels))
    core_start(jnp.int32(parts))
    halo_core(1, head).wait_recv()
    pl.when(at.gives_next)(lambda: halo_plane(1, head, at.next).wait_recv())
    for group in range(2):

        @pl.when(at.is_first)
        def _():
            d_conv[2 * group, rows : rows + 8, :] = halo[2, 2 * group]
            d_conv[2 * group + 1, rows : rows + 8, :] = halo[2, 2 * group + 1]

        @pl.when(at.is_last)
        def _():
            d_conv[2 * group, rows : rows + 8, :] = halo[2, 2 * group + 1]
            d_conv[2 * group + 1, rows : rows + 8, :] = halo[3, 2 * group]

    def convolve_back(b, carry):
        place = place_in(b, 0)
        d_gated = jnp.zeros((rows, channels), jnp.float32)
        for j in range(3):
            ahead = 2 - j
            moved = jnp.where(
                place_in(b, ahead) >= ahead, d_conv[b, ahead : ahead + rows, :], 0.0
            )
            d_gated = d_gated + moved * taps[2 + j : 3 + j, :]
            product = d_conv[b, 0:rows, :] * gated[b, 6 + j : 6 + j + rows, :]
            small[2 + j : 3 + j, channel_columns] += jnp.sum(
                jnp.where(place >= ahead, product, 0.0), axis=0, keepdims=True
            )
        x_part = total_a[b, :, 2 * channels : 3 * channels]
        n_one[b, :, 0:channels] = (d_gated * x_part).astype(jnp.bfloat16)
        b_part = total_a[b, :, 0:channels]
        n_one[b, :, channels : 2 * channels] = (d_gated * b_part).astype(jnp.bfloat16)
        return carry

    lax.fori_loop(0, 4, convolve_back, 0)
    first_hop(jnp.int32(parts))

    def d_normed(i, carry):
        t, q = lax.div(i, planes // 2), lax.rem(i, planes // 2)
        grad = n_one[pair(t), :, 0 : 2 * channels].reshape(2 * rows, 2 * channels)
        out = times_transposed(grad, two_planes(1, q, 0, 2 * channels))
        out = total_b[pair(t), :, two_columns(q)] + out.reshape(2, rows, 2 * wide)
        sent_a[pair(t), :, two_columns(q)] = out.astype(jnp.bfloat16)
        return carry

    lax.fori_loop(0, planes, d_normed, 0)
    part_start(sent_a, got_a, 3)

    def b_and_x_weight(n, carry):
        span = pl.ds(pl.multiple_of(n * channels, channels), channels)
        grad = n_one[:, :, span].reshape(4 * rows, channels)
        weight_grad(2, grad, 1, span)
        return carry

    lax.fori_loop(0, 2, b_and_x_weight, 0)
    core_start(jnp.int32(parts + 1))
    tick(7)
    part_pass(sent_a, got_a, 3)
    first_hop(jnp.int32(parts + 1))
    part_pass(sent_b, n_two, 1)
    tick(8)
    part_wait(sent_a, got_a, 3)

    def through_first(span):
        hidden = tokens[span, :].astype(jnp.float32)
        grad = back_through_norm(summed(sent_a, got_a, span), hidden, gains[0:1, :], 0)
        d_tokens[span, :] = (d_hidden[span, :] + grad).astype(jnp.bfloat16)

    by_rows(through_first)

    def small_copy(i, to):
        return remote(small, small_in.at[i], small_send.at[i], small_recv.at[i], to)

    def small_plane(t):
        to = lax.rem(at.me + 4 * t, count)
        return remote(
            small, small_in.at[2 + t], small_send.at[2 + t], small_recv.at[2 + t], (to, at.x)
        )

    small_copy(0, at.core).start()
    tick(9)
    for i, (here, following) in enumerate(
        ((at.core, at.beside), (at.beside, at.across), (at.across, None))
    ):
        small_copy(i, here).wait()
        small[...] += small_in[i]
        if following is not None:
            small_copy(i + 1, following).start()
    for t in range(1, planes):
        small_plane(t).start()
    tick(10)
    for t in range(1, planes):
        small_plane(t).wait()
    for t in range(1, planes):
        small[...] += small_in[2 + t]
    part_wait(sent_b, n_two, 1)

    def last_out(span):
        result[span, :] = (hidden_one[span, :] + summed(sent_b, n_two, span)).astype(jnp.bfloat16)

    by_rows(last_out)
    for j in range(11, chunks + planes - 1):
        tick(j)

    part_done(sent_a, got_a, 3)
    all_done(e_all, 1)
    part_done(sent_b, n_two, 1)
    all_done(f_all, 3)
    halo_core(0, tail).wait_send()
    halo_core(1, head).wait_send()
    pl.when(at.gives_next)(lambda: halo_plane(0, tail, at.next).wait_send())
    pl.when(at.gives_last)(lambda: halo_plane(1, head, at.last).wait_send())
    for v in range(2, chunks):
        sum_done(v)


def one_kernel(planes, seq_len, weights, tokens, d_out, gains):
    chunks, _, share, cols = weights.shape
    parts = chunks - 2
    rows, width = tokens.shape
    channels = width // 4
    low, full = jnp.bfloat16, jnp.float32
    shape = jax.ShapeDtypeStruct
    vmem, anywhere = pl.BlockSpec(memory_space=pltpu.VMEM), pl.BlockSpec(memory_space=pl.ANY)
    dma = pltpu.SemaphoreType.DMA
    block = (4, rows, width)
    return pl.pallas_call(
        functools.partial(kernel, planes, parts, seq_len),
        out_shape=(
            shape((rows, width), low),
            shape((rows, width), low),
            shape((chunks, share, cols), low),
            shape((chunks, share, cols), low),
            shape((8, width), full),
            shape((2, planes, 2, 2, share, cols), low),
            shape(block, full),
        ),
        in_specs=[anywhere, vmem, anywhere, vmem],
        out_specs=[vmem, vmem, anywhere, anywhere, vmem, anywhere, anywhere],
        scratch_shapes=[
            pltpu.VMEM((chunks, planes, 2, 2, share, cols), low),
            pltpu.VMEM((2, planes, 2, share, cols), low),
            pltpu.VMEM((chunks, 2, share, cols), low),
            pltpu.VMEM(block, low),
            pltpu.VMEM(block, low),
            pltpu.VMEM(block, low),
            pltpu.VMEM(block, low),
            pltpu.VMEM(block, low),
            pltpu.VMEM(block, low),
            pltpu.VMEM(block, full),
            pltpu.VMEM(block, full),
            pltpu.VMEM((3, rows, width), low),
            pltpu.VMEM((4, rows + 8, channels), full),
            pltpu.VMEM((4, rows + 8, channels), full),
            pltpu.VMEM((4, rows, channels), low),
            pltpu.VMEM((4 * rows, PART), low),
            pltpu.VMEM((4 * rows, 2 * PART), low),
            pltpu.VMEM((rows, width), full),
            pltpu.VMEM((rows, width), full),
            pltpu.VMEM((4, 4, 8, channels), full),
            pltpu.VMEM((4 * planes,) + gains.shape, low),
            pltpu.VMEM((8, width), full),
            pltpu.VMEM((8, channels), full),
            pltpu.VMEM((2 + planes, 8, width), full),
            dma((4 * planes,)),
            dma((4 * planes,)),
            dma((2 + planes,)),
            dma((2 + planes,)),
            dma((chunks,)),
            dma((chunks,)),
            dma((chunks,)),
            dma((chunks, 2, planes)),
            dma((chunks, planes)),
            dma((chunks, planes)),
            dma((chunks, planes)),
            dma((chunks,)),
            dma((chunks,)),
            pltpu.SemaphoreType.REGULAR,
            dma((chunks, 2, planes)),
            dma((chunks, 2, planes)),
            pltpu.SemaphoreType.REGULAR((2,)),
            dma((chunks,)),
            dma((chunks,)),
            dma((chunks,)),
            dma((4, 6)),
            dma((4, 6)),
            dma((4, 6)),
            dma((4, 6)),
            dma((4,)),
            dma((4,)),
            dma((3,)),
        ],
        compiler_params=pltpu.CompilerParams(
            collective_id=0, has_side_effects=True, vmem_limit_bytes=64 * 1024 * 1024
        ),
    )(weights, tokens, d_out, gains)


def split_kernel(hidden, parts, gate, up, down, in_weight, out_weight, weights):
    channels = out_weight.shape[1] // 2
    left = parts * PART - hidden
    blank = jnp.zeros((gate.shape[0], left), jnp.bfloat16)
    for which, source in enumerate((gate, up, down)):
        here = pl.ds(which * PART, PART)
        for half in range(2):
            for part in range(parts):
                low = half * hidden + part * PART
                if part < parts - 1 or left == 0:
                    weights[2 + part, half, :, here] = source[:, low : low + PART]
                else:
                    last = source[:, low : low + PART - left]
                    weights[2 + part, half, :, here] = jnp.concatenate([last, blank], axis=1)
    for half in range(2):
        span = slice(half * channels, (half + 1) * channels)
        weights[0, half, :, 0:channels] = in_weight[1, :, span]
        weights[0, half, :, channels:] = out_weight[:, span]
        weights[1, half, :, 0:channels] = in_weight[0, :, span]
        weights[1, half, :, channels:] = in_weight[2, :, span]


def split(gate, up, down, in_weight, out_weight, step=32):
    share, columns = gate.shape
    hidden = columns // 2
    parts = -(-hidden // PART)
    by_rows = pl.BlockSpec((step, columns), lambda i: (i, 0))
    cols = 3 * PART
    return pl.pallas_call(
        functools.partial(split_kernel, hidden, parts),
        grid=(share // step,),
        out_shape=jax.ShapeDtypeStruct((parts + 2, 2, share, cols), jnp.bfloat16),
        in_specs=[
            by_rows,
            by_rows,
            by_rows,
            pl.BlockSpec((3, step, in_weight.shape[2]), lambda i: (0, i, 0)),
            pl.BlockSpec((step, out_weight.shape[1]), lambda i: (i, 0)),
        ],
        out_specs=pl.BlockSpec((parts + 2, 2, step, cols), lambda i: (0, 0, i, 0)),
    )(gate, up, down, in_weight, out_weight)


def join_kernel(hidden, parts, own, other, gate, up, down, in_weight, out_weight):
    channels = out_weight.shape[1] // 2
    side = lax.rem(lax.div(lax.axis_index("seq"), 2), 2)

    def put(half, source):
        for which, target in enumerate((gate, up, down)):
            pieces = [
                source[2 + part, :, which * PART : (which + 1) * PART].astype(jnp.float32)
                for part in range(parts)
            ]
            whole = jnp.concatenate(pieces, axis=1)[:, :hidden]
            target[:, half * hidden : (half + 1) * hidden] = whole
        span = slice(half * channels, (half + 1) * channels)
        in_weight[1, :, span] = source[0, :, 0:channels].astype(jnp.float32)
        out_weight[:, span] = source[0, :, channels:].astype(jnp.float32)
        in_weight[0, :, span] = source[1, :, 0:channels].astype(jnp.float32)
        in_weight[2, :, span] = source[1, :, channels:].astype(jnp.float32)

    @pl.when(side == 0)
    def _():
        put(0, own)
        put(1, other)

    @pl.when(side == 1)
    def _():
        put(0, other)
        put(1, own)


def join(own, other, hidden, channels, step=32):
    chunks, share, cols = own.shape
    parts = chunks - 2
    full = jnp.float32
    part = pl.BlockSpec((chunks, step, cols), lambda i: (0, i, 0))
    by_rows = pl.BlockSpec((step, 2 * hidden), lambda i: (i, 0))
    shape = jax.ShapeDtypeStruct
    return pl.pallas_call(
        functools.partial(join_kernel, hidden, parts),
        grid=(share // step,),
        out_shape=(
            shape((share, 2 * hidden), full),
            shape((share, 2 * hidden), full),
            shape((share, 2 * hidden), full),
            shape((3, share, 2 * channels), full),
            shape((share, 2 * channels), full),
        ),
        in_specs=[part, part],
        out_specs=(
            by_rows,
            by_rows,
            by_rows,
            pl.BlockSpec((3, step, 2 * channels), lambda i: (0, i, 0)),
            pl.BlockSpec((step, 2 * channels), lambda i: (i, 0)),
        ),
    )(own, other)


def on_device(
    tokens,
    norm1_gain,
    in_weight,
    conv_kernel,
    out_weight,
    norm2_gain,
    gate_weight,
    up_weight,
    down_weight,
    d_out,
):
    planes = lax.axis_size("seq") // 4
    here = lax.axis_index("seq")
    rows, width = tokens.shape[1:]
    share = gate_weight.shape[0]
    channels = in_weight.shape[2] // 2
    hidden = gate_weight.shape[1] // 2

    gains = jnp.concatenate([norm1_gain[None], norm2_gain[None], conv_kernel.T], axis=0)
    gains = jnp.pad(gains, ((0, 16 - gains.shape[0]), (0, 128 - share)))

    weights = split(
        gate_weight, up_weight, down_weight, jnp.swapaxes(in_weight, 0, 1), out_weight
    )
    result, d_tokens, own_grad, other_grad, small, _, _ = one_kernel(
        planes,
        lax.axis_size("seq") * rows // SEQS,
        weights,
        tokens[0],
        d_out[0],
        gains,
    )
    d_gate, d_up, d_down, d_in, d_branch = join(own_grad, other_grad, hidden, channels)
    sums = lax.dynamic_slice_in_dim(small, here * share, share, 1)
    return (
        result[None],
        d_tokens[None],
        sums[0],
        jnp.swapaxes(d_in, 0, 1),
        sums[2:5].T,
        d_branch,
        sums[1],
        d_gate,
        d_up,
        d_down,
    )


def fits(mesh):
    return mesh.shape["seq"] <= 16


def solution(mesh):
    return jax.shard_map(
        on_device if fits(mesh) else plain_on_device,
        mesh=mesh,
        in_specs=(
            P("fsdp", "seq", None),
            P("seq"),
            P("seq", None, "fsdp"),
            P("seq", None),
            P("seq", "fsdp"),
            P("seq"),
            P("seq", "fsdp"),
            P("seq", "fsdp"),
            P("seq", "fsdp"),
            P("fsdp", "seq", None),
        ),
        out_specs=(
            P("fsdp", "seq", None),
            P("fsdp", "seq", None),
            P("seq"),
            P("seq", None, "fsdp"),
            P("seq", None),
            P("seq", "fsdp"),
            P("seq"),
            P("seq", "fsdp"),
            P("seq", "fsdp"),
            P("seq", "fsdp"),
        ),
        check_vma=False,
    )
```

```python
import functools

import jax
import jax.numpy as jnp
from jax import lax
from jax.experimental import pallas as pl
from jax.experimental.pallas import tpu as pltpu
from jax.sharding import PartitionSpec as P

SEQS = 3
EPSILON = 1e-05
BOTH = ("seq", "fsdp")
MESH = pl.DeviceIdType.MESH
PART = 256


def times_transposed(left, right):
    return lax.dot_general(
        left, right, (((1,), (1,)), ((), ())), preferred_element_type=jnp.float32
    )


def transposed_times(left, right):
    return lax.dot_general(
        left, right, (((0,), (0,)), ((), ())), preferred_element_type=jnp.float32
    )


def times(left, right):
    return jnp.dot(left, right, preferred_element_type=jnp.float32)


def root_norm(hidden, gain):
    scale = lax.rsqrt(jnp.mean(hidden * hidden, axis=-1, keepdims=True) + EPSILON)
    return (hidden * scale * gain, scale)


def norm_back(grad, hidden, scale, gain):
    weighted = grad * gain
    inner = jnp.sum(weighted * hidden, axis=-1, keepdims=True)
    d_hidden = scale * weighted - hidden * (scale * scale * scale) * inner / hidden.shape[-1]
    d_gain = jnp.sum(grad * hidden * scale, axis=0)
    return (d_hidden, d_gain)


def device(z, y, c, x):
    return (z * 4 + y * 2 + c) * 2 + x


def every(planes):
    return [
        (z, y, c, x) for z in range(planes) for y in range(2) for c in range(2) for x in range(2)
    ]


def plain_on_device(
    tokens,
    norm1_gain,
    in_weight,
    conv_kernel,
    out_weight,
    norm2_gain,
    gate_weight,
    up_weight,
    down_weight,
    d_out,
):
    planes = lax.axis_size("seq") // 4
    here = lax.axis_index("seq")
    y, c, x = (here // 2) % 2, here % 2, lax.axis_index("fsdp")
    z = here // 4
    rows, width = tokens.shape[1:]
    share = gate_weight.shape[0]
    plane_groups = [
        [device(z, y, c, x) for x in range(2) for y in range(2)]
        for z in range(planes)
        for c in range(2)
    ]
    column_groups = [
        [z * 4 + y * 2 + c for z in range(planes) for c in range(2)] for y in range(2)
    ]
    members = 2 * planes

    def moved(value, target):
        pairs = []
        for place in every(planes):
            to = target(*place)
            if to is not None:
                pairs.append((device(*place), device(*to)))
        return lax.ppermute(value, BOTH, pairs)

    def swap_y(value):
        return moved(value, lambda z, y, c, x: (z, 1 - y, c, x))

    def swap_x(value):
        return moved(value, lambda z, y, c, x: (z, y, c, 1 - x))

    def swap_both(value):
        return moved(value, lambda z, y, c, x: (z, 1 - y, c, 1 - x))

    def ordered(first, second, flag):
        return jnp.where(flag == 0, jnp.stack([first, second]), jnp.stack([second, first]))

    def plane_gather(value):
        by_y = ordered(value, swap_y(value), y)
        other = ordered(swap_x(value), swap_both(value), y)
        return ordered(by_y, other, x).reshape((4 * value.shape[0],) + value.shape[1:])

    def plane_sum(partial):
        sent = partial.astype(jnp.bfloat16).reshape(4, rows, width)
        got = lax.all_to_all(sent, BOTH, 0, 0, axis_index_groups=plane_groups, tiled=True)
        return jnp.sum(got.astype(jnp.float32), axis=0)

    def fetch(weight):
        halves = weight.reshape(share, 2, -1)
        mine = jnp.where(y == 0, halves[:, 0], halves[:, 1])
        theirs = jnp.where(y == 0, halves[:, 1], halves[:, 0])
        pair = ordered(mine, swap_y(theirs), y)
        got = lax.all_gather(pair, "seq", axis=0, tiled=False, axis_index_groups=column_groups)
        got = got.reshape(planes, 2, 2, share, -1)
        return jnp.swapaxes(got, 1, 2).reshape(width, -1)

    def give(grad):
        sent = grad.astype(jnp.bfloat16).reshape(planes, 2, 2, share, -1)
        sent = jnp.swapaxes(sent, 1, 2).reshape(members * 2, share, -1)
        got = lax.psum_scatter(
            sent, "seq", scatter_dimension=0, tiled=True, axis_index_groups=column_groups
        )
        mine = jnp.where(y == 0, got[0], got[1])
        theirs = jnp.where(y == 0, got[1], got[0])
        pair = ordered(mine, swap_y(theirs), y).astype(jnp.float32)
        return jnp.concatenate([pair[0], pair[1]], axis=1)

    gains = lax.all_gather(
        jnp.concatenate(
            [norm1_gain[:, None], norm2_gain[:, None], conv_kernel], axis=1
        ),
        "seq",
        axis=0,
        tiled=True,
    ).astype(jnp.float32)
    gain_one, gain_two, kernel = gains[:, 0], gains[:, 1], gains[:, 2:]
    taps = kernel.shape[1]
    margin = taps - 1
    channels = in_weight.shape[2] // 2
    first_channel = x * (2 * channels) + y * channels
    kernel_here = lax.dynamic_slice_in_dim(kernel, first_channel, channels, 0)

    w_in_halves = jnp.swapaxes(in_weight.reshape(share, 3, 2, channels), 1, 2)
    w_mixer = fetch(
        jnp.concatenate(
            [w_in_halves.reshape(share, 2, 3 * channels), out_weight.reshape(share, 2, channels)],
            axis=2,
        ).reshape(share, 8 * channels)
    )
    w_in, w_out = w_mixer[:, : 3 * channels], w_mixer[:, 3 * channels :]

    hidden = tokens[0].astype(jnp.float32)
    normed, scale_one = root_norm(hidden, gain_one)
    normed_low = plane_gather(normed.astype(jnp.bfloat16))
    grad_low = plane_gather(d_out[0])

    w_gate = fetch(gate_weight)
    w_up = fetch(up_weight)
    w_down = fetch(down_weight)

    projected = times(normed_low, w_in).reshape(2, 2, rows, 3 * channels)
    b_part = projected[..., :channels]
    c_part = projected[..., channels : 2 * channels]
    x_part = projected[..., 2 * channels :]
    gated = (b_part * x_part).astype(jnp.bfloat16)

    def swap_core(value):
        return moved(value, lambda z, y, c, x: (z, y, 1 - c, x))

    def to_next(value):
        return moved(
            value, lambda z, y, c, x: (z + 1, y, 0, x) if c == 1 and z + 1 < planes else None
        )

    def to_last(value):
        return moved(value, lambda z, y, c, x: (z - 1, y, 1, x) if c == 0 and z > 0 else None)

    tail = gated[:, :, rows - margin :]
    from_core, from_plane = swap_core(tail), to_next(tail[:, 1])
    before = jnp.where(
        c == 1, from_core, jnp.stack([from_plane, from_core[:, 0]], axis=1)
    )
    padded = jnp.concatenate([before, gated], axis=2).astype(jnp.float32)
    seq_len = lax.axis_size("seq") * rows // SEQS
    block = z * 4 + jnp.arange(2, dtype=jnp.int32) * 2 + c
    position = block[:, None] * rows + jnp.arange(rows, dtype=jnp.int32)
    in_sequence = position % seq_len
    masks = [
        (in_sequence >= margin - offset).astype(jnp.float32)[None, :, :, None]
        for offset in range(taps)
    ]
    conv = jnp.zeros_like(b_part)
    for offset in range(taps):
        conv = conv + masks[offset] * padded[:, :, offset : offset + rows] * kernel_here[:, offset]
    mixed = (c_part * conv).astype(jnp.bfloat16).reshape(4 * rows, channels)
    hidden_one = hidden + plane_sum(times_transposed(mixed, w_out))

    normed_two, scale_two = root_norm(hidden_one, gain_two)
    normed_two_low = plane_gather(normed_two.astype(jnp.bfloat16))
    gate = times(normed_two_low, w_gate)
    upper = times(normed_two_low, w_up)
    sigma = jax.nn.sigmoid(gate)
    active = (gate * sigma * upper).astype(jnp.bfloat16)
    d_active = times(grad_low, w_down)
    d_upper = (d_active * gate * sigma).astype(jnp.bfloat16)
    d_gate = (d_active * upper * sigma * (1.0 + gate * (1.0 - sigma))).astype(jnp.bfloat16)
    d_normed_two = plane_sum(times_transposed(d_gate, w_gate) + times_transposed(d_upper, w_up))
    result = hidden_one + plane_sum(times_transposed(active, w_down))
    d_gate_w = give(transposed_times(normed_two_low, d_gate))
    d_up_w = give(transposed_times(normed_two_low, d_upper))
    d_down_w = give(transposed_times(grad_low, active))

    d_hidden_two, d_gain_two = norm_back(d_normed_two, hidden_one, scale_two, gain_two)
    grad_one = d_out[0].astype(jnp.float32) + d_hidden_two
    grad_one_low = plane_gather(grad_one.astype(jnp.bfloat16))
    d_out_w = transposed_times(grad_one_low, mixed)
    d_mixed = times(grad_one_low, w_out).reshape(2, 2, rows, channels)
    d_c = d_mixed * conv
    d_conv = d_mixed * c_part
    kernel_cols = []
    d_padded = jnp.zeros((2, 2, rows + margin, channels), jnp.float32)
    for offset in range(taps):
        masked = masks[offset] * d_conv
        kernel_cols.append(jnp.sum(masked * padded[:, :, offset : offset + rows], axis=(0, 1, 2)))
        d_padded = d_padded + jnp.pad(
            masked * kernel_here[:, offset],
            ((0, 0), (0, 0), (offset, margin - offset), (0, 0)),
        )
    head = d_padded[:, :, :margin]
    from_core, from_plane = swap_core(head), to_last(head[:, 0])
    after = jnp.where(c == 0, from_core, jnp.stack([from_core[:, 1], from_plane], axis=1))
    d_gated = d_padded[:, :, margin:] + jnp.pad(
        after, ((0, 0), (0, 0), (rows - margin, 0), (0, 0))
    )
    d_projected = (
        jnp.concatenate([d_gated * x_part, d_c, d_gated * b_part], axis=3)
        .astype(jnp.bfloat16)
        .reshape(4 * rows, 3 * channels)
    )
    d_in_w = transposed_times(normed_low, d_projected)
    d_normed = plane_sum(times_transposed(d_projected, w_in))
    d_mixer = give(jnp.concatenate([d_in_w, d_out_w], axis=1)).reshape(share, 2, 4 * channels)
    d_in_w = jnp.swapaxes(d_mixer[:, :, : 3 * channels].reshape(share, 2, 3, channels), 1, 2)
    d_in_w = d_in_w.reshape(share, 3, 2 * channels)
    d_out_w = d_mixer[:, :, 3 * channels :].reshape(share, 2 * channels)
    d_hidden, d_gain_one = norm_back(d_normed, hidden, scale_one, gain_one)
    d_tokens = (grad_one + d_hidden).astype(jnp.bfloat16)

    d_kernel = lax.dynamic_update_slice(
        jnp.zeros((width, taps), jnp.float32), jnp.stack(kernel_cols, axis=1), (first_channel, 0)
    )
    small = jnp.concatenate([d_gain_one[:, None], d_gain_two[:, None], d_kernel], axis=1)
    small = lax.psum(small, BOTH)
    small = lax.dynamic_slice_in_dim(small, here * share, share, 0)
    return (
        result.astype(jnp.bfloat16)[None],
        d_tokens[None],
        small[:, 0],
        d_in_w,
        small[:, 2:],
        d_out_w,
        small[:, 1],
        d_gate_w,
        d_up_w,
        d_down_w,
    )


class Place:
    def __init__(self, planes):
        self.planes = planes
        self.me, self.x = lax.axis_index("seq"), lax.axis_index("fsdp")
        self.z = lax.div(self.me, 4)
        self.y = lax.rem(lax.div(self.me, 2), 2)
        self.c = lax.rem(self.me, 2)
        self.core = (self.me + 1 - 2 * self.c, self.x)
        self.across = (self.me + 2 - 4 * self.y, self.x)
        self.low, self.high = (self.me - 4, self.x), (self.me + 4, self.x)
        self.has_low, self.has_high = self.z > 0, self.z < planes - 1
        self.block = self.x * 2 + self.y
        self.beside = (self.me, 1 - self.x)
        self.beside_block = (1 - self.x) * 2 + self.y
        self.across_block = self.x * 2 + 1 - self.y
        self.far_block = (1 - self.x) * 2 + 1 - self.y
        self.is_first, self.is_last = self.c == 0, self.c == 1
        self.gives_next = jnp.logical_and(self.is_last, self.has_high)
        self.gives_last = jnp.logical_and(self.is_first, self.has_low)
        self.next, self.last = (self.me + 3, self.x), (self.me - 3, self.x)


def remote(source, target, send, receive, device_id):
    return pltpu.make_async_remote_copy(
        src_ref=source,
        dst_ref=target,
        send_sem=send,
        recv_sem=receive,
        device_id=device_id,
        device_id_type=MESH,
    )


def signal(semaphore, device_id):
    pl.semaphore_signal(semaphore, inc=1, device_id=device_id, device_id_type=MESH)


def dot(left, right):
    return jnp.dot(left, right, preferred_element_type=jnp.float32)


def kernel(
    planes,
    parts,
    seq_len,
    weights,
    tokens,
    d_out,
    gains_here,
    result,
    d_tokens,
    own_grad,
    other_grad,
    small,
    kept_weights,
    kept_mixer,
    w,
    core_in,
    extra,
    n_one,
    f_all,
    n_two,
    e_all,
    sent_a,
    sent_b,
    total_a,
    total_b,
    got_a,
    gated,
    d_conv,
    mixed,
    active,
    d_gate_up,
    hidden_one,
    d_hidden,
    halo,
    gains_in,
    gains,
    taps,
    small_in,
    gain_send,
    gain_recv,
    small_send,
    small_recv,
    local_sem,
    y_send,
    y_recv,
    z_send,
    z_recv,
    c_send,
    c_recv,
    core_send,
    core_recv,
    core_free,
    sum_send,
    sum_recv,
    ready,
    last_send,
    last_recv,
    own_sem,
    all_send,
    all_recv,
    part_send,
    part_recv,
    halo_send,
    halo_recv,
    keep_sem,
):
    at = Place(planes)
    z, y, c = at.z, at.y, at.c
    rows, width = tokens.shape
    channels = taps.shape[1]
    count = 4 * planes
    share = weights.shape[2]
    wide = 4 * share
    chunks = parts + 2
    step_cols = weights.shape[3] // 3

    def y_copies(k):
        return (
            pltpu.make_async_copy(weights.at[k, y], w.at[k, z, y, c], local_sem.at[k]),
            remote(weights.at[k, 1 - y], w.at[k, z, y, c], y_send.at[k], y_recv.at[k], at.across),
        )

    def piece(k, p):
        return w.at[k, p, :, c]

    def to_side(k, p, side):
        return remote(
            piece(k, p),
            piece(k, p),
            z_send.at[k, side, p],
            z_recv.at[k, p],
            at.high if side else at.low,
        )

    def to_core(k, p):
        return remote(piece(k, p), piece(k, p), c_send.at[k, p], c_recv.at[k, p], at.core)

    def begin(k):
        for copy in y_copies(k):
            copy.start()

    def own(k):
        y_copies(k)[0].wait()
        remote(
            weights.at[k, y], w.at[k, z, 1 - y, c], y_send.at[k], y_recv.at[k], at.across
        ).wait_recv()
        pl.when(at.has_low)(lambda: to_side(k, z, 0).start())
        pl.when(at.has_high)(lambda: to_side(k, z, 1).start())
        to_core(k, z).start()

    def relay(k, t):
        below, above = z - t, z + t

        @pl.when(below >= 0)
        def _():
            to_side(k, below, 1).wait_recv()
            pl.when(at.has_high)(lambda: to_side(k, below, 1).start())
            to_core(k, below).start()

        @pl.when(above < planes)
        def _():
            to_side(k, above, 0).wait_recv()
            pl.when(at.has_low)(lambda: to_side(k, above, 0).start())
            to_core(k, above).start()

    between = jnp.logical_and(at.has_low, at.has_high)

    def pass_on(k, t):
        pl.when(between)(lambda: relay(k, t))

    def own_between(k):
        pl.when(between)(lambda: own(k))

    def own_at_end(k):
        pl.when(jnp.logical_not(between))(lambda: own(k))

    def take_last(k):
        @pl.when(jnp.logical_not(between))
        def _():
            for t in range(1, planes):
                relay(k, t)

    def core_wait(k):
        for p in range(planes):
            remote(
                w.at[k, p, :, 1 - c], w.at[k, p, :, 1 - c], c_send.at[k, p], c_recv.at[k, p], at.core
            ).wait_recv()

    def gather_done(k):
        y_copies(k)[1].wait_send()
        for p in range(planes):
            pl.when(jnp.logical_and(at.has_low, p >= z))(lambda: to_side(k, p, 0).wait_send())
            pl.when(jnp.logical_and(at.has_high, p <= z))(lambda: to_side(k, p, 1).wait_send())
            to_core(k, p).wait_send()

    def chunk_of(v):
        return lax.rem(v + 2, chunks)

    def core_copy(v):
        k = chunk_of(v)
        return remote(
            w.at[k, :, :, 1 - c],
            core_in.at[lax.rem(v, 2)],
            core_send.at[k],
            core_recv.at[k],
            at.core,
        )

    def core_start(v):
        pl.when(v >= 2)(lambda: pl.semaphore_wait(core_free, 1))
        core_copy(v).start()

    def core_add(v):
        k, slot = chunk_of(v), lax.rem(v, 2)
        core_copy(v).wait()

        def add(p, carry):
            total = w[k, p, :, c].astype(jnp.float32) + core_in[slot, p].astype(jnp.float32)
            w[k, p, :, c] = total.astype(jnp.bfloat16)
            return carry

        lax.fori_loop(0, planes, add, 0)
        pl.when(v < chunks - 2)(lambda: signal(core_free, at.core))
        pl.when(at.has_low)(lambda: signal(ready.at[1], at.low))
        pl.when(at.has_high)(lambda: signal(ready.at[0], at.high))

    def landing(k, d):
        return w.at[k, d, :, 1 - c]

    def sum_up(k, d):
        return remote(
            landing(k, d), landing(k, d), sum_send.at[k, 1, d], sum_recv.at[k, 1, d], at.high
        )

    def sum_down(k, d):
        return remote(
            landing(k, d), landing(k, d), sum_send.at[k, 0, d], sum_recv.at[k, 0, d], at.low
        )

    def sum_down_last(k, d):
        return remote(
            landing(k, d), extra.at[k], sum_send.at[k, 0, d], sum_recv.at[k, 0, d], at.low
        )

    def add_here(k, d, arrived):
        here = w[k, d, :, c].astype(jnp.float32)

        @pl.when(arrived)
        def _():
            w[k, d, :, 1 - c] = (w[k, d, :, 1 - c].astype(jnp.float32) + here).astype(jnp.bfloat16)

        @pl.when(jnp.logical_not(arrived))
        def _():
            w[k, d, :, 1 - c] = w[k, d, :, c]

    def add_up(v):
        k = chunk_of(v)
        pl.when(at.has_high)(lambda: pl.semaphore_wait(ready.at[1], 1))
        for d in range(planes - 1, -1, -1):

            @pl.when(d > z)
            def _():
                pl.when(at.has_low)(lambda: sum_up(k, d).wait_recv())
                add_here(k, d, at.has_low)
                sum_up(k, d).start()

            @pl.when(jnp.logical_and(z == d, at.has_low))
            def _():
                sum_up(k, d).wait_recv()
                total = w[k, d, :, c].astype(jnp.float32) + w[k, d, :, 1 - c].astype(jnp.float32)
                w[k, d, :, c] = total.astype(jnp.bfloat16)

    def add_down(v):
        k = chunk_of(v)
        pl.when(at.has_low)(lambda: pl.semaphore_wait(ready.at[0], 1))
        for d in range(planes):

            @pl.when(d < z)
            def _():
                pl.when(at.has_high)(lambda: sum_down(k, d).wait_recv())
                add_here(k, d, at.has_high)
                pl.when(z - 1 > d)(lambda: sum_down(k, d).start())
                pl.when(z - 1 == d)(lambda: sum_down_last(k, d).start())

            @pl.when(jnp.logical_and(z == d, at.has_high))
            def _():
                sum_down_last(k, d).wait_recv()
                total = w[k, d, :, c].astype(jnp.float32) + extra[k].astype(jnp.float32)
                w[k, d, :, c] = total.astype(jnp.bfloat16)

    def give_copies(k):
        return (
            pltpu.make_async_copy(w.at[k, z, y, c], own_grad.at[k], own_sem.at[k]),
            remote(
                w.at[k, z, 1 - y, c], other_grad.at[k], last_send.at[k], last_recv.at[k], at.across
            ),
        )

    def give(v):
        for copy in give_copies(chunk_of(v)):
            copy.start()

    def sum_done(v):
        k = chunk_of(v)
        for d in range(planes):
            pl.when(d > z)(lambda: sum_up(k, d).wait_send())
            pl.when(d < z)(lambda: sum_down(k, d).wait_send())
        for copy in give_copies(k):
            copy.wait()

    def first_hop(v):
        core_add(v)
        pl.when(jnp.logical_not(at.has_low))(lambda: add_up(v))
        pl.when(jnp.logical_not(at.has_high))(lambda: add_down(v))

    def tick(j):
        def stage(o, extra_flag, do):
            there = jnp.logical_and(o >= 0, o < chunks)
            pl.when(jnp.logical_and(there, extra_flag))(lambda: do(o))

        far = jnp.maximum(z, planes - 1 - z)
        stage(j - z, at.has_low, add_up)
        stage(j - (planes - 1 - z), at.has_high, add_down)
        stage(j - far, far >= 0, give)

    part_rows = rows // 2

    def half_of(buffer, block, which_half):
        return buffer.at[block, pl.ds(which_half * part_rows, part_rows), :]

    def all_copy(buffer, which, i):
        block, which_half, to = (
            (at.block, 0, at.across if which < 2 else at.beside),
            (at.block, 1, at.across),
            (at.block, 1, at.beside),
            (at.block, 0, at.beside if which < 2 else at.across),
            (at.across_block, 0, at.beside)
            if which < 2
            else (at.beside_block, 0, at.across),
            (at.across_block, 1, at.beside),
        )[i]
        ref = half_of(buffer, block, which_half)
        return remote(ref, ref, all_send.at[which, i], all_recv.at[which, i], to)

    def all_landed(buffer, which, i):
        block, which_half = (
            (at.across_block if which < 2 else at.beside_block, 0),
            (at.across_block, 1),
            (at.beside_block, 1),
            (at.beside_block if which < 2 else at.across_block, 0),
            (at.far_block, 0),
            (at.far_block, 1),
        )[i]
        ref = half_of(buffer, block, which_half)
        remote(
            ref, ref, all_send.at[which, i], all_recv.at[which, i], at.across
        ).wait_recv()

    def all_start(buffer, which):
        for i in range(4):
            all_copy(buffer, which, i).start()

    def all_pass(buffer, which):
        for i in range(2):
            all_landed(buffer, which, i)
            all_copy(buffer, which, 4 + i).start()

    def all_wait(buffer, which):
        for i in range(2, 6):
            all_landed(buffer, which, i)

    def near_wait(buffer, which):
        all_landed(buffer, which, 3)

    def far_wait(buffer, which):
        for i in (2, 4, 5):
            all_landed(buffer, which, i)

    def all_done(buffer, which):
        for i in range(6):
            all_copy(buffer, which, i).wait_send()

    def part_copy(source, target, which, i):
        block, which_half, slot, to = (
            (at.far_block, 0, 2, at.beside),
            (at.far_block, 1, 2, at.across),
            (at.beside_block, 0, 0, at.beside),
            (at.across_block, 1, 1, at.across),
            (at.across_block, 0, 1, at.across),
            (at.beside_block, 1, 0, at.beside),
        )[i]
        return remote(
            half_of(source, block, which_half),
            half_of(target, slot, which_half),
            part_send.at[which, i],
            part_recv.at[which, i],
            to,
        )

    def part_start(source, target, which):
        for i in range(4):
            part_copy(source, target, which, i).start()

    def part_pass(source, target, which):
        for i, block in enumerate((at.across_block, at.beside_block)):
            part_copy(source, target, which, i).wait_recv()
            here = pl.ds(i * part_rows, part_rows)
            total = source[block, here, :].astype(jnp.float32)
            total = total + target[2, here, :].astype(jnp.float32)
            source[block, here, :] = total.astype(jnp.bfloat16)
            part_copy(source, target, which, 4 + i).start()

    def part_wait(source, target, which):
        for i in range(2, 6):
            part_copy(source, target, which, i).wait_recv()

    def part_done(source, target, which):
        for i in range(6):
            part_copy(source, target, which, i).wait_send()

    tile = 48

    def by_rows(body):
        def run(i, carry):
            body(pl.ds(pl.multiple_of(i * tile, tile), tile))
            return carry

        lax.fori_loop(0, rows // tile, run, 0)

    def scale_of(hidden):
        return lax.rsqrt(jnp.mean(hidden * hidden, axis=-1, keepdims=True) + EPSILON)

    def summed(source, target, span):
        total = source[at.block, span, :].astype(jnp.float32)
        for i in range(2):
            total = total + target[i, span, :].astype(jnp.float32)
        return total

    def back_through_norm(grad, hidden, gain, row):
        scale = scale_of(hidden)
        weighted = grad * gain
        inner = jnp.sum(weighted * hidden, axis=-1, keepdims=True)
        small[row : row + 1, :] += jnp.sum(grad * hidden * scale, axis=0, keepdims=True)
        return scale * weighted - hidden * (scale * scale * scale) * inner / width

    def transposed(buffer, k):
        def one(p, carry):
            cols = pl.ds(pl.multiple_of(p * wide, wide), wide)
            block = buffer[:, :, cols].reshape(4 * rows, wide).T
            w[k, p] = block.reshape(2, 2, share, 4 * rows)
            return carry

        lax.fori_loop(0, planes, one, 0)

    def whole(k, low, high):
        return w[k, :, :, :, :, low:high].reshape(planes * wide, high - low)

    def two_planes(k, q, low, high):
        return w[k, pair(q), :, :, :, low:high].reshape(2 * wide, high - low)

    def pair(t):
        return pl.ds(2 * t, 2)

    def two_columns(q):
        return pl.ds(pl.multiple_of(q * 2 * wide, 2 * wide), 2 * wide)

    def weight_grad(turned, grads, k, span):
        def some(q, carry):
            here = pair(q)
            out = dot(w[turned, here].reshape(2 * wide, 4 * rows), grads).astype(jnp.bfloat16)
            w[k, here, :, :, :, span] = out.reshape(2, 2, 2, share, grads.shape[1])
            return carry

        if grads.shape[1] <= PART:
            out = dot(w[turned].reshape(planes * wide, 4 * rows), grads).astype(jnp.bfloat16)
            w[k, :, :, :, :, span] = out.reshape(planes, 2, 2, share, grads.shape[1])
        else:
            lax.fori_loop(0, planes // 2, some, 0)

    halo[...] = jnp.zeros_like(halo)
    barrier = pltpu.get_barrier_semaphore()
    signal(barrier, at.beside)

    def greet(t, carry):
        signal(barrier, (lax.rem(at.me + t, count), at.x))
        return carry

    lax.fori_loop(1, count, greet, 0)
    pl.semaphore_wait(barrier, count)

    def gain_copy(t):
        other = lax.rem(at.me + t, count)
        return remote(
            gains_here,
            gains_in.at[at.me],
            gain_send.at[t],
            gain_recv.at[t],
            (other, at.x),
        )

    def gain_start(t, carry):
        gain_copy(t).start()
        return carry

    def gain_wait(t, carry):
        gain_copy(t).wait()
        return carry

    lax.fori_loop(1, count, gain_start, 0)
    begin(0)
    begin(1)
    e_copy = pltpu.make_async_copy(d_out, e_all.at[at.block], keep_sem.at[0])
    e_copy.start()
    small[...] = jnp.zeros_like(small)
    gains_in[at.me] = gains_here[...]
    lax.fori_loop(1, count, gain_wait, 0)
    for d in range(count):
        found = gains_in[d].astype(jnp.float32)[0:8, :share]
        gains[:, d * share : (d + 1) * share] = found
    channel_columns = pl.ds(pl.multiple_of(at.block * channels, channels), channels)
    taps[...] = gains[:, channel_columns]

    def first_norm(span):
        hidden = tokens[span, :].astype(jnp.float32)
        n_one[at.block, span, :] = (hidden * scale_of(hidden) * gains[0:1, :]).astype(jnp.bfloat16)

    by_rows(first_norm)
    all_start(n_one, 0)
    own(0)
    own(1)
    begin(2)
    relay(0, 1)
    all_pass(n_one, 0)
    e_copy.wait()
    all_start(e_all, 1)
    begin(3)
    relay(1, 1)
    relay(0, 2)
    relay(1, 2)
    own(2)
    all_pass(e_all, 1)
    for k in range(4, chunks - 2):
        begin(k)
    for t in range(3, planes):
        relay(0, t)
    core_wait(0)
    all_wait(n_one, 0)

    def project_c(t, carry):
        normed = n_one[pair(t)].reshape(2 * rows, width)
        c_part = dot(normed, whole(0, 0, channels))
        total_a[pair(t), :, channels : 2 * channels] = c_part.reshape(2, rows, channels)
        return carry

    def project_b_x(t, carry):
        normed = n_one[pair(t)].reshape(2 * rows, width)
        b_x = dot(normed, whole(1, 0, 2 * channels)).reshape(2, rows, 2 * channels)
        total_a[pair(t), :, 0:channels] = b_x[:, :, :channels]
        total_a[pair(t), :, 2 * channels : 3 * channels] = b_x[:, :, channels:]
        product = (b_x[:, :, :channels] * b_x[:, :, channels:]).astype(jnp.bfloat16)
        gated[pair(t), 8 : 8 + rows, :] = product.astype(jnp.float32)
        return carry

    lax.fori_loop(0, 2, project_c, 0)
    for t in range(3, planes):
        relay(1, t)
    own(3)
    core_wait(1)
    lax.fori_loop(0, 2, project_b_x, 0)

    def halo_core(which, edge):
        return remote(
            edge, halo.at[2 * which], halo_send.at[2 * which], halo_recv.at[2 * which], at.core
        )

    def halo_plane(which, edge, target):
        return remote(
            edge,
            halo.at[2 * which + 1],
            halo_send.at[2 * which + 1],
            halo_recv.at[2 * which + 1],
            target,
        )

    tail = gated.at[:, pl.ds(rows, 8), :]
    halo_core(0, tail).start()
    pl.when(at.gives_next)(lambda: halo_plane(0, tail, at.next).start())
    halo_core(0, tail).wait_recv()
    pl.when(at.gives_last)(lambda: halo_plane(0, tail, at.last).wait_recv())
    for group in range(2):

        @pl.when(at.is_last)
        def _():
            gated[2 * group, 0:8, :] = halo[0, 2 * group]
            gated[2 * group + 1, 0:8, :] = halo[0, 2 * group + 1]

        @pl.when(at.is_first)
        def _():
            gated[2 * group, 0:8, :] = halo[1, 2 * group + 1]
            gated[2 * group + 1, 0:8, :] = halo[0, 2 * group]

    def start_of(block):
        return lax.rem((z * 4 + lax.rem(block, 2) * 2 + c) * rows, seq_len)

    def place_in(block, ahead):
        place = start_of(block) + ahead + lax.broadcasted_iota(jnp.int32, (rows, channels), 0)
        return jnp.where(place >= seq_len, place - seq_len, place)

    def convolve(b, carry):
        place = place_in(b, 0)
        conv = jnp.zeros((rows, channels), jnp.float32)
        for j in range(3):
            moved = gated[b, 6 + j : 6 + j + rows, :]
            conv = conv + jnp.where(place >= 2 - j, moved, 0.0) * taps[2 + j : 3 + j, :]
        total_a[b, :, 3 * channels : 4 * channels] = conv
        mixed[b] = (total_a[b, :, channels : 2 * channels] * conv).astype(jnp.bfloat16)
        return carry

    lax.fori_loop(0, 4, convolve, 0)

    def branch(i, carry):
        t, q = lax.div(i, planes // 2), lax.rem(i, planes // 2)
        left = mixed[pair(t)].reshape(2 * rows, channels)
        out = times_transposed(left, two_planes(0, q, channels, 2 * channels))
        out = out.reshape(2, rows, 2 * wide).astype(jnp.bfloat16)
        sent_a[pair(t), :, two_columns(q)] = out
        return carry

    lax.fori_loop(0, planes, branch, 0)
    part_start(sent_a, got_a, 0)
    gather_done(0)
    gather_done(1)
    keep_weights = pltpu.make_async_copy(w.at[pl.ds(0, 2)], kept_weights, keep_sem.at[1])
    keep_mixer = pltpu.make_async_copy(total_a, kept_mixer, keep_sem.at[2])
    keep_weights.start()
    keep_mixer.start()
    pass_on(2, 1)
    part_pass(sent_a, got_a, 0)
    for k in range(4, chunks - 2):
        own_at_end(k)
    own_between(4)
    for t in range(2, planes):
        pass_on(2, t)
    own_between(5)
    keep_weights.wait()
    keep_mixer.wait()
    total_a[...] = jnp.zeros_like(total_a)
    total_b[...] = jnp.zeros_like(total_b)
    all_wait(e_all, 1)
    transposed(e_all, 1)
    part_wait(sent_a, got_a, 0)

    def second_norm(span):
        hidden = tokens[span, :].astype(jnp.float32) + summed(sent_a, got_a, span)
        hidden_one[span, :] = hidden
        n_two[at.block, span, :] = (hidden * scale_of(hidden) * gains[1:2, :]).astype(jnp.bfloat16)

    by_rows(second_norm)
    all_start(n_two, 2)
    part_done(sent_a, got_a, 0)
    pass_on(3, 1)
    all_pass(n_two, 2)
    begin(7)
    begin(8)
    for t in range(2, planes):
        pass_on(3, t)
    pass_on(4, 1)
    take_last(2)
    near_wait(n_two, 2)

    def cast(source, target):
        def run(b, carry):
            target[b] = source[b].astype(jnp.bfloat16)
            return carry

        lax.fori_loop(0, 4, run, 0)

    def feed_forward(k):
        def half(j, carry):
            t = lax.rem(at.x + j, 2)

            @pl.when(jnp.logical_and(k == 2, j == 1))
            def _():
                own_at_end(7)
                own_at_end(8)
                far_wait(n_two, 2)

            normed = n_two[pair(t)].reshape(2 * rows, width)
            both = dot(normed, whole(k, 0, 2 * step_cols))
            d_active = dot(
                e_all[pair(t)].reshape(2 * rows, width), whole(k, 2 * step_cols, 3 * step_cols)
            )
            gate, upper = both[:, :step_cols], both[:, step_cols:]
            sigma = jax.nn.sigmoid(gate)
            soft = gate * sigma
            here = pl.ds(pl.multiple_of(t * 2 * rows, 2 * rows), 2 * rows)
            active[here, :] = (soft * upper).astype(jnp.bfloat16)
            d_gate_up[here, step_cols:] = (d_active * soft).astype(jnp.bfloat16)
            d_gate_up[here, :step_cols] = (
                d_active * upper * sigma * (1.0 + gate * (1.0 - sigma))
            ).astype(jnp.bfloat16)

            def spread(q, inner):
                back = times_transposed(d_gate_up[here, :], two_planes(k, q, 0, 2 * step_cols))
                total_b[pair(t), :, two_columns(q)] += back.reshape(2, rows, 2 * wide)
                out = times_transposed(
                    active[here, :], two_planes(k, q, 2 * step_cols, 3 * step_cols)
                )
                total_a[pair(t), :, two_columns(q)] += out.reshape(2, rows, 2 * wide)
                return inner

            lax.fori_loop(0, planes // 2, spread, 0)
            return carry

        lax.fori_loop(0, 2, half, 0)

        @pl.when(k == chunks - 1)
        def _():
            cast(total_b, sent_a)
            part_start(sent_a, got_a, 2)

        gather_done(k)
        pl.when(k == 2)(lambda: transposed(n_two, 0))

        def grads(n, carry):
            span = pl.ds(pl.multiple_of(n * step_cols, step_cols), step_cols)
            weight_grad(0, d_gate_up[:, span], k, span)
            return carry

        lax.fori_loop(0, 2, grads, 0)
        weight_grad(1, active[...], k, pl.ds(2 * step_cols, step_cols))

    def one_part(i, carry):
        k = i + 2
        core_wait(k)
        feed_forward(k)
        core_start(i)
        pl.when(k + 2 < chunks)(lambda: pass_on(k + 2, 2))
        pl.when(k + 3 < chunks)(lambda: pass_on(k + 3, 1))
        pl.when(i == 0)(lambda: own_between(6))
        pl.when(i == 0)(lambda: own_between(7))
        pl.when(i == 1)(lambda: own_between(8))
        pl.when(k + 1 < chunks)(lambda: take_last(k + 1))
        first_hop(i)
        pl.when(jnp.logical_and(i >= 3, i < parts - 1))(lambda: tick(i - 2))

        @pl.when(k + 1 < chunks)
        def _():
            for t in range(3, planes):
                pass_on(k + 1, t)

        return carry

    lax.fori_loop(0, parts, one_part, 0)

    restore_weights = pltpu.make_async_copy(kept_weights, w.at[pl.ds(0, 2)], keep_sem.at[1])
    restore_weights.start()

    cast(total_a, sent_b)
    restore_mixer = pltpu.make_async_copy(kept_mixer, total_a, keep_sem.at[2])
    restore_mixer.start()
    part_pass(sent_a, got_a, 2)
    tick(4)
    part_wait(sent_a, got_a, 2)

    def through_second(span):
        grad = back_through_norm(
            summed(sent_a, got_a, span), hidden_one[span, :], gains[1:2, :], 1
        )
        grad = e_all[at.block, span, :].astype(jnp.float32) + grad
        d_hidden[span, :] = grad
        f_all[at.block, span, :] = grad.astype(jnp.bfloat16)

    by_rows(through_second)
    all_done(n_two, 2)
    all_start(f_all, 3)
    part_done(sent_a, got_a, 2)
    all_pass(f_all, 3)
    part_start(sent_b, n_two, 1)
    sum_done(0)
    transposed(n_one, 2)
    all_done(n_one, 0)
    restore_weights.wait()
    restore_mixer.wait()
    tick(5)
    all_wait(f_all, 3)

    def into_mixer(t, carry):
        grad = f_all[pair(t)].reshape(2 * rows, width)
        d_mixed = dot(grad, whole(0, channels, 2 * channels)).reshape(2, rows, channels)
        conv = total_a[pair(t), :, 3 * channels : 4 * channels]
        c_part = total_a[pair(t), :, channels : 2 * channels]
        n_one[pair(t), :, 2 * channels : 3 * channels] = (d_mixed * conv).astype(jnp.bfloat16)
        d_conv[pair(t), 0:rows, :] = d_mixed * c_part
        return carry

    lax.fori_loop(0, 2, into_mixer, 0)
    head = d_conv.at[:, pl.ds(0, 8), :]
    halo_core(1, head).start()
    pl.when(at.gives_last)(lambda: halo_plane(1, head, at.last).start())

    def from_c(i, carry):
        t, q = lax.div(i, planes // 2), lax.rem(i, planes // 2)
        grad = n_one[pair(t), :, 2 * channels : 3 * channels].reshape(2 * rows, channels)
        out = times_transposed(grad, two_planes(0, q, 0, channels))
        total_b[pair(t), :, two_columns(q)] = out.reshape(2, rows, 2 * wide)
        return carry

    lax.fori_loop(0, planes, from_c, 0)
    sum_done(1)
    transposed(f_all, 3)

    d_c = n_one[:, :, 2 * channels : 3 * channels].reshape(4 * rows, channels)
    weight_grad(2, d_c, 0, pl.ds(0, channels))
    weight_grad(3, mixed[...].reshape(4 * rows, channels), 0, pl.ds(channels, channels))
    core_start(jnp.int32(parts))
    tick(6)
    halo_core(1, head).wait_recv()
    pl.when(at.gives_next)(lambda: halo_plane(1, head, at.next).wait_recv())
    for group in range(2):

        @pl.when(at.is_first)
        def _():
            d_conv[2 * group, rows : rows + 8, :] = halo[2, 2 * group]
            d_conv[2 * group + 1, rows : rows + 8, :] = halo[2, 2 * group + 1]

        @pl.when(at.is_last)
        def _():
            d_conv[2 * group, rows : rows + 8, :] = halo[2, 2 * group + 1]
            d_conv[2 * group + 1, rows : rows + 8, :] = halo[3, 2 * group]

    def convolve_back(b, carry):
        place = place_in(b, 0)
        d_gated = jnp.zeros((rows, channels), jnp.float32)
        for j in range(3):
            ahead = 2 - j
            moved = jnp.where(
                place_in(b, ahead) >= ahead, d_conv[b, ahead : ahead + rows, :], 0.0
            )
            d_gated = d_gated + moved * taps[2 + j : 3 + j, :]
            product = d_conv[b, 0:rows, :] * gated[b, 6 + j : 6 + j + rows, :]
            small[2 + j : 3 + j, channel_columns] += jnp.sum(
                jnp.where(place >= ahead, product, 0.0), axis=0, keepdims=True
            )
        x_part = total_a[b, :, 2 * channels : 3 * channels]
        n_one[b, :, 0:channels] = (d_gated * x_part).astype(jnp.bfloat16)
        b_part = total_a[b, :, 0:channels]
        n_one[b, :, channels : 2 * channels] = (d_gated * b_part).astype(jnp.bfloat16)
        return carry

    lax.fori_loop(0, 4, convolve_back, 0)
    first_hop(jnp.int32(parts))

    def d_normed(i, carry):
        t, q = lax.div(i, planes // 2), lax.rem(i, planes // 2)
        grad = n_one[pair(t), :, 0 : 2 * channels].reshape(2 * rows, 2 * channels)
        out = times_transposed(grad, two_planes(1, q, 0, 2 * channels))
        out = total_b[pair(t), :, two_columns(q)] + out.reshape(2, rows, 2 * wide)
        sent_a[pair(t), :, two_columns(q)] = out.astype(jnp.bfloat16)
        return carry

    lax.fori_loop(0, planes, d_normed, 0)
    part_start(sent_a, got_a, 3)

    def b_and_x_weight(n, carry):
        span = pl.ds(pl.multiple_of(n * channels, channels), channels)
        grad = n_one[:, :, span].reshape(4 * rows, channels)
        weight_grad(2, grad, 1, span)
        return carry

    lax.fori_loop(0, 2, b_and_x_weight, 0)
    core_start(jnp.int32(parts + 1))
    tick(7)
    part_pass(sent_a, got_a, 3)
    first_hop(jnp.int32(parts + 1))
    part_pass(sent_b, n_two, 1)
    tick(8)
    part_wait(sent_a, got_a, 3)

    def through_first(span):
        hidden = tokens[span, :].astype(jnp.float32)
        grad = back_through_norm(summed(sent_a, got_a, span), hidden, gains[0:1, :], 0)
        sent_a[at.block, span, :] = (d_hidden[span, :] + grad).astype(jnp.bfloat16)

    by_rows(through_first)
    d_tokens_copy = pltpu.make_async_copy(sent_a.at[at.block], d_tokens, keep_sem.at[3])
    d_tokens_copy.start()

    def small_copy(i, to):
        return remote(small, small_in.at[i], small_send.at[i], small_recv.at[i], to)

    def small_plane(t):
        to = lax.rem(at.me + 4 * t, count)
        return remote(
            small, small_in.at[2 + t], small_send.at[2 + t], small_recv.at[2 + t], (to, at.x)
        )

    small_copy(0, at.core).start()
    tick(9)
    for i, (here, following) in enumerate(
        ((at.core, at.beside), (at.beside, at.across), (at.across, None))
    ):
        small_copy(i, here).wait()
        small[...] += small_in[i]
        if following is not None:
            small_copy(i + 1, following).start()
    for t in range(1, planes):
        small_plane(t).start()
    tick(10)
    for t in range(1, planes):
        small_plane(t).wait()
    for t in range(1, planes):
        small[...] += small_in[2 + t]
    part_wait(sent_b, n_two, 1)

    def last_out(span):
        total = hidden_one[span, :] + summed(sent_b, n_two, span)
        sent_b[at.block, span, :] = total.astype(jnp.bfloat16)

    by_rows(last_out)
    result_copy = pltpu.make_async_copy(sent_b.at[at.block], result, keep_sem.at[4])
    result_copy.start()
    for j in range(11, chunks + planes - 1):
        tick(j)

    d_tokens_copy.wait()
    result_copy.wait()
    part_done(sent_a, got_a, 3)
    all_done(e_all, 1)
    part_done(sent_b, n_two, 1)
    all_done(f_all, 3)
    halo_core(0, tail).wait_send()
    halo_core(1, head).wait_send()
    pl.when(at.gives_next)(lambda: halo_plane(0, tail, at.next).wait_send())
    pl.when(at.gives_last)(lambda: halo_plane(1, head, at.last).wait_send())
    for v in range(2, chunks):
        sum_done(v)


def one_kernel(planes, seq_len, weights, tokens, d_out, gains):
    chunks, _, share, cols = weights.shape
    parts = chunks - 2
    rows, width = tokens.shape
    channels = width // 4
    low, full = jnp.bfloat16, jnp.float32
    shape = jax.ShapeDtypeStruct
    vmem, anywhere = pl.BlockSpec(memory_space=pltpu.VMEM), pl.BlockSpec(memory_space=pl.ANY)
    dma = pltpu.SemaphoreType.DMA
    block = (4, rows, width)
    return pl.pallas_call(
        functools.partial(kernel, planes, parts, seq_len),
        out_shape=(
            shape((rows, width), low),
            shape((rows, width), low),
            shape((chunks, share, cols), low),
            shape((chunks, share, cols), low),
            shape((8, width), full),
            shape((2, planes, 2, 2, share, cols), low),
            shape(block, full),
        ),
        in_specs=[anywhere, vmem, anywhere, vmem],
        out_specs=[anywhere, anywhere, anywhere, anywhere, vmem, anywhere, anywhere],
        scratch_shapes=[
            pltpu.VMEM((chunks, planes, 2, 2, share, cols), low),
            pltpu.VMEM((2, planes, 2, share, cols), low),
            pltpu.VMEM((chunks, 2, share, cols), low),
            pltpu.VMEM(block, low),
            pltpu.VMEM(block, low),
            pltpu.VMEM(block, low),
            pltpu.VMEM(block, low),
            pltpu.VMEM(block, low),
            pltpu.VMEM(block, low),
            pltpu.VMEM(block, full),
            pltpu.VMEM(block, full),
            pltpu.VMEM((3, rows, width), low),
            pltpu.VMEM((4, rows + 8, channels), full),
            pltpu.VMEM((4, rows + 8, channels), full),
            pltpu.VMEM((4, rows, channels), low),
            pltpu.VMEM((4 * rows, PART), low),
            pltpu.VMEM((4 * rows, 2 * PART), low),
            pltpu.VMEM((rows, width), full),
            pltpu.VMEM((rows, width), full),
            pltpu.VMEM((4, 4, 8, channels), full),
            pltpu.VMEM((4 * planes,) + gains.shape, low),
            pltpu.VMEM((8, width), full),
            pltpu.VMEM((8, channels), full),
            pltpu.VMEM((2 + planes, 8, width), full),
            dma((4 * planes,)),
            dma((4 * planes,)),
            dma((2 + planes,)),
            dma((2 + planes,)),
            dma((chunks,)),
            dma((chunks,)),
            dma((chunks,)),
            dma((chunks, 2, planes)),
            dma((chunks, planes)),
            dma((chunks, planes)),
            dma((chunks, planes)),
            dma((chunks,)),
            dma((chunks,)),
            pltpu.SemaphoreType.REGULAR,
            dma((chunks, 2, planes)),
            dma((chunks, 2, planes)),
            pltpu.SemaphoreType.REGULAR((2,)),
            dma((chunks,)),
            dma((chunks,)),
            dma((chunks,)),
            dma((4, 6)),
            dma((4, 6)),
            dma((4, 6)),
            dma((4, 6)),
            dma((4,)),
            dma((4,)),
            dma((5,)),
        ],
        compiler_params=pltpu.CompilerParams(
            collective_id=0, has_side_effects=True, vmem_limit_bytes=64 * 1024 * 1024
        ),
    )(weights, tokens, d_out, gains)


def split_kernel(hidden, parts, gate, up, down, in_weight, out_weight, weights):
    channels = out_weight.shape[1] // 2
    left = parts * PART - hidden
    blank = jnp.zeros((gate.shape[0], left), jnp.bfloat16)
    for which, source in enumerate((gate, up, down)):
        here = pl.ds(which * PART, PART)
        for half in range(2):
            for part in range(parts):
                low = half * hidden + part * PART
                if part < parts - 1 or left == 0:
                    weights[2 + part, half, :, here] = source[:, low : low + PART]
                else:
                    last = source[:, low : low + PART - left]
                    weights[2 + part, half, :, here] = jnp.concatenate([last, blank], axis=1)
    for half in range(2):
        span = slice(half * channels, (half + 1) * channels)
        weights[0, half, :, 0:channels] = in_weight[1, :, span]
        weights[0, half, :, channels:] = out_weight[:, span]
        weights[1, half, :, 0:channels] = in_weight[0, :, span]
        weights[1, half, :, channels:] = in_weight[2, :, span]


def split(gate, up, down, in_weight, out_weight, step=32):
    share, columns = gate.shape
    hidden = columns // 2
    parts = -(-hidden // PART)
    by_rows = pl.BlockSpec((step, columns), lambda i: (i, 0))
    cols = 3 * PART
    return pl.pallas_call(
        functools.partial(split_kernel, hidden, parts),
        grid=(share // step,),
        out_shape=jax.ShapeDtypeStruct((parts + 2, 2, share, cols), jnp.bfloat16),
        in_specs=[
            by_rows,
            by_rows,
            by_rows,
            pl.BlockSpec((3, step, in_weight.shape[2]), lambda i: (0, i, 0)),
            pl.BlockSpec((step, out_weight.shape[1]), lambda i: (i, 0)),
        ],
        out_specs=pl.BlockSpec((parts + 2, 2, step, cols), lambda i: (0, 0, i, 0)),
    )(gate, up, down, in_weight, out_weight)


def join_kernel(hidden, parts, own, other, gate, up, down, in_weight, out_weight):
    channels = out_weight.shape[1] // 2
    side = lax.rem(lax.div(lax.axis_index("seq"), 2), 2)

    def put(half, source):
        for which, target in enumerate((gate, up, down)):
            pieces = [
                source[2 + part, :, which * PART : (which + 1) * PART].astype(jnp.float32)
                for part in range(parts)
            ]
            whole = jnp.concatenate(pieces, axis=1)[:, :hidden]
            target[:, half * hidden : (half + 1) * hidden] = whole
        span = slice(half * channels, (half + 1) * channels)
        in_weight[1, :, span] = source[0, :, 0:channels].astype(jnp.float32)
        out_weight[:, span] = source[0, :, channels:].astype(jnp.float32)
        in_weight[0, :, span] = source[1, :, 0:channels].astype(jnp.float32)
        in_weight[2, :, span] = source[1, :, channels:].astype(jnp.float32)

    @pl.when(side == 0)
    def _():
        put(0, own)
        put(1, other)

    @pl.when(side == 1)
    def _():
        put(0, other)
        put(1, own)


def join(own, other, hidden, channels, step=32):
    chunks, share, cols = own.shape
    parts = chunks - 2
    full = jnp.float32
    part = pl.BlockSpec((chunks, step, cols), lambda i: (0, i, 0))
    by_rows = pl.BlockSpec((step, 2 * hidden), lambda i: (i, 0))
    shape = jax.ShapeDtypeStruct
    return pl.pallas_call(
        functools.partial(join_kernel, hidden, parts),
        grid=(share // step,),
        out_shape=(
            shape((share, 2 * hidden), full),
            shape((share, 2 * hidden), full),
            shape((share, 2 * hidden), full),
            shape((3, share, 2 * channels), full),
            shape((share, 2 * channels), full),
        ),
        in_specs=[part, part],
        out_specs=(
            by_rows,
            by_rows,
            by_rows,
            pl.BlockSpec((3, step, 2 * channels), lambda i: (0, i, 0)),
            pl.BlockSpec((step, 2 * channels), lambda i: (i, 0)),
        ),
    )(own, other)


def on_device(
    tokens,
    norm1_gain,
    in_weight,
    conv_kernel,
    out_weight,
    norm2_gain,
    gate_weight,
    up_weight,
    down_weight,
    d_out,
):
    planes = lax.axis_size("seq") // 4
    here = lax.axis_index("seq")
    rows, width = tokens.shape[1:]
    share = gate_weight.shape[0]
    channels = in_weight.shape[2] // 2
    hidden = gate_weight.shape[1] // 2

    gains = jnp.concatenate([norm1_gain[None], norm2_gain[None], conv_kernel.T], axis=0)
    gains = jnp.pad(gains, ((0, 16 - gains.shape[0]), (0, 128 - share)))

    weights = split(
        gate_weight, up_weight, down_weight, jnp.swapaxes(in_weight, 0, 1), out_weight
    )
    result, d_tokens, own_grad, other_grad, small, _, _ = one_kernel(
        planes,
        lax.axis_size("seq") * rows // SEQS,
        weights,
        tokens[0],
        d_out[0],
        gains,
    )
    d_gate, d_up, d_down, d_in, d_branch = join(own_grad, other_grad, hidden, channels)
    sums = lax.dynamic_slice_in_dim(small, here * share, share, 1)
    return (
        result[None],
        d_tokens[None],
        sums[0],
        jnp.swapaxes(d_in, 0, 1),
        sums[2:5].T,
        d_branch,
        sums[1],
        d_gate,
        d_up,
        d_down,
    )


def fits(mesh):
    return mesh.shape["seq"] <= 16


def solution(mesh):
    return jax.shard_map(
        on_device if fits(mesh) else plain_on_device,
        mesh=mesh,
        in_specs=(
            P("fsdp", "seq", None),
            P("seq"),
            P("seq", None, "fsdp"),
            P("seq", None),
            P("seq", "fsdp"),
            P("seq"),
            P("seq", "fsdp"),
            P("seq", "fsdp"),
            P("seq", "fsdp"),
            P("fsdp", "seq", None),
        ),
        out_specs=(
            P("fsdp", "seq", None),
            P("fsdp", "seq", None),
            P("seq"),
            P("seq", None, "fsdp"),
            P("seq", None),
            P("seq", "fsdp"),
            P("seq"),
            P("seq", "fsdp"),
            P("seq", "fsdp"),
            P("seq", "fsdp"),
        ),
        check_vma=False,
    )
```

```python
import functools

import jax
import jax.numpy as jnp
from jax import lax
from jax.experimental import pallas as pl
from jax.experimental.pallas import tpu as pltpu
from jax.sharding import PartitionSpec as P

SEQS = 3
EPSILON = 1e-05
BOTH = ("seq", "fsdp")
MESH = pl.DeviceIdType.MESH
PART = 256


def times_transposed(left, right):
    return lax.dot_general(
        left, right, (((1,), (1,)), ((), ())), preferred_element_type=jnp.float32
    )


def transposed_times(left, right):
    return lax.dot_general(
        left, right, (((0,), (0,)), ((), ())), preferred_element_type=jnp.float32
    )


def times(left, right):
    return jnp.dot(left, right, preferred_element_type=jnp.float32)


def root_norm(hidden, gain):
    scale = lax.rsqrt(jnp.mean(hidden * hidden, axis=-1, keepdims=True) + EPSILON)
    return (hidden * scale * gain, scale)


def norm_back(grad, hidden, scale, gain):
    weighted = grad * gain
    inner = jnp.sum(weighted * hidden, axis=-1, keepdims=True)
    d_hidden = scale * weighted - hidden * (scale * scale * scale) * inner / hidden.shape[-1]
    d_gain = jnp.sum(grad * hidden * scale, axis=0)
    return (d_hidden, d_gain)


def device(z, y, c, x):
    return (z * 4 + y * 2 + c) * 2 + x


def every(planes):
    return [
        (z, y, c, x) for z in range(planes) for y in range(2) for c in range(2) for x in range(2)
    ]


def plain_on_device(
    tokens,
    norm1_gain,
    in_weight,
    conv_kernel,
    out_weight,
    norm2_gain,
    gate_weight,
    up_weight,
    down_weight,
    d_out,
):
    planes = lax.axis_size("seq") // 4
    here = lax.axis_index("seq")
    y, c, x = (here // 2) % 2, here % 2, lax.axis_index("fsdp")
    z = here // 4
    rows, width = tokens.shape[1:]
    share = gate_weight.shape[0]
    plane_groups = [
        [device(z, y, c, x) for x in range(2) for y in range(2)]
        for z in range(planes)
        for c in range(2)
    ]
    column_groups = [
        [z * 4 + y * 2 + c for z in range(planes) for c in range(2)] for y in range(2)
    ]
    members = 2 * planes

    def moved(value, target):
        pairs = []
        for place in every(planes):
            to = target(*place)
            if to is not None:
                pairs.append((device(*place), device(*to)))
        return lax.ppermute(value, BOTH, pairs)

    def swap_y(value):
        return moved(value, lambda z, y, c, x: (z, 1 - y, c, x))

    def swap_x(value):
        return moved(value, lambda z, y, c, x: (z, y, c, 1 - x))

    def swap_both(value):
        return moved(value, lambda z, y, c, x: (z, 1 - y, c, 1 - x))

    def ordered(first, second, flag):
        return jnp.where(flag == 0, jnp.stack([first, second]), jnp.stack([second, first]))

    def plane_gather(value):
        by_y = ordered(value, swap_y(value), y)
        other = ordered(swap_x(value), swap_both(value), y)
        return ordered(by_y, other, x).reshape((4 * value.shape[0],) + value.shape[1:])

    def plane_sum(partial):
        sent = partial.astype(jnp.bfloat16).reshape(4, rows, width)
        got = lax.all_to_all(sent, BOTH, 0, 0, axis_index_groups=plane_groups, tiled=True)
        return jnp.sum(got.astype(jnp.float32), axis=0)

    def fetch(weight):
        halves = weight.reshape(share, 2, -1)
        mine = jnp.where(y == 0, halves[:, 0], halves[:, 1])
        theirs = jnp.where(y == 0, halves[:, 1], halves[:, 0])
        pair = ordered(mine, swap_y(theirs), y)
        got = lax.all_gather(pair, "seq", axis=0, tiled=False, axis_index_groups=column_groups)
        got = got.reshape(planes, 2, 2, share, -1)
        return jnp.swapaxes(got, 1, 2).reshape(width, -1)

    def give(grad):
        sent = grad.astype(jnp.bfloat16).reshape(planes, 2, 2, share, -1)
        sent = jnp.swapaxes(sent, 1, 2).reshape(members * 2, share, -1)
        got = lax.psum_scatter(
            sent, "seq", scatter_dimension=0, tiled=True, axis_index_groups=column_groups
        )
        mine = jnp.where(y == 0, got[0], got[1])
        theirs = jnp.where(y == 0, got[1], got[0])
        pair = ordered(mine, swap_y(theirs), y).astype(jnp.float32)
        return jnp.concatenate([pair[0], pair[1]], axis=1)

    gains = lax.all_gather(
        jnp.concatenate(
            [norm1_gain[:, None], norm2_gain[:, None], conv_kernel], axis=1
        ),
        "seq",
        axis=0,
        tiled=True,
    ).astype(jnp.float32)
    gain_one, gain_two, kernel = gains[:, 0], gains[:, 1], gains[:, 2:]
    taps = kernel.shape[1]
    margin = taps - 1
    channels = in_weight.shape[2] // 2
    first_channel = x * (2 * channels) + y * channels
    kernel_here = lax.dynamic_slice_in_dim(kernel, first_channel, channels, 0)

    w_in_halves = jnp.swapaxes(in_weight.reshape(share, 3, 2, channels), 1, 2)
    w_mixer = fetch(
        jnp.concatenate(
            [w_in_halves.reshape(share, 2, 3 * channels), out_weight.reshape(share, 2, channels)],
            axis=2,
        ).reshape(share, 8 * channels)
    )
    w_in, w_out = w_mixer[:, : 3 * channels], w_mixer[:, 3 * channels :]

    hidden = tokens[0].astype(jnp.float32)
    normed, scale_one = root_norm(hidden, gain_one)
    normed_low = plane_gather(normed.astype(jnp.bfloat16))
    grad_low = plane_gather(d_out[0])

    w_gate = fetch(gate_weight)
    w_up = fetch(up_weight)
    w_down = fetch(down_weight)

    projected = times(normed_low, w_in).reshape(2, 2, rows, 3 * channels)
    b_part = projected[..., :channels]
    c_part = projected[..., channels : 2 * channels]
    x_part = projected[..., 2 * channels :]
    gated = (b_part * x_part).astype(jnp.bfloat16)

    def swap_core(value):
        return moved(value, lambda z, y, c, x: (z, y, 1 - c, x))

    def to_next(value):
        return moved(
            value, lambda z, y, c, x: (z + 1, y, 0, x) if c == 1 and z + 1 < planes else None
        )

    def to_last(value):
        return moved(value, lambda z, y, c, x: (z - 1, y, 1, x) if c == 0 and z > 0 else None)

    tail = gated[:, :, rows - margin :]
    from_core, from_plane = swap_core(tail), to_next(tail[:, 1])
    before = jnp.where(
        c == 1, from_core, jnp.stack([from_plane, from_core[:, 0]], axis=1)
    )
    padded = jnp.concatenate([before, gated], axis=2).astype(jnp.float32)
    seq_len = lax.axis_size("seq") * rows // SEQS
    block = z * 4 + jnp.arange(2, dtype=jnp.int32) * 2 + c
    position = block[:, None] * rows + jnp.arange(rows, dtype=jnp.int32)
    in_sequence = position % seq_len
    masks = [
        (in_sequence >= margin - offset).astype(jnp.float32)[None, :, :, None]
        for offset in range(taps)
    ]
    conv = jnp.zeros_like(b_part)
    for offset in range(taps):
        conv = conv + masks[offset] * padded[:, :, offset : offset + rows] * kernel_here[:, offset]
    mixed = (c_part * conv).astype(jnp.bfloat16).reshape(4 * rows, channels)
    hidden_one = hidden + plane_sum(times_transposed(mixed, w_out))

    normed_two, scale_two = root_norm(hidden_one, gain_two)
    normed_two_low = plane_gather(normed_two.astype(jnp.bfloat16))
    gate = times(normed_two_low, w_gate)
    upper = times(normed_two_low, w_up)
    sigma = jax.nn.sigmoid(gate)
    active = (gate * sigma * upper).astype(jnp.bfloat16)
    d_active = times(grad_low, w_down)
    d_upper = (d_active * gate * sigma).astype(jnp.bfloat16)
    d_gate = (d_active * upper * sigma * (1.0 + gate * (1.0 - sigma))).astype(jnp.bfloat16)
    d_normed_two = plane_sum(times_transposed(d_gate, w_gate) + times_transposed(d_upper, w_up))
    result = hidden_one + plane_sum(times_transposed(active, w_down))
    d_gate_w = give(transposed_times(normed_two_low, d_gate))
    d_up_w = give(transposed_times(normed_two_low, d_upper))
    d_down_w = give(transposed_times(grad_low, active))

    d_hidden_two, d_gain_two = norm_back(d_normed_two, hidden_one, scale_two, gain_two)
    grad_one = d_out[0].astype(jnp.float32) + d_hidden_two
    grad_one_low = plane_gather(grad_one.astype(jnp.bfloat16))
    d_out_w = transposed_times(grad_one_low, mixed)
    d_mixed = times(grad_one_low, w_out).reshape(2, 2, rows, channels)
    d_c = d_mixed * conv
    d_conv = d_mixed * c_part
    kernel_cols = []
    d_padded = jnp.zeros((2, 2, rows + margin, channels), jnp.float32)
    for offset in range(taps):
        masked = masks[offset] * d_conv
        kernel_cols.append(jnp.sum(masked * padded[:, :, offset : offset + rows], axis=(0, 1, 2)))
        d_padded = d_padded + jnp.pad(
            masked * kernel_here[:, offset],
            ((0, 0), (0, 0), (offset, margin - offset), (0, 0)),
        )
    head = d_padded[:, :, :margin]
    from_core, from_plane = swap_core(head), to_last(head[:, 0])
    after = jnp.where(c == 0, from_core, jnp.stack([from_core[:, 1], from_plane], axis=1))
    d_gated = d_padded[:, :, margin:] + jnp.pad(
        after, ((0, 0), (0, 0), (rows - margin, 0), (0, 0))
    )
    d_projected = (
        jnp.concatenate([d_gated * x_part, d_c, d_gated * b_part], axis=3)
        .astype(jnp.bfloat16)
        .reshape(4 * rows, 3 * channels)
    )
    d_in_w = transposed_times(normed_low, d_projected)
    d_normed = plane_sum(times_transposed(d_projected, w_in))
    d_mixer = give(jnp.concatenate([d_in_w, d_out_w], axis=1)).reshape(share, 2, 4 * channels)
    d_in_w = jnp.swapaxes(d_mixer[:, :, : 3 * channels].reshape(share, 2, 3, channels), 1, 2)
    d_in_w = d_in_w.reshape(share, 3, 2 * channels)
    d_out_w = d_mixer[:, :, 3 * channels :].reshape(share, 2 * channels)
    d_hidden, d_gain_one = norm_back(d_normed, hidden, scale_one, gain_one)
    d_tokens = (grad_one + d_hidden).astype(jnp.bfloat16)

    d_kernel = lax.dynamic_update_slice(
        jnp.zeros((width, taps), jnp.float32), jnp.stack(kernel_cols, axis=1), (first_channel, 0)
    )
    small = jnp.concatenate([d_gain_one[:, None], d_gain_two[:, None], d_kernel], axis=1)
    small = lax.psum(small, BOTH)
    small = lax.dynamic_slice_in_dim(small, here * share, share, 0)
    return (
        result.astype(jnp.bfloat16)[None],
        d_tokens[None],
        small[:, 0],
        d_in_w,
        small[:, 2:],
        d_out_w,
        small[:, 1],
        d_gate_w,
        d_up_w,
        d_down_w,
    )


class Place:
    def __init__(self, planes):
        self.planes = planes
        self.me, self.x = lax.axis_index("seq"), lax.axis_index("fsdp")
        self.z = lax.div(self.me, 4)
        self.y = lax.rem(lax.div(self.me, 2), 2)
        self.c = lax.rem(self.me, 2)
        self.core = (self.me + 1 - 2 * self.c, self.x)
        self.across = (self.me + 2 - 4 * self.y, self.x)
        self.low, self.high = (self.me - 4, self.x), (self.me + 4, self.x)
        self.has_low, self.has_high = self.z > 0, self.z < planes - 1
        self.block = self.x * 2 + self.y
        self.beside = (self.me, 1 - self.x)
        self.beside_block = (1 - self.x) * 2 + self.y
        self.across_block = self.x * 2 + 1 - self.y
        self.far_block = (1 - self.x) * 2 + 1 - self.y
        self.is_first, self.is_last = self.c == 0, self.c == 1
        self.gives_next = jnp.logical_and(self.is_last, self.has_high)
        self.gives_last = jnp.logical_and(self.is_first, self.has_low)
        self.next, self.last = (self.me + 3, self.x), (self.me - 3, self.x)


def remote(source, target, send, receive, device_id):
    return pltpu.make_async_remote_copy(
        src_ref=source,
        dst_ref=target,
        send_sem=send,
        recv_sem=receive,
        device_id=device_id,
        device_id_type=MESH,
    )


def signal(semaphore, device_id):
    pl.semaphore_signal(semaphore, inc=1, device_id=device_id, device_id_type=MESH)


def dot(left, right):
    return jnp.dot(left, right, preferred_element_type=jnp.float32)


def kernel(
    planes,
    parts,
    seq_len,
    weights,
    tokens,
    d_out,
    gains_here,
    result,
    d_tokens,
    own_grad,
    other_grad,
    small,
    kept_weights,
    kept_mixer,
    w,
    core_in,
    extra,
    n_one,
    f_all,
    n_two,
    e_all,
    sent_a,
    sent_b,
    total_a,
    total_b,
    got_a,
    gated,
    d_conv,
    mixed,
    active,
    d_gate_up,
    hidden_one,
    d_hidden,
    halo,
    gains_in,
    gains,
    taps,
    small_in,
    gain_send,
    gain_recv,
    small_send,
    small_recv,
    local_sem,
    y_send,
    y_recv,
    z_send,
    z_recv,
    c_send,
    c_recv,
    core_send,
    core_recv,
    core_free,
    sum_send,
    sum_recv,
    ready,
    last_send,
    last_recv,
    own_sem,
    all_send,
    all_recv,
    part_send,
    part_recv,
    halo_send,
    halo_recv,
    keep_sem,
):
    at = Place(planes)
    z, y, c = at.z, at.y, at.c
    rows, width = tokens.shape
    channels = taps.shape[1]
    count = 4 * planes
    share = weights.shape[2]
    wide = 4 * share
    chunks = parts + 2
    step_cols = weights.shape[3] // 3

    def y_copies(k):
        return (
            pltpu.make_async_copy(weights.at[k, y], w.at[k, z, y, c], local_sem.at[k]),
            remote(weights.at[k, 1 - y], w.at[k, z, y, c], y_send.at[k], y_recv.at[k], at.across),
        )

    def piece(k, p):
        return w.at[k, p, :, c]

    def to_side(k, p, side):
        return remote(
            piece(k, p),
            piece(k, p),
            z_send.at[k, side, p],
            z_recv.at[k, p],
            at.high if side else at.low,
        )

    def to_core(k, p):
        return remote(piece(k, p), piece(k, p), c_send.at[k, p], c_recv.at[k, p], at.core)

    def begin(k):
        for copy in y_copies(k):
            copy.start()

    def own(k):
        y_copies(k)[0].wait()
        remote(
            weights.at[k, y], w.at[k, z, 1 - y, c], y_send.at[k], y_recv.at[k], at.across
        ).wait_recv()
        pl.when(at.has_low)(lambda: to_side(k, z, 0).start())
        pl.when(at.has_high)(lambda: to_side(k, z, 1).start())
        to_core(k, z).start()

    def relay(k, t):
        below, above = z - t, z + t

        @pl.when(below >= 0)
        def _():
            to_side(k, below, 1).wait_recv()
            pl.when(at.has_high)(lambda: to_side(k, below, 1).start())
            to_core(k, below).start()

        @pl.when(above < planes)
        def _():
            to_side(k, above, 0).wait_recv()
            pl.when(at.has_low)(lambda: to_side(k, above, 0).start())
            to_core(k, above).start()

    between = jnp.logical_and(at.has_low, at.has_high)

    def pass_on(k, t):
        pl.when(between)(lambda: relay(k, t))

    def own_between(k):
        pl.when(between)(lambda: own(k))

    def own_at_end(k):
        pl.when(jnp.logical_not(between))(lambda: own(k))

    def take_last(k):
        @pl.when(jnp.logical_not(between))
        def _():
            for t in range(1, planes):
                relay(k, t)

    def core_wait(k):
        for p in range(planes):
            remote(
                w.at[k, p, :, 1 - c], w.at[k, p, :, 1 - c], c_send.at[k, p], c_recv.at[k, p], at.core
            ).wait_recv()

    def gather_done(k):
        y_copies(k)[1].wait_send()
        for p in range(planes):
            pl.when(jnp.logical_and(at.has_low, p >= z))(lambda: to_side(k, p, 0).wait_send())
            pl.when(jnp.logical_and(at.has_high, p <= z))(lambda: to_side(k, p, 1).wait_send())
            to_core(k, p).wait_send()

    def chunk_of(v):
        return lax.rem(v + 2, chunks)

    def core_copy(v):
        k = chunk_of(v)
        return remote(
            w.at[k, :, :, 1 - c],
            core_in.at[lax.rem(v, 2)],
            core_send.at[k],
            core_recv.at[k],
            at.core,
        )

    def core_start(v):
        pl.when(v >= 2)(lambda: pl.semaphore_wait(core_free, 1))
        core_copy(v).start()

    def core_add(v):
        k, slot = chunk_of(v), lax.rem(v, 2)
        core_copy(v).wait()

        def add(p, carry):
            total = w[k, p, :, c].astype(jnp.float32) + core_in[slot, p].astype(jnp.float32)
            w[k, p, :, c] = total.astype(jnp.bfloat16)
            return carry

        lax.fori_loop(0, planes, add, 0)
        pl.when(v < chunks - 2)(lambda: signal(core_free, at.core))
        pl.when(at.has_low)(lambda: signal(ready.at[1], at.low))
        pl.when(at.has_high)(lambda: signal(ready.at[0], at.high))

    def landing(k, d):
        return w.at[k, d, :, 1 - c]

    def sum_up(k, d):
        return remote(
            landing(k, d), landing(k, d), sum_send.at[k, 1, d], sum_recv.at[k, 1, d], at.high
        )

    def sum_down(k, d):
        return remote(
            landing(k, d), landing(k, d), sum_send.at[k, 0, d], sum_recv.at[k, 0, d], at.low
        )

    def sum_down_last(k, d):
        return remote(
            landing(k, d), extra.at[k], sum_send.at[k, 0, d], sum_recv.at[k, 0, d], at.low
        )

    def add_here(k, d, arrived):
        here = w[k, d, :, c].astype(jnp.float32)

        @pl.when(arrived)
        def _():
            w[k, d, :, 1 - c] = (w[k, d, :, 1 - c].astype(jnp.float32) + here).astype(jnp.bfloat16)

        @pl.when(jnp.logical_not(arrived))
        def _():
            w[k, d, :, 1 - c] = w[k, d, :, c]

    def each_plane(body):
        def run(i, carry):
            body(i)
            return carry

        lax.fori_loop(0, planes, run, 0)

    def up_pass(v):
        k = chunk_of(v)
        pl.when(at.has_high)(lambda: pl.semaphore_wait(ready.at[1], 1))

        def one(i):
            d = planes - 1 - i

            @pl.when(d > z)
            def _():
                pl.when(at.has_low)(lambda: sum_up(k, d).wait_recv())
                add_here(k, d, at.has_low)
                sum_up(k, d).start()

        each_plane(one)

    def up_last(v):
        k = chunk_of(v)

        @pl.when(at.has_low)
        def _():
            sum_up(k, z).wait_recv()
            total = w[k, z, :, c].astype(jnp.float32) + w[k, z, :, 1 - c].astype(jnp.float32)
            w[k, z, :, c] = total.astype(jnp.bfloat16)

    def add_up(v):
        up_pass(v)
        up_last(v)

    def down_pass(v):
        k = chunk_of(v)
        pl.when(at.has_low)(lambda: pl.semaphore_wait(ready.at[0], 1))

        def one(d):
            @pl.when(d < z)
            def _():
                pl.when(at.has_high)(lambda: sum_down(k, d).wait_recv())
                add_here(k, d, at.has_high)
                pl.when(z - 1 > d)(lambda: sum_down(k, d).start())
                pl.when(z - 1 == d)(lambda: sum_down_last(k, d).start())

        each_plane(one)

    def down_last(v):
        k = chunk_of(v)

        @pl.when(at.has_high)
        def _():
            sum_down_last(k, z).wait_recv()
            total = w[k, z, :, c].astype(jnp.float32) + extra[k].astype(jnp.float32)
            w[k, z, :, c] = total.astype(jnp.bfloat16)

    def add_down(v):
        down_pass(v)
        down_last(v)

    def give_copies(k):
        return (
            pltpu.make_async_copy(w.at[k, z, y, c], own_grad.at[k], own_sem.at[k]),
            remote(
                w.at[k, z, 1 - y, c], other_grad.at[k], last_send.at[k], last_recv.at[k], at.across
            ),
        )

    def give(v):
        for copy in give_copies(chunk_of(v)):
            copy.start()

    def sum_done(v):
        k = chunk_of(v)
        for d in range(planes):
            pl.when(d > z)(lambda: sum_up(k, d).wait_send())
            pl.when(d < z)(lambda: sum_down(k, d).wait_send())
        for copy in give_copies(k):
            copy.wait()

    def first_hop(v):
        core_add(v)
        pl.when(jnp.logical_not(at.has_low))(lambda: add_up(v))
        pl.when(jnp.logical_not(at.has_high))(lambda: add_down(v))

    near_low = z < planes - 1 - z

    def stage(o, flag, do):
        there = jnp.logical_and(o >= 0, o < chunks)
        pl.when(jnp.logical_and(there, flag))(lambda: do(o))

    far = jnp.maximum(z, planes - 1 - z)

    def older(j):
        stage(j - far, jnp.logical_and(near_low, at.has_high), add_down)
        stage(j - far, jnp.logical_and(jnp.logical_not(near_low), at.has_low), add_up)

    def tick(j):
        older(j)
        near = planes - 1 - far
        stage(j - near, jnp.logical_and(near_low, at.has_low), add_up)
        stage(j - near, jnp.logical_and(jnp.logical_not(near_low), at.has_high), add_down)
        stage(j - far, far >= 0, give)

    last = jnp.int32(chunks - 1)

    def last_passes(first):
        @pl.when(between)
        def _():
            older(first)
            pl.when(near_low)(lambda: up_pass(last))
            down_pass(last)
            pl.when(jnp.logical_not(near_low))(lambda: up_pass(last))
            stage(first - far, far >= 0, give)

    def last_ticks(first):
        @pl.when(between)
        def _():
            up_last(last)
            down_last(last)
            give(last)

        @pl.when(jnp.logical_not(between))
        def _():
            for j in range(first, chunks + planes - 1):
                older(j)
                stage(j - far, far >= 0, give)

    part_rows = rows // 2

    def half_of(buffer, block, which_half):
        return buffer.at[block, pl.ds(which_half * part_rows, part_rows), :]

    def all_copy(buffer, which, i):
        block, which_half, to = (
            (at.block, 0, at.across if which < 2 else at.beside),
            (at.block, 1, at.across),
            (at.block, 1, at.beside),
            (at.block, 0, at.beside if which < 2 else at.across),
            (at.across_block, 0, at.beside)
            if which < 2
            else (at.beside_block, 0, at.across),
            (at.across_block, 1, at.beside),
        )[i]
        ref = half_of(buffer, block, which_half)
        return remote(ref, ref, all_send.at[which, i], all_recv.at[which, i], to)

    def all_landed(buffer, which, i):
        block, which_half = (
            (at.across_block if which < 2 else at.beside_block, 0),
            (at.across_block, 1),
            (at.beside_block, 1),
            (at.beside_block if which < 2 else at.across_block, 0),
            (at.far_block, 0),
            (at.far_block, 1),
        )[i]
        ref = half_of(buffer, block, which_half)
        remote(
            ref, ref, all_send.at[which, i], all_recv.at[which, i], at.across
        ).wait_recv()

    def all_start(buffer, which):
        for i in range(4):
            all_copy(buffer, which, i).start()

    def all_pass(buffer, which):
        for i in range(2):
            all_landed(buffer, which, i)
            all_copy(buffer, which, 4 + i).start()

    def all_wait(buffer, which):
        for i in range(2, 6):
            all_landed(buffer, which, i)

    def near_wait(buffer, which):
        all_landed(buffer, which, 3)

    def far_wait(buffer, which):
        for i in (2, 4, 5):
            all_landed(buffer, which, i)

    def all_done(buffer, which):
        for i in range(6):
            all_copy(buffer, which, i).wait_send()

    def part_copy(source, target, which, i):
        block, which_half, slot, to = (
            (at.far_block, 0, 2, at.beside),
            (at.far_block, 1, 2, at.across),
            (at.beside_block, 0, 0, at.beside),
            (at.across_block, 1, 1, at.across),
            (at.across_block, 0, 1, at.across),
            (at.beside_block, 1, 0, at.beside),
        )[i]
        return remote(
            half_of(source, block, which_half),
            half_of(target, slot, which_half),
            part_send.at[which, i],
            part_recv.at[which, i],
            to,
        )

    def part_start(source, target, which):
        for i in range(4):
            part_copy(source, target, which, i).start()

    def part_pass(source, target, which):
        for i, block in enumerate((at.across_block, at.beside_block)):
            part_copy(source, target, which, i).wait_recv()
            here = pl.ds(i * part_rows, part_rows)
            total = source[block, here, :].astype(jnp.float32)
            total = total + target[2, here, :].astype(jnp.float32)
            source[block, here, :] = total.astype(jnp.bfloat16)
            part_copy(source, target, which, 4 + i).start()

    def part_wait(source, target, which):
        for i in range(2, 6):
            part_copy(source, target, which, i).wait_recv()

    def part_done(source, target, which):
        for i in range(6):
            part_copy(source, target, which, i).wait_send()

    tile = 48

    def by_rows(body):
        def run(i, carry):
            body(pl.ds(pl.multiple_of(i * tile, tile), tile))
            return carry

        lax.fori_loop(0, rows // tile, run, 0)

    def scale_of(hidden):
        return lax.rsqrt(jnp.mean(hidden * hidden, axis=-1, keepdims=True) + EPSILON)

    def summed(source, target, span):
        total = source[at.block, span, :].astype(jnp.float32)
        for i in range(2):
            total = total + target[i, span, :].astype(jnp.float32)
        return total

    def back_through_norm(grad, hidden, gain, row):
        scale = scale_of(hidden)
        weighted = grad * gain
        inner = jnp.sum(weighted * hidden, axis=-1, keepdims=True)
        small[row : row + 1, :] += jnp.sum(grad * hidden * scale, axis=0, keepdims=True)
        return scale * weighted - hidden * (scale * scale * scale) * inner / width

    def transposed(buffer, k):
        def one(p, carry):
            cols = pl.ds(pl.multiple_of(p * wide, wide), wide)
            block = buffer[:, :, cols].reshape(4 * rows, wide).T
            w[k, p] = block.reshape(2, 2, share, 4 * rows)
            return carry

        lax.fori_loop(0, planes, one, 0)

    def whole(k, low, high):
        return w[k, :, :, :, :, low:high].reshape(planes * wide, high - low)

    def two_planes(k, q, low, high):
        return w[k, pair(q), :, :, :, low:high].reshape(2 * wide, high - low)

    def pair(t):
        return pl.ds(2 * t, 2)

    def two_columns(q):
        return pl.ds(pl.multiple_of(q * 2 * wide, 2 * wide), 2 * wide)

    def weight_grad(turned, grads, k, span):
        def some(q, carry):
            here = pair(q)
            out = dot(w[turned, here].reshape(2 * wide, 4 * rows), grads).astype(jnp.bfloat16)
            w[k, here, :, :, :, span] = out.reshape(2, 2, 2, share, grads.shape[1])
            return carry

        if grads.shape[1] <= PART:
            out = dot(w[turned].reshape(planes * wide, 4 * rows), grads).astype(jnp.bfloat16)
            w[k, :, :, :, :, span] = out.reshape(planes, 2, 2, share, grads.shape[1])
        else:
            lax.fori_loop(0, planes // 2, some, 0)

    halo[...] = jnp.zeros_like(halo)
    barrier = pltpu.get_barrier_semaphore()
    signal(barrier, at.beside)

    def greet(t, carry):
        signal(barrier, (lax.rem(at.me + t, count), at.x))
        return carry

    lax.fori_loop(1, count, greet, 0)
    pl.semaphore_wait(barrier, count)

    def gain_copy(t):
        other = lax.rem(at.me + t, count)
        return remote(
            gains_here,
            gains_in.at[at.me],
            gain_send.at[t],
            gain_recv.at[t],
            (other, at.x),
        )

    def gain_start(t, carry):
        gain_copy(t).start()
        return carry

    def gain_wait(t, carry):
        gain_copy(t).wait()
        return carry

    lax.fori_loop(1, count, gain_start, 0)
    begin(0)
    begin(1)
    e_copy = pltpu.make_async_copy(d_out, e_all.at[at.block], keep_sem.at[0])
    e_copy.start()
    small[...] = jnp.zeros_like(small)
    gains_in[at.me] = gains_here[...]
    lax.fori_loop(1, count, gain_wait, 0)
    for d in range(count):
        found = gains_in[d].astype(jnp.float32)[0:8, :share]
        gains[:, d * share : (d + 1) * share] = found
    channel_columns = pl.ds(pl.multiple_of(at.block * channels, channels), channels)
    taps[...] = gains[:, channel_columns]

    def first_norm(span):
        hidden = tokens[span, :].astype(jnp.float32)
        n_one[at.block, span, :] = (hidden * scale_of(hidden) * gains[0:1, :]).astype(jnp.bfloat16)

    by_rows(first_norm)
    all_start(n_one, 0)
    own(0)
    own(1)
    begin(2)
    relay(0, 1)
    relay(1, 1)
    all_pass(n_one, 0)
    e_copy.wait()
    all_start(e_all, 1)
    begin(3)
    relay(0, 2)
    relay(1, 2)
    own(2)
    all_pass(e_all, 1)
    for k in range(4, chunks):
        begin(k)
    for t in range(3, planes):
        relay(0, t)
    core_wait(0)
    all_wait(n_one, 0)

    def project_c(t, carry):
        normed = n_one[pair(t)].reshape(2 * rows, width)
        c_part = dot(normed, whole(0, 0, channels))
        total_a[pair(t), :, channels : 2 * channels] = c_part.reshape(2, rows, channels)
        return carry

    def project_b_x(t, carry):
        normed = n_one[pair(t)].reshape(2 * rows, width)
        b_x = dot(normed, whole(1, 0, 2 * channels)).reshape(2, rows, 2 * channels)
        total_a[pair(t), :, 0:channels] = b_x[:, :, :channels]
        total_a[pair(t), :, 2 * channels : 3 * channels] = b_x[:, :, channels:]
        product = (b_x[:, :, :channels] * b_x[:, :, channels:]).astype(jnp.bfloat16)
        gated[pair(t), 8 : 8 + rows, :] = product.astype(jnp.float32)
        return carry

    lax.fori_loop(0, 2, project_c, 0)
    for t in range(3, planes):
        relay(1, t)
    own(3)
    core_wait(1)
    lax.fori_loop(0, 2, project_b_x, 0)

    def halo_core(which, edge):
        return remote(
            edge, halo.at[2 * which], halo_send.at[2 * which], halo_recv.at[2 * which], at.core
        )

    def halo_plane(which, edge, target):
        return remote(
            edge,
            halo.at[2 * which + 1],
            halo_send.at[2 * which + 1],
            halo_recv.at[2 * which + 1],
            target,
        )

    tail = gated.at[:, pl.ds(rows, 8), :]
    halo_core(0, tail).start()
    pl.when(at.gives_next)(lambda: halo_plane(0, tail, at.next).start())
    halo_core(0, tail).wait_recv()
    pl.when(at.gives_last)(lambda: halo_plane(0, tail, at.last).wait_recv())
    for group in range(2):

        @pl.when(at.is_last)
        def _():
            gated[2 * group, 0:8, :] = halo[0, 2 * group]
            gated[2 * group + 1, 0:8, :] = halo[0, 2 * group + 1]

        @pl.when(at.is_first)
        def _():
            gated[2 * group, 0:8, :] = halo[1, 2 * group + 1]
            gated[2 * group + 1, 0:8, :] = halo[0, 2 * group]

    def start_of(block):
        return lax.rem((z * 4 + lax.rem(block, 2) * 2 + c) * rows, seq_len)

    def place_in(block, ahead):
        place = start_of(block) + ahead + lax.broadcasted_iota(jnp.int32, (rows, channels), 0)
        return jnp.where(place >= seq_len, place - seq_len, place)

    def convolve(b, carry):
        place = place_in(b, 0)
        conv = jnp.zeros((rows, channels), jnp.float32)
        for j in range(3):
            moved = gated[b, 6 + j : 6 + j + rows, :]
            conv = conv + jnp.where(place >= 2 - j, moved, 0.0) * taps[2 + j : 3 + j, :]
        total_a[b, :, 3 * channels : 4 * channels] = conv
        mixed[b] = (total_a[b, :, channels : 2 * channels] * conv).astype(jnp.bfloat16)
        return carry

    lax.fori_loop(0, 4, convolve, 0)

    def branch(i, carry):
        t, q = lax.div(i, planes // 2), lax.rem(i, planes // 2)
        left = mixed[pair(t)].reshape(2 * rows, channels)
        out = times_transposed(left, two_planes(0, q, channels, 2 * channels))
        out = out.reshape(2, rows, 2 * wide).astype(jnp.bfloat16)
        sent_a[pair(t), :, two_columns(q)] = out
        return carry

    lax.fori_loop(0, planes, branch, 0)
    part_start(sent_a, got_a, 0)
    gather_done(0)
    gather_done(1)
    keep_weights = pltpu.make_async_copy(w.at[pl.ds(0, 2)], kept_weights, keep_sem.at[1])
    keep_mixer = pltpu.make_async_copy(total_a, kept_mixer, keep_sem.at[2])
    keep_weights.start()
    keep_mixer.start()
    pass_on(2, 1)
    part_pass(sent_a, got_a, 0)
    for k in range(4, chunks):
        own_at_end(k)
    own_between(4)
    for t in range(2, planes):
        pass_on(2, t)
    own_between(5)
    keep_weights.wait()
    keep_mixer.wait()
    total_a[...] = jnp.zeros_like(total_a)
    total_b[...] = jnp.zeros_like(total_b)
    all_wait(e_all, 1)
    transposed(e_all, 1)
    part_wait(sent_a, got_a, 0)

    def second_norm(span):
        hidden = tokens[span, :].astype(jnp.float32) + summed(sent_a, got_a, span)
        hidden_one[span, :] = hidden
        n_two[at.block, span, :] = (hidden * scale_of(hidden) * gains[1:2, :]).astype(jnp.bfloat16)

    by_rows(second_norm)
    all_start(n_two, 2)
    part_done(sent_a, got_a, 0)
    pass_on(3, 1)
    all_pass(n_two, 2)
    for t in range(2, planes):
        pass_on(3, t)
    pass_on(4, 1)
    take_last(2)
    near_wait(n_two, 2)

    def cast(source, target):
        def run(b, carry):
            target[b] = source[b].astype(jnp.bfloat16)
            return carry

        lax.fori_loop(0, 4, run, 0)

    def feed_forward(k):
        def half(j, carry):
            t = lax.rem(at.x + j, 2)

            @pl.when(jnp.logical_and(k == 2, j == 1))
            def _():
                far_wait(n_two, 2)

            normed = n_two[pair(t)].reshape(2 * rows, width)
            both = dot(normed, whole(k, 0, 2 * step_cols))
            d_active = dot(
                e_all[pair(t)].reshape(2 * rows, width), whole(k, 2 * step_cols, 3 * step_cols)
            )
            gate, upper = both[:, :step_cols], both[:, step_cols:]
            sigma = jax.nn.sigmoid(gate)
            soft = gate * sigma
            here = pl.ds(pl.multiple_of(t * 2 * rows, 2 * rows), 2 * rows)
            active[here, :] = (soft * upper).astype(jnp.bfloat16)
            d_gate_up[here, step_cols:] = (d_active * soft).astype(jnp.bfloat16)
            d_gate_up[here, :step_cols] = (
                d_active * upper * sigma * (1.0 + gate * (1.0 - sigma))
            ).astype(jnp.bfloat16)

            def spread(q, inner):
                back = times_transposed(d_gate_up[here, :], two_planes(k, q, 0, 2 * step_cols))
                total_b[pair(t), :, two_columns(q)] += back.reshape(2, rows, 2 * wide)
                out = times_transposed(
                    active[here, :], two_planes(k, q, 2 * step_cols, 3 * step_cols)
                )
                total_a[pair(t), :, two_columns(q)] += out.reshape(2, rows, 2 * wide)
                return inner

            lax.fori_loop(0, planes // 2, spread, 0)
            return carry

        lax.fori_loop(0, 2, half, 0)

        @pl.when(k == chunks - 1)
        def _():
            cast(total_b, sent_a)
            part_start(sent_a, got_a, 2)

        gather_done(k)
        pl.when(k == 2)(lambda: transposed(n_two, 0))

        def grads(n, carry):
            span = pl.ds(pl.multiple_of(n * step_cols, step_cols), step_cols)
            weight_grad(0, d_gate_up[:, span], k, span)
            return carry

        lax.fori_loop(0, 2, grads, 0)
        weight_grad(1, active[...], k, pl.ds(2 * step_cols, step_cols))

    def one_part(i, carry):
        k = i + 2
        core_wait(k)
        feed_forward(k)
        core_start(i)
        pl.when(k + 2 < chunks)(lambda: pass_on(k + 2, 2))
        pl.when(k + 3 < chunks)(lambda: pass_on(k + 3, 1))
        pl.when(i == 0)(lambda: own_between(6))
        pl.when(i == 0)(lambda: own_between(7))
        pl.when(i == 1)(lambda: own_between(8))
        pl.when(k + 1 < chunks)(lambda: take_last(k + 1))
        first_hop(i)
        now = jnp.logical_and(i >= 3, i < parts - 1)
        pl.when(jnp.logical_and(between, now))(lambda: tick(i - 2))

        @pl.when(k + 1 < chunks)
        def _():
            for t in range(3, planes):
                pass_on(k + 1, t)

        return carry

    lax.fori_loop(0, parts, one_part, 0)

    restore_weights = pltpu.make_async_copy(kept_weights, w.at[pl.ds(0, 2)], keep_sem.at[1])
    restore_weights.start()

    cast(total_a, sent_b)
    restore_mixer = pltpu.make_async_copy(kept_mixer, total_a, keep_sem.at[2])
    restore_mixer.start()
    part_pass(sent_a, got_a, 2)
    pl.when(jnp.logical_not(between))(lambda: tick(3))
    tick(4)
    part_wait(sent_a, got_a, 2)

    def through_second(span):
        grad = back_through_norm(
            summed(sent_a, got_a, span), hidden_one[span, :], gains[1:2, :], 1
        )
        grad = e_all[at.block, span, :].astype(jnp.float32) + grad
        d_hidden[span, :] = grad
        f_all[at.block, span, :] = grad.astype(jnp.bfloat16)

    by_rows(through_second)
    all_done(n_two, 2)
    all_start(f_all, 3)
    part_done(sent_a, got_a, 2)
    all_pass(f_all, 3)
    part_start(sent_b, n_two, 1)
    sum_done(0)
    transposed(n_one, 2)
    all_done(n_one, 0)
    restore_weights.wait()
    restore_mixer.wait()
    tick(5)
    all_wait(f_all, 3)

    def into_mixer(t, carry):
        grad = f_all[pair(t)].reshape(2 * rows, width)
        d_mixed = dot(grad, whole(0, channels, 2 * channels)).reshape(2, rows, channels)
        conv = total_a[pair(t), :, 3 * channels : 4 * channels]
        c_part = total_a[pair(t), :, channels : 2 * channels]
        n_one[pair(t), :, 2 * channels : 3 * channels] = (d_mixed * conv).astype(jnp.bfloat16)
        d_conv[pair(t), 0:rows, :] = d_mixed * c_part
        return carry

    lax.fori_loop(0, 2, into_mixer, 0)
    head = d_conv.at[:, pl.ds(0, 8), :]
    halo_core(1, head).start()
    pl.when(at.gives_last)(lambda: halo_plane(1, head, at.last).start())

    def from_c(i, carry):
        t, q = lax.div(i, planes // 2), lax.rem(i, planes // 2)
        grad = n_one[pair(t), :, 2 * channels : 3 * channels].reshape(2 * rows, channels)
        out = times_transposed(grad, two_planes(0, q, 0, channels))
        total_b[pair(t), :, two_columns(q)] = out.reshape(2, rows, 2 * wide)
        return carry

    lax.fori_loop(0, planes, from_c, 0)
    sum_done(1)
    transposed(f_all, 3)

    d_c = n_one[:, :, 2 * channels : 3 * channels].reshape(4 * rows, channels)
    weight_grad(2, d_c, 0, pl.ds(0, channels))
    weight_grad(3, mixed[...].reshape(4 * rows, channels), 0, pl.ds(channels, channels))
    core_start(jnp.int32(parts))
    tick(6)
    halo_core(1, head).wait_recv()
    pl.when(at.gives_next)(lambda: halo_plane(1, head, at.next).wait_recv())
    for group in range(2):

        @pl.when(at.is_first)
        def _():
            d_conv[2 * group, rows : rows + 8, :] = halo[2, 2 * group]
            d_conv[2 * group + 1, rows : rows + 8, :] = halo[2, 2 * group + 1]

        @pl.when(at.is_last)
        def _():
            d_conv[2 * group, rows : rows + 8, :] = halo[2, 2 * group + 1]
            d_conv[2 * group + 1, rows : rows + 8, :] = halo[3, 2 * group]

    def convolve_back(b, carry):
        place = place_in(b, 0)
        d_gated = jnp.zeros((rows, channels), jnp.float32)
        for j in range(3):
            ahead = 2 - j
            moved = jnp.where(
                place_in(b, ahead) >= ahead, d_conv[b, ahead : ahead + rows, :], 0.0
            )
            d_gated = d_gated + moved * taps[2 + j : 3 + j, :]
            product = d_conv[b, 0:rows, :] * gated[b, 6 + j : 6 + j + rows, :]
            small[2 + j : 3 + j, channel_columns] += jnp.sum(
                jnp.where(place >= ahead, product, 0.0), axis=0, keepdims=True
            )
        x_part = total_a[b, :, 2 * channels : 3 * channels]
        n_one[b, :, 0:channels] = (d_gated * x_part).astype(jnp.bfloat16)
        b_part = total_a[b, :, 0:channels]
        n_one[b, :, channels : 2 * channels] = (d_gated * b_part).astype(jnp.bfloat16)
        return carry

    lax.fori_loop(0, 4, convolve_back, 0)
    first_hop(jnp.int32(parts))

    def d_normed(i, carry):
        t, q = lax.div(i, planes // 2), lax.rem(i, planes // 2)
        grad = n_one[pair(t), :, 0 : 2 * channels].reshape(2 * rows, 2 * channels)
        out = times_transposed(grad, two_planes(1, q, 0, 2 * channels))
        out = total_b[pair(t), :, two_columns(q)] + out.reshape(2, rows, 2 * wide)
        sent_a[pair(t), :, two_columns(q)] = out.astype(jnp.bfloat16)
        return carry

    lax.fori_loop(0, planes, d_normed, 0)
    part_start(sent_a, got_a, 3)

    def b_and_x_weight(n, carry):
        span = pl.ds(pl.multiple_of(n * channels, channels), channels)
        grad = n_one[:, :, span].reshape(4 * rows, channels)
        weight_grad(2, grad, 1, span)
        return carry

    lax.fori_loop(0, 2, b_and_x_weight, 0)
    core_start(jnp.int32(parts + 1))
    tick(7)
    part_pass(sent_a, got_a, 3)
    first_hop(jnp.int32(parts + 1))
    part_pass(sent_b, n_two, 1)
    tick(8)
    last_passes(9)
    part_wait(sent_a, got_a, 3)

    def through_first(span):
        hidden = tokens[span, :].astype(jnp.float32)
        grad = back_through_norm(summed(sent_a, got_a, span), hidden, gains[0:1, :], 0)
        sent_a[at.block, span, :] = (d_hidden[span, :] + grad).astype(jnp.bfloat16)

    by_rows(through_first)
    d_tokens_copy = pltpu.make_async_copy(sent_a.at[at.block], d_tokens, keep_sem.at[3])
    d_tokens_copy.start()

    def small_copy(i, to):
        return remote(small, small_in.at[i], small_send.at[i], small_recv.at[i], to)

    def small_plane(t):
        to = lax.rem(at.me + 4 * t, count)
        return remote(
            small, small_in.at[2 + t], small_send.at[2 + t], small_recv.at[2 + t], (to, at.x)
        )

    small_copy(0, at.core).start()
    for i, (here, following) in enumerate(
        ((at.core, at.beside), (at.beside, at.across), (at.across, None))
    ):
        small_copy(i, here).wait()
        small[...] += small_in[i]
        if following is not None:
            small_copy(i + 1, following).start()
    for t in range(1, planes):
        small_plane(t).start()
    last_ticks(9)
    part_wait(sent_b, n_two, 1)

    def last_out(span):
        total = hidden_one[span, :] + summed(sent_b, n_two, span)
        sent_b[at.block, span, :] = total.astype(jnp.bfloat16)

    by_rows(last_out)
    result_copy = pltpu.make_async_copy(sent_b.at[at.block], result, keep_sem.at[4])
    result_copy.start()
    for t in range(1, planes):
        small_plane(t).wait()
    for t in range(1, planes):
        small[...] += small_in[2 + t]

    d_tokens_copy.wait()
    result_copy.wait()
    part_done(sent_a, got_a, 3)
    all_done(e_all, 1)
    part_done(sent_b, n_two, 1)
    all_done(f_all, 3)
    halo_core(0, tail).wait_send()
    halo_core(1, head).wait_send()
    pl.when(at.gives_next)(lambda: halo_plane(0, tail, at.next).wait_send())
    pl.when(at.gives_last)(lambda: halo_plane(1, head, at.last).wait_send())
    for v in range(2, chunks):
        sum_done(v)


def one_kernel(planes, seq_len, weights, tokens, d_out, gains):
    chunks, _, share, cols = weights.shape
    parts = chunks - 2
    rows, width = tokens.shape
    channels = width // 4
    low, full = jnp.bfloat16, jnp.float32
    shape = jax.ShapeDtypeStruct
    vmem, anywhere = pl.BlockSpec(memory_space=pltpu.VMEM), pl.BlockSpec(memory_space=pl.ANY)
    dma = pltpu.SemaphoreType.DMA
    block = (4, rows, width)
    return pl.pallas_call(
        functools.partial(kernel, planes, parts, seq_len),
        out_shape=(
            shape((rows, width), low),
            shape((rows, width), low),
            shape((chunks, share, cols), low),
            shape((chunks, share, cols), low),
            shape((8, width), full),
            shape((2, planes, 2, 2, share, cols), low),
            shape(block, full),
        ),
        in_specs=[anywhere, vmem, anywhere, vmem],
        out_specs=[anywhere, anywhere, anywhere, anywhere, vmem, anywhere, anywhere],
        scratch_shapes=[
            pltpu.VMEM((chunks, planes, 2, 2, share, cols), low),
            pltpu.VMEM((2, planes, 2, share, cols), low),
            pltpu.VMEM((chunks, 2, share, cols), low),
            pltpu.VMEM(block, low),
            pltpu.VMEM(block, low),
            pltpu.VMEM(block, low),
            pltpu.VMEM(block, low),
            pltpu.VMEM(block, low),
            pltpu.VMEM(block, low),
            pltpu.VMEM(block, full),
            pltpu.VMEM(block, full),
            pltpu.VMEM((3, rows, width), low),
            pltpu.VMEM((4, rows + 8, channels), full),
            pltpu.VMEM((4, rows + 8, channels), full),
            pltpu.VMEM((4, rows, channels), low),
            pltpu.VMEM((4 * rows, PART), low),
            pltpu.VMEM((4 * rows, 2 * PART), low),
            pltpu.VMEM((rows, width), full),
            pltpu.VMEM((rows, width), full),
            pltpu.VMEM((4, 4, 8, channels), full),
            pltpu.VMEM((4 * planes,) + gains.shape, low),
            pltpu.VMEM((8, width), full),
            pltpu.VMEM((8, channels), full),
            pltpu.VMEM((2 + planes, 8, width), full),
            dma((4 * planes,)),
            dma((4 * planes,)),
            dma((2 + planes,)),
            dma((2 + planes,)),
            dma((chunks,)),
            dma((chunks,)),
            dma((chunks,)),
            dma((chunks, 2, planes)),
            dma((chunks, planes)),
            dma((chunks, planes)),
            dma((chunks, planes)),
            dma((chunks,)),
            dma((chunks,)),
            pltpu.SemaphoreType.REGULAR,
            dma((chunks, 2, planes)),
            dma((chunks, 2, planes)),
            pltpu.SemaphoreType.REGULAR((2,)),
            dma((chunks,)),
            dma((chunks,)),
            dma((chunks,)),
            dma((4, 6)),
            dma((4, 6)),
            dma((4, 6)),
            dma((4, 6)),
            dma((4,)),
            dma((4,)),
            dma((5,)),
        ],
        compiler_params=pltpu.CompilerParams(
            collective_id=0, has_side_effects=True, vmem_limit_bytes=64 * 1024 * 1024
        ),
    )(weights, tokens, d_out, gains)


def split_kernel(hidden, parts, gate, up, down, in_weight, out_weight, weights):
    channels = out_weight.shape[1] // 2
    left = parts * PART - hidden
    blank = jnp.zeros((gate.shape[0], left), jnp.bfloat16)
    for which, source in enumerate((gate, up, down)):
        here = pl.ds(which * PART, PART)
        for half in range(2):
            for part in range(parts):
                low = half * hidden + part * PART
                if part < parts - 1 or left == 0:
                    weights[2 + part, half, :, here] = source[:, low : low + PART]
                else:
                    last = source[:, low : low + PART - left]
                    weights[2 + part, half, :, here] = jnp.concatenate([last, blank], axis=1)
    for half in range(2):
        span = slice(half * channels, (half + 1) * channels)
        weights[0, half, :, 0:channels] = in_weight[1, :, span]
        weights[0, half, :, channels:] = out_weight[:, span]
        weights[1, half, :, 0:channels] = in_weight[0, :, span]
        weights[1, half, :, channels:] = in_weight[2, :, span]


def split(gate, up, down, in_weight, out_weight, step=32):
    share, columns = gate.shape
    hidden = columns // 2
    parts = -(-hidden // PART)
    by_rows = pl.BlockSpec((step, columns), lambda i: (i, 0))
    cols = 3 * PART
    return pl.pallas_call(
        functools.partial(split_kernel, hidden, parts),
        grid=(share // step,),
        out_shape=jax.ShapeDtypeStruct((parts + 2, 2, share, cols), jnp.bfloat16),
        in_specs=[
            by_rows,
            by_rows,
            by_rows,
            pl.BlockSpec((3, step, in_weight.shape[2]), lambda i: (0, i, 0)),
            pl.BlockSpec((step, out_weight.shape[1]), lambda i: (i, 0)),
        ],
        out_specs=pl.BlockSpec((parts + 2, 2, step, cols), lambda i: (0, 0, i, 0)),
    )(gate, up, down, in_weight, out_weight)


def join_kernel(hidden, parts, own, other, gate, up, down, in_weight, out_weight):
    channels = out_weight.shape[1] // 2
    side = lax.rem(lax.div(lax.axis_index("seq"), 2), 2)

    def put(half, source):
        for which, target in enumerate((gate, up, down)):
            pieces = [
                source[2 + part, :, which * PART : (which + 1) * PART].astype(jnp.float32)
                for part in range(parts)
            ]
            whole = jnp.concatenate(pieces, axis=1)[:, :hidden]
            target[:, half * hidden : (half + 1) * hidden] = whole
        span = slice(half * channels, (half + 1) * channels)
        in_weight[1, :, span] = source[0, :, 0:channels].astype(jnp.float32)
        out_weight[:, span] = source[0, :, channels:].astype(jnp.float32)
        in_weight[0, :, span] = source[1, :, 0:channels].astype(jnp.float32)
        in_weight[2, :, span] = source[1, :, channels:].astype(jnp.float32)

    @pl.when(side == 0)
    def _():
        put(0, own)
        put(1, other)

    @pl.when(side == 1)
    def _():
        put(0, other)
        put(1, own)


def join(own, other, hidden, channels, step=32):
    chunks, share, cols = own.shape
    parts = chunks - 2
    full = jnp.float32
    part = pl.BlockSpec((chunks, step, cols), lambda i: (0, i, 0))
    by_rows = pl.BlockSpec((step, 2 * hidden), lambda i: (i, 0))
    shape = jax.ShapeDtypeStruct
    return pl.pallas_call(
        functools.partial(join_kernel, hidden, parts),
        grid=(share // step,),
        out_shape=(
            shape((share, 2 * hidden), full),
            shape((share, 2 * hidden), full),
            shape((share, 2 * hidden), full),
            shape((3, share, 2 * channels), full),
            shape((share, 2 * channels), full),
        ),
        in_specs=[part, part],
        out_specs=(
            by_rows,
            by_rows,
            by_rows,
            pl.BlockSpec((3, step, 2 * channels), lambda i: (0, i, 0)),
            pl.BlockSpec((step, 2 * channels), lambda i: (i, 0)),
        ),
    )(own, other)


def on_device(
    tokens,
    norm1_gain,
    in_weight,
    conv_kernel,
    out_weight,
    norm2_gain,
    gate_weight,
    up_weight,
    down_weight,
    d_out,
):
    planes = lax.axis_size("seq") // 4
    here = lax.axis_index("seq")
    rows, width = tokens.shape[1:]
    share = gate_weight.shape[0]
    channels = in_weight.shape[2] // 2
    hidden = gate_weight.shape[1] // 2

    gains = jnp.concatenate([norm1_gain[None], norm2_gain[None], conv_kernel.T], axis=0)
    gains = jnp.pad(gains, ((0, 16 - gains.shape[0]), (0, 128 - share)))

    weights = split(
        gate_weight, up_weight, down_weight, jnp.swapaxes(in_weight, 0, 1), out_weight
    )
    result, d_tokens, own_grad, other_grad, small, _, _ = one_kernel(
        planes,
        lax.axis_size("seq") * rows // SEQS,
        weights,
        tokens[0],
        d_out[0],
        gains,
    )
    d_gate, d_up, d_down, d_in, d_branch = join(own_grad, other_grad, hidden, channels)
    sums = lax.dynamic_slice_in_dim(small, here * share, share, 1)
    return (
        result[None],
        d_tokens[None],
        sums[0],
        jnp.swapaxes(d_in, 0, 1),
        sums[2:5].T,
        d_branch,
        sums[1],
        d_gate,
        d_up,
        d_down,
    )


def fits(mesh):
    return mesh.shape["seq"] <= 16


def solution(mesh):
    return jax.shard_map(
        on_device if fits(mesh) else plain_on_device,
        mesh=mesh,
        in_specs=(
            P("fsdp", "seq", None),
            P("seq"),
            P("seq", None, "fsdp"),
            P("seq", None),
            P("seq", "fsdp"),
            P("seq"),
            P("seq", "fsdp"),
            P("seq", "fsdp"),
            P("seq", "fsdp"),
            P("fsdp", "seq", None),
        ),
        out_specs=(
            P("fsdp", "seq", None),
            P("fsdp", "seq", None),
            P("seq"),
            P("seq", None, "fsdp"),
            P("seq", None),
            P("seq", "fsdp"),
            P("seq"),
            P("seq", "fsdp"),
            P("seq", "fsdp"),
            P("seq", "fsdp"),
        ),
        check_vma=False,
    )
```

```python
import functools

import jax
import jax.numpy as jnp
from jax import lax
from jax.experimental import pallas as pl
from jax.experimental.pallas import tpu as pltpu
from jax.sharding import PartitionSpec as P

SEQS = 3
EPSILON = 1e-05
BOTH = ("seq", "fsdp")
MESH = pl.DeviceIdType.MESH
PART = 256


def times_transposed(left, right):
    return lax.dot_general(
        left, right, (((1,), (1,)), ((), ())), preferred_element_type=jnp.float32
    )


def transposed_times(left, right):
    return lax.dot_general(
        left, right, (((0,), (0,)), ((), ())), preferred_element_type=jnp.float32
    )


def times(left, right):
    return jnp.dot(left, right, preferred_element_type=jnp.float32)


def root_norm(hidden, gain):
    scale = lax.rsqrt(jnp.mean(hidden * hidden, axis=-1, keepdims=True) + EPSILON)
    return (hidden * scale * gain, scale)


def norm_back(grad, hidden, scale, gain):
    weighted = grad * gain
    inner = jnp.sum(weighted * hidden, axis=-1, keepdims=True)
    d_hidden = scale * weighted - hidden * (scale * scale * scale) * inner / hidden.shape[-1]
    d_gain = jnp.sum(grad * hidden * scale, axis=0)
    return (d_hidden, d_gain)


def device(z, y, c, x):
    return (z * 4 + y * 2 + c) * 2 + x


def every(planes):
    return [
        (z, y, c, x) for z in range(planes) for y in range(2) for c in range(2) for x in range(2)
    ]


def plain_on_device(
    tokens,
    norm1_gain,
    in_weight,
    conv_kernel,
    out_weight,
    norm2_gain,
    gate_weight,
    up_weight,
    down_weight,
    d_out,
):
    planes = lax.axis_size("seq") // 4
    here = lax.axis_index("seq")
    y, c, x = (here // 2) % 2, here % 2, lax.axis_index("fsdp")
    z = here // 4
    rows, width = tokens.shape[1:]
    share = gate_weight.shape[0]
    plane_groups = [
        [device(z, y, c, x) for x in range(2) for y in range(2)]
        for z in range(planes)
        for c in range(2)
    ]
    column_groups = [
        [z * 4 + y * 2 + c for z in range(planes) for c in range(2)] for y in range(2)
    ]
    members = 2 * planes

    def moved(value, target):
        pairs = []
        for place in every(planes):
            to = target(*place)
            if to is not None:
                pairs.append((device(*place), device(*to)))
        return lax.ppermute(value, BOTH, pairs)

    def swap_y(value):
        return moved(value, lambda z, y, c, x: (z, 1 - y, c, x))

    def swap_x(value):
        return moved(value, lambda z, y, c, x: (z, y, c, 1 - x))

    def swap_both(value):
        return moved(value, lambda z, y, c, x: (z, 1 - y, c, 1 - x))

    def ordered(first, second, flag):
        return jnp.where(flag == 0, jnp.stack([first, second]), jnp.stack([second, first]))

    def plane_gather(value):
        by_y = ordered(value, swap_y(value), y)
        other = ordered(swap_x(value), swap_both(value), y)
        return ordered(by_y, other, x).reshape((4 * value.shape[0],) + value.shape[1:])

    def plane_sum(partial):
        sent = partial.astype(jnp.bfloat16).reshape(4, rows, width)
        got = lax.all_to_all(sent, BOTH, 0, 0, axis_index_groups=plane_groups, tiled=True)
        return jnp.sum(got.astype(jnp.float32), axis=0)

    def fetch(weight):
        halves = weight.reshape(share, 2, -1)
        mine = jnp.where(y == 0, halves[:, 0], halves[:, 1])
        theirs = jnp.where(y == 0, halves[:, 1], halves[:, 0])
        pair = ordered(mine, swap_y(theirs), y)
        got = lax.all_gather(pair, "seq", axis=0, tiled=False, axis_index_groups=column_groups)
        got = got.reshape(planes, 2, 2, share, -1)
        return jnp.swapaxes(got, 1, 2).reshape(width, -1)

    def give(grad):
        sent = grad.astype(jnp.bfloat16).reshape(planes, 2, 2, share, -1)
        sent = jnp.swapaxes(sent, 1, 2).reshape(members * 2, share, -1)
        got = lax.psum_scatter(
            sent, "seq", scatter_dimension=0, tiled=True, axis_index_groups=column_groups
        )
        mine = jnp.where(y == 0, got[0], got[1])
        theirs = jnp.where(y == 0, got[1], got[0])
        pair = ordered(mine, swap_y(theirs), y).astype(jnp.float32)
        return jnp.concatenate([pair[0], pair[1]], axis=1)

    gains = lax.all_gather(
        jnp.concatenate(
            [norm1_gain[:, None], norm2_gain[:, None], conv_kernel], axis=1
        ),
        "seq",
        axis=0,
        tiled=True,
    ).astype(jnp.float32)
    gain_one, gain_two, kernel = gains[:, 0], gains[:, 1], gains[:, 2:]
    taps = kernel.shape[1]
    margin = taps - 1
    channels = in_weight.shape[2] // 2
    first_channel = x * (2 * channels) + y * channels
    kernel_here = lax.dynamic_slice_in_dim(kernel, first_channel, channels, 0)

    w_in_halves = jnp.swapaxes(in_weight.reshape(share, 3, 2, channels), 1, 2)
    w_mixer = fetch(
        jnp.concatenate(
            [w_in_halves.reshape(share, 2, 3 * channels), out_weight.reshape(share, 2, channels)],
            axis=2,
        ).reshape(share, 8 * channels)
    )
    w_in, w_out = w_mixer[:, : 3 * channels], w_mixer[:, 3 * channels :]

    hidden = tokens[0].astype(jnp.float32)
    normed, scale_one = root_norm(hidden, gain_one)
    normed_low = plane_gather(normed.astype(jnp.bfloat16))
    grad_low = plane_gather(d_out[0])

    w_gate = fetch(gate_weight)
    w_up = fetch(up_weight)
    w_down = fetch(down_weight)

    projected = times(normed_low, w_in).reshape(2, 2, rows, 3 * channels)
    b_part = projected[..., :channels]
    c_part = projected[..., channels : 2 * channels]
    x_part = projected[..., 2 * channels :]
    gated = (b_part * x_part).astype(jnp.bfloat16)

    def swap_core(value):
        return moved(value, lambda z, y, c, x: (z, y, 1 - c, x))

    def to_next(value):
        return moved(
            value, lambda z, y, c, x: (z + 1, y, 0, x) if c == 1 and z + 1 < planes else None
        )

    def to_last(value):
        return moved(value, lambda z, y, c, x: (z - 1, y, 1, x) if c == 0 and z > 0 else None)

    tail = gated[:, :, rows - margin :]
    from_core, from_plane = swap_core(tail), to_next(tail[:, 1])
    before = jnp.where(
        c == 1, from_core, jnp.stack([from_plane, from_core[:, 0]], axis=1)
    )
    padded = jnp.concatenate([before, gated], axis=2).astype(jnp.float32)
    seq_len = lax.axis_size("seq") * rows // SEQS
    block = z * 4 + jnp.arange(2, dtype=jnp.int32) * 2 + c
    position = block[:, None] * rows + jnp.arange(rows, dtype=jnp.int32)
    in_sequence = position % seq_len
    masks = [
        (in_sequence >= margin - offset).astype(jnp.float32)[None, :, :, None]
        for offset in range(taps)
    ]
    conv = jnp.zeros_like(b_part)
    for offset in range(taps):
        conv = conv + masks[offset] * padded[:, :, offset : offset + rows] * kernel_here[:, offset]
    mixed = (c_part * conv).astype(jnp.bfloat16).reshape(4 * rows, channels)
    hidden_one = hidden + plane_sum(times_transposed(mixed, w_out))

    normed_two, scale_two = root_norm(hidden_one, gain_two)
    normed_two_low = plane_gather(normed_two.astype(jnp.bfloat16))
    gate = times(normed_two_low, w_gate)
    upper = times(normed_two_low, w_up)
    sigma = jax.nn.sigmoid(gate)
    active = (gate * sigma * upper).astype(jnp.bfloat16)
    d_active = times(grad_low, w_down)
    d_upper = (d_active * gate * sigma).astype(jnp.bfloat16)
    d_gate = (d_active * upper * sigma * (1.0 + gate * (1.0 - sigma))).astype(jnp.bfloat16)
    d_normed_two = plane_sum(times_transposed(d_gate, w_gate) + times_transposed(d_upper, w_up))
    result = hidden_one + plane_sum(times_transposed(active, w_down))
    d_gate_w = give(transposed_times(normed_two_low, d_gate))
    d_up_w = give(transposed_times(normed_two_low, d_upper))
    d_down_w = give(transposed_times(grad_low, active))

    d_hidden_two, d_gain_two = norm_back(d_normed_two, hidden_one, scale_two, gain_two)
    grad_one = d_out[0].astype(jnp.float32) + d_hidden_two
    grad_one_low = plane_gather(grad_one.astype(jnp.bfloat16))
    d_out_w = transposed_times(grad_one_low, mixed)
    d_mixed = times(grad_one_low, w_out).reshape(2, 2, rows, channels)
    d_c = d_mixed * conv
    d_conv = d_mixed * c_part
    kernel_cols = []
    d_padded = jnp.zeros((2, 2, rows + margin, channels), jnp.float32)
    for offset in range(taps):
        masked = masks[offset] * d_conv
        kernel_cols.append(jnp.sum(masked * padded[:, :, offset : offset + rows], axis=(0, 1, 2)))
        d_padded = d_padded + jnp.pad(
            masked * kernel_here[:, offset],
            ((0, 0), (0, 0), (offset, margin - offset), (0, 0)),
        )
    head = d_padded[:, :, :margin]
    from_core, from_plane = swap_core(head), to_last(head[:, 0])
    after = jnp.where(c == 0, from_core, jnp.stack([from_core[:, 1], from_plane], axis=1))
    d_gated = d_padded[:, :, margin:] + jnp.pad(
        after, ((0, 0), (0, 0), (rows - margin, 0), (0, 0))
    )
    d_projected = (
        jnp.concatenate([d_gated * x_part, d_c, d_gated * b_part], axis=3)
        .astype(jnp.bfloat16)
        .reshape(4 * rows, 3 * channels)
    )
    d_in_w = transposed_times(normed_low, d_projected)
    d_normed = plane_sum(times_transposed(d_projected, w_in))
    d_mixer = give(jnp.concatenate([d_in_w, d_out_w], axis=1)).reshape(share, 2, 4 * channels)
    d_in_w = jnp.swapaxes(d_mixer[:, :, : 3 * channels].reshape(share, 2, 3, channels), 1, 2)
    d_in_w = d_in_w.reshape(share, 3, 2 * channels)
    d_out_w = d_mixer[:, :, 3 * channels :].reshape(share, 2 * channels)
    d_hidden, d_gain_one = norm_back(d_normed, hidden, scale_one, gain_one)
    d_tokens = (grad_one + d_hidden).astype(jnp.bfloat16)

    d_kernel = lax.dynamic_update_slice(
        jnp.zeros((width, taps), jnp.float32), jnp.stack(kernel_cols, axis=1), (first_channel, 0)
    )
    small = jnp.concatenate([d_gain_one[:, None], d_gain_two[:, None], d_kernel], axis=1)
    small = lax.psum(small, BOTH)
    small = lax.dynamic_slice_in_dim(small, here * share, share, 0)
    return (
        result.astype(jnp.bfloat16)[None],
        d_tokens[None],
        small[:, 0],
        d_in_w,
        small[:, 2:],
        d_out_w,
        small[:, 1],
        d_gate_w,
        d_up_w,
        d_down_w,
    )


class Place:
    def __init__(self, planes):
        self.planes = planes
        self.me, self.x = lax.axis_index("seq"), lax.axis_index("fsdp")
        self.z = lax.div(self.me, 4)
        self.y = lax.rem(lax.div(self.me, 2), 2)
        self.c = lax.rem(self.me, 2)
        self.core = (self.me + 1 - 2 * self.c, self.x)
        self.across = (self.me + 2 - 4 * self.y, self.x)
        self.low, self.high = (self.me - 4, self.x), (self.me + 4, self.x)
        self.has_low, self.has_high = self.z > 0, self.z < planes - 1
        self.block = self.x * 2 + self.y
        self.beside = (self.me, 1 - self.x)
        self.beside_block = (1 - self.x) * 2 + self.y
        self.across_block = self.x * 2 + 1 - self.y
        self.far_block = (1 - self.x) * 2 + 1 - self.y
        self.is_first, self.is_last = self.c == 0, self.c == 1
        self.gives_next = jnp.logical_and(self.is_last, self.has_high)
        self.gives_last = jnp.logical_and(self.is_first, self.has_low)
        self.next, self.last = (self.me + 3, self.x), (self.me - 3, self.x)


def remote(source, target, send, receive, device_id):
    return pltpu.make_async_remote_copy(
        src_ref=source,
        dst_ref=target,
        send_sem=send,
        recv_sem=receive,
        device_id=device_id,
        device_id_type=MESH,
    )


def signal(semaphore, device_id):
    pl.semaphore_signal(semaphore, inc=1, device_id=device_id, device_id_type=MESH)


def dot(left, right):
    return jnp.dot(left, right, preferred_element_type=jnp.float32)


def kernel(
    planes,
    parts,
    seq_len,
    weights,
    tokens,
    d_out,
    gains_here,
    result,
    d_tokens,
    own_grad,
    other_grad,
    small,
    kept_weights,
    kept_mixer,
    w,
    core_in,
    extra,
    n_one,
    f_all,
    n_two,
    e_all,
    sent_a,
    sent_b,
    total_a,
    total_b,
    got_a,
    gated,
    d_conv,
    mixed,
    active,
    d_gate_up,
    hidden_one,
    d_hidden,
    halo,
    gains_in,
    gains,
    taps,
    small_in,
    gain_send,
    gain_recv,
    small_send,
    small_recv,
    local_sem,
    y_send,
    y_recv,
    z_send,
    z_recv,
    c_send,
    c_recv,
    core_send,
    core_recv,
    core_free,
    sum_send,
    sum_recv,
    ready,
    last_send,
    last_recv,
    own_sem,
    all_send,
    all_recv,
    part_send,
    part_recv,
    halo_send,
    halo_recv,
    keep_sem,
):
    at = Place(planes)
    z, y, c = at.z, at.y, at.c
    rows, width = tokens.shape
    channels = taps.shape[1]
    count = 4 * planes
    share = weights.shape[2]
    wide = 4 * share
    chunks = parts + 2
    step_cols = weights.shape[3] // 3

    def y_copies(k):
        return (
            pltpu.make_async_copy(weights.at[k, y], w.at[k, z, y, c], local_sem.at[k]),
            remote(weights.at[k, 1 - y], w.at[k, z, y, c], y_send.at[k], y_recv.at[k], at.across),
        )

    def piece(k, p):
        return w.at[k, p, :, c]

    def to_side(k, p, side):
        return remote(
            piece(k, p),
            piece(k, p),
            z_send.at[k, side, p],
            z_recv.at[k, p],
            at.high if side else at.low,
        )

    def to_core(k, p):
        return remote(piece(k, p), piece(k, p), c_send.at[k, p], c_recv.at[k, p], at.core)

    def begin(k):
        for copy in y_copies(k):
            copy.start()

    def own(k):
        y_copies(k)[0].wait()
        remote(
            weights.at[k, y], w.at[k, z, 1 - y, c], y_send.at[k], y_recv.at[k], at.across
        ).wait_recv()
        pl.when(at.has_low)(lambda: to_side(k, z, 0).start())
        pl.when(at.has_high)(lambda: to_side(k, z, 1).start())
        to_core(k, z).start()

    def relay(k, t):
        below, above = z - t, z + t

        @pl.when(below >= 0)
        def _():
            to_side(k, below, 1).wait_recv()
            pl.when(at.has_high)(lambda: to_side(k, below, 1).start())
            to_core(k, below).start()

        @pl.when(above < planes)
        def _():
            to_side(k, above, 0).wait_recv()
            pl.when(at.has_low)(lambda: to_side(k, above, 0).start())
            to_core(k, above).start()

    between = jnp.logical_and(at.has_low, at.has_high)

    def pass_on(k, t):
        pl.when(between)(lambda: relay(k, t))

    def own_between(k):
        pl.when(between)(lambda: own(k))

    def own_at_end(k):
        pl.when(jnp.logical_not(between))(lambda: own(k))

    def take_last(k):
        @pl.when(jnp.logical_not(between))
        def _():
            for t in range(1, planes):
                relay(k, t)

    def core_wait(k):
        for p in range(planes):
            remote(
                w.at[k, p, :, 1 - c], w.at[k, p, :, 1 - c], c_send.at[k, p], c_recv.at[k, p], at.core
            ).wait_recv()

    def gather_done(k):
        y_copies(k)[1].wait_send()
        for p in range(planes):
            pl.when(jnp.logical_and(at.has_low, p >= z))(lambda: to_side(k, p, 0).wait_send())
            pl.when(jnp.logical_and(at.has_high, p <= z))(lambda: to_side(k, p, 1).wait_send())
            to_core(k, p).wait_send()

    def chunk_of(v):
        return lax.rem(v + 2, chunks)

    def core_copy(v):
        k = chunk_of(v)
        return remote(
            w.at[k, :, :, 1 - c],
            core_in.at[lax.rem(v, 2)],
            core_send.at[k],
            core_recv.at[k],
            at.core,
        )

    def core_start(v):
        pl.when(v >= 2)(lambda: pl.semaphore_wait(core_free, 1))
        core_copy(v).start()

    def core_add(v):
        k, slot = chunk_of(v), lax.rem(v, 2)
        core_copy(v).wait()

        def add(p, carry):
            total = w[k, p, :, c].astype(jnp.float32) + core_in[slot, p].astype(jnp.float32)
            w[k, p, :, c] = total.astype(jnp.bfloat16)
            return carry

        lax.fori_loop(0, planes, add, 0)
        pl.when(v < chunks - 2)(lambda: signal(core_free, at.core))
        pl.when(at.has_low)(lambda: signal(ready.at[1], at.low))
        pl.when(at.has_high)(lambda: signal(ready.at[0], at.high))

    def landing(k, d):
        return w.at[k, d, :, 1 - c]

    def sum_up(k, d):
        return remote(
            landing(k, d), landing(k, d), sum_send.at[k, 1, d], sum_recv.at[k, 1, d], at.high
        )

    def sum_down(k, d):
        return remote(
            landing(k, d), landing(k, d), sum_send.at[k, 0, d], sum_recv.at[k, 0, d], at.low
        )

    def sum_down_last(k, d):
        return remote(
            landing(k, d), extra.at[k], sum_send.at[k, 0, d], sum_recv.at[k, 0, d], at.low
        )

    def add_here(k, d, arrived):
        here = w[k, d, :, c].astype(jnp.float32)

        @pl.when(arrived)
        def _():
            w[k, d, :, 1 - c] = (w[k, d, :, 1 - c].astype(jnp.float32) + here).astype(jnp.bfloat16)

        @pl.when(jnp.logical_not(arrived))
        def _():
            w[k, d, :, 1 - c] = w[k, d, :, c]

    def each_plane(body):
        def run(i, carry):
            body(i)
            return carry

        lax.fori_loop(0, planes, run, 0)

    def up_pass(v):
        k = chunk_of(v)
        pl.when(at.has_high)(lambda: pl.semaphore_wait(ready.at[1], 1))

        def one(i):
            d = planes - 1 - i

            @pl.when(d > z)
            def _():
                pl.when(at.has_low)(lambda: sum_up(k, d).wait_recv())
                add_here(k, d, at.has_low)
                sum_up(k, d).start()

        each_plane(one)

    def up_last(v):
        k = chunk_of(v)

        @pl.when(at.has_low)
        def _():
            sum_up(k, z).wait_recv()
            total = w[k, z, :, c].astype(jnp.float32) + w[k, z, :, 1 - c].astype(jnp.float32)
            w[k, z, :, c] = total.astype(jnp.bfloat16)

    def add_up(v):
        up_pass(v)
        up_last(v)

    def down_pass(v):
        k = chunk_of(v)
        pl.when(at.has_low)(lambda: pl.semaphore_wait(ready.at[0], 1))

        def one(d):
            @pl.when(d < z)
            def _():
                pl.when(at.has_high)(lambda: sum_down(k, d).wait_recv())
                add_here(k, d, at.has_high)
                pl.when(z - 1 > d)(lambda: sum_down(k, d).start())
                pl.when(z - 1 == d)(lambda: sum_down_last(k, d).start())

        each_plane(one)

    def down_last(v):
        k = chunk_of(v)

        @pl.when(at.has_high)
        def _():
            sum_down_last(k, z).wait_recv()
            total = w[k, z, :, c].astype(jnp.float32) + extra[k].astype(jnp.float32)
            w[k, z, :, c] = total.astype(jnp.bfloat16)

    def add_down(v):
        down_pass(v)
        down_last(v)

    def give_copies(k):
        return (
            pltpu.make_async_copy(w.at[k, z, y, c], own_grad.at[k], own_sem.at[k]),
            remote(
                w.at[k, z, 1 - y, c], other_grad.at[k], last_send.at[k], last_recv.at[k], at.across
            ),
        )

    def give(v):
        for copy in give_copies(chunk_of(v)):
            copy.start()

    def sum_done(v):
        k = chunk_of(v)
        for d in range(planes):
            pl.when(d > z)(lambda: sum_up(k, d).wait_send())
            pl.when(d < z)(lambda: sum_down(k, d).wait_send())
        for copy in give_copies(k):
            copy.wait()

    def first_hop(v):
        core_add(v)
        pl.when(jnp.logical_not(at.has_low))(lambda: add_up(v))
        pl.when(jnp.logical_not(at.has_high))(lambda: add_down(v))

    near_low = z < planes - 1 - z

    def stage(o, flag, do):
        there = jnp.logical_and(o >= 0, o < chunks)
        pl.when(jnp.logical_and(there, flag))(lambda: do(o))

    far = jnp.maximum(z, planes - 1 - z)

    def older(j):
        stage(j - far, jnp.logical_and(near_low, at.has_high), add_down)
        stage(j - far, jnp.logical_and(jnp.logical_not(near_low), at.has_low), add_up)

    def tick(j):
        older(j)
        near = planes - 1 - far
        stage(j - near, jnp.logical_and(near_low, at.has_low), add_up)
        stage(j - near, jnp.logical_and(jnp.logical_not(near_low), at.has_high), add_down)
        stage(j - far, far >= 0, give)

    last = jnp.int32(chunks - 1)

    def last_passes(first):
        @pl.when(between)
        def _():
            older(first)
            pl.when(near_low)(lambda: up_pass(last))
            down_pass(last)
            pl.when(jnp.logical_not(near_low))(lambda: up_pass(last))
            stage(first - far, far >= 0, give)

    def last_ticks(first):
        @pl.when(between)
        def _():
            up_last(last)
            down_last(last)
            give(last)

        @pl.when(jnp.logical_not(between))
        def _():
            for j in range(first, chunks + planes - 1):
                older(j)
                stage(j - far, far >= 0, give)

    part_rows = rows // 2

    def half_of(buffer, block, which_half):
        return buffer.at[block, pl.ds(which_half * part_rows, part_rows), :]

    def all_copy(buffer, which, i):
        block, which_half, to = (
            (at.block, 0, at.across if which < 2 else at.beside),
            (at.block, 1, at.across),
            (at.block, 1, at.beside),
            (at.block, 0, at.beside if which < 2 else at.across),
            (at.across_block, 0, at.beside)
            if which < 2
            else (at.beside_block, 0, at.across),
            (at.across_block, 1, at.beside),
        )[i]
        ref = half_of(buffer, block, which_half)
        return remote(ref, ref, all_send.at[which, i], all_recv.at[which, i], to)

    def all_landed(buffer, which, i):
        block, which_half = (
            (at.across_block if which < 2 else at.beside_block, 0),
            (at.across_block, 1),
            (at.beside_block, 1),
            (at.beside_block if which < 2 else at.across_block, 0),
            (at.far_block, 0),
            (at.far_block, 1),
        )[i]
        ref = half_of(buffer, block, which_half)
        remote(
            ref, ref, all_send.at[which, i], all_recv.at[which, i], at.across
        ).wait_recv()

    def all_start(buffer, which):
        for i in range(4):
            all_copy(buffer, which, i).start()

    def all_pass(buffer, which):
        for i in range(2):
            all_landed(buffer, which, i)
            all_copy(buffer, which, 4 + i).start()

    def all_wait(buffer, which):
        for i in range(2, 6):
            all_landed(buffer, which, i)

    def near_wait(buffer, which):
        all_landed(buffer, which, 3)

    def far_wait(buffer, which):
        for i in (2, 4, 5):
            all_landed(buffer, which, i)

    def all_done(buffer, which):
        for i in range(6):
            all_copy(buffer, which, i).wait_send()

    def part_copy(source, target, which, i):
        block, which_half, slot, to = (
            (at.far_block, 0, 2, at.beside),
            (at.far_block, 1, 2, at.across),
            (at.beside_block, 0, 0, at.beside),
            (at.across_block, 1, 1, at.across),
            (at.across_block, 0, 1, at.across),
            (at.beside_block, 1, 0, at.beside),
        )[i]
        return remote(
            half_of(source, block, which_half),
            half_of(target, slot, which_half),
            part_send.at[which, i],
            part_recv.at[which, i],
            to,
        )

    def part_start(source, target, which):
        for i in range(4):
            part_copy(source, target, which, i).start()

    def part_pass(source, target, which):
        for i, block in enumerate((at.across_block, at.beside_block)):
            part_copy(source, target, which, i).wait_recv()
            here = pl.ds(i * part_rows, part_rows)
            total = source[block, here, :].astype(jnp.float32)
            total = total + target[2, here, :].astype(jnp.float32)
            source[block, here, :] = total.astype(jnp.bfloat16)
            part_copy(source, target, which, 4 + i).start()

    def part_wait(source, target, which):
        for i in range(2, 6):
            part_copy(source, target, which, i).wait_recv()

    def part_done(source, target, which):
        for i in range(6):
            part_copy(source, target, which, i).wait_send()

    tile = 48

    def by_rows(body):
        def run(i, carry):
            body(pl.ds(pl.multiple_of(i * tile, tile), tile))
            return carry

        lax.fori_loop(0, rows // tile, run, 0)

    def scale_of(hidden):
        return lax.rsqrt(jnp.mean(hidden * hidden, axis=-1, keepdims=True) + EPSILON)

    def summed(source, target, span):
        total = source[at.block, span, :].astype(jnp.float32)
        for i in range(2):
            total = total + target[i, span, :].astype(jnp.float32)
        return total

    def back_through_norm(grad, hidden, gain, row):
        scale = scale_of(hidden)
        weighted = grad * gain
        inner = jnp.sum(weighted * hidden, axis=-1, keepdims=True)
        small[row : row + 1, :] += jnp.sum(grad * hidden * scale, axis=0, keepdims=True)
        return scale * weighted - hidden * (scale * scale * scale) * inner / width

    def transposed(buffer, k):
        def one(p, carry):
            cols = pl.ds(pl.multiple_of(p * wide, wide), wide)
            block = buffer[:, :, cols].reshape(4 * rows, wide).T
            w[k, p] = block.reshape(2, 2, share, 4 * rows)
            return carry

        lax.fori_loop(0, planes, one, 0)

    def whole(k, low, high):
        return w[k, :, :, :, :, low:high].reshape(planes * wide, high - low)

    def two_planes(k, q, low, high):
        return w[k, pair(q), :, :, :, low:high].reshape(2 * wide, high - low)

    def pair(t):
        return pl.ds(2 * t, 2)

    def two_columns(q):
        return pl.ds(pl.multiple_of(q * 2 * wide, 2 * wide), 2 * wide)

    def weight_grad(turned, grads, k, span):
        def some(q, carry):
            here = pair(q)
            out = dot(w[turned, here].reshape(2 * wide, 4 * rows), grads).astype(jnp.bfloat16)
            w[k, here, :, :, :, span] = out.reshape(2, 2, 2, share, grads.shape[1])
            return carry

        if grads.shape[1] <= PART:
            out = dot(w[turned].reshape(planes * wide, 4 * rows), grads).astype(jnp.bfloat16)
            w[k, :, :, :, :, span] = out.reshape(planes, 2, 2, share, grads.shape[1])
        else:
            lax.fori_loop(0, planes // 2, some, 0)

    halo[...] = jnp.zeros_like(halo)
    barrier = pltpu.get_barrier_semaphore()
    signal(barrier, at.beside)

    def greet(t, carry):
        signal(barrier, (lax.rem(at.me + t, count), at.x))
        return carry

    lax.fori_loop(1, count, greet, 0)
    pl.semaphore_wait(barrier, count)

    def gain_copy(t):
        other = lax.rem(at.me + t, count)
        return remote(
            gains_here,
            gains_in.at[at.me],
            gain_send.at[t],
            gain_recv.at[t],
            (other, at.x),
        )

    def gain_start(t, carry):
        gain_copy(t).start()
        return carry

    def gain_wait(t, carry):
        gain_copy(t).wait()
        return carry

    lax.fori_loop(1, count, gain_start, 0)
    begin(0)
    begin(1)
    e_copy = pltpu.make_async_copy(d_out, e_all.at[at.block], keep_sem.at[0])
    e_copy.start()
    small[...] = jnp.zeros_like(small)
    gains_in[at.me] = gains_here[...]
    lax.fori_loop(1, count, gain_wait, 0)
    for d in range(count):
        found = gains_in[d].astype(jnp.float32)[0:8, :share]
        gains[:, d * share : (d + 1) * share] = found
    channel_columns = pl.ds(pl.multiple_of(at.block * channels, channels), channels)
    taps[...] = gains[:, channel_columns]

    def first_norm(span):
        hidden = tokens[span, :].astype(jnp.float32)
        n_one[at.block, span, :] = (hidden * scale_of(hidden) * gains[0:1, :]).astype(jnp.bfloat16)

    by_rows(first_norm)
    all_start(n_one, 0)
    own(0)
    own(1)
    begin(2)
    relay(0, 1)
    relay(1, 1)
    all_pass(n_one, 0)
    e_copy.wait()
    all_start(e_all, 1)
    begin(3)
    relay(0, 2)
    relay(1, 2)
    own(2)
    all_pass(e_all, 1)
    for k in range(4, chunks):
        begin(k)
    for t in range(3, planes):
        relay(0, t)
    core_wait(0)
    all_wait(n_one, 0)

    def project_c(t, carry):
        normed = n_one[pair(t)].reshape(2 * rows, width)
        c_part = dot(normed, whole(0, 0, channels))
        total_a[pair(t), :, channels : 2 * channels] = c_part.reshape(2, rows, channels)
        return carry

    def project_b_x(t, carry):
        normed = n_one[pair(t)].reshape(2 * rows, width)
        b_x = dot(normed, whole(1, 0, 2 * channels)).reshape(2, rows, 2 * channels)
        total_a[pair(t), :, 0:channels] = b_x[:, :, :channels]
        total_a[pair(t), :, 2 * channels : 3 * channels] = b_x[:, :, channels:]
        product = (b_x[:, :, :channels] * b_x[:, :, channels:]).astype(jnp.bfloat16)
        gated[pair(t), 8 : 8 + rows, :] = product.astype(jnp.float32)
        return carry

    lax.fori_loop(0, 2, project_c, 0)
    for t in range(3, planes):
        relay(1, t)
    own(3)
    core_wait(1)
    lax.fori_loop(0, 2, project_b_x, 0)

    def halo_core(which, edge):
        return remote(
            edge, halo.at[2 * which], halo_send.at[2 * which], halo_recv.at[2 * which], at.core
        )

    def halo_plane(which, edge, target):
        return remote(
            edge,
            halo.at[2 * which + 1],
            halo_send.at[2 * which + 1],
            halo_recv.at[2 * which + 1],
            target,
        )

    tail = gated.at[:, pl.ds(rows, 8), :]
    halo_core(0, tail).start()
    pl.when(at.gives_next)(lambda: halo_plane(0, tail, at.next).start())
    halo_core(0, tail).wait_recv()
    pl.when(at.gives_last)(lambda: halo_plane(0, tail, at.last).wait_recv())
    for group in range(2):

        @pl.when(at.is_last)
        def _():
            gated[2 * group, 0:8, :] = halo[0, 2 * group]
            gated[2 * group + 1, 0:8, :] = halo[0, 2 * group + 1]

        @pl.when(at.is_first)
        def _():
            gated[2 * group, 0:8, :] = halo[1, 2 * group + 1]
            gated[2 * group + 1, 0:8, :] = halo[0, 2 * group]

    def start_of(block):
        return lax.rem((z * 4 + lax.rem(block, 2) * 2 + c) * rows, seq_len)

    def place_in(block, ahead):
        place = start_of(block) + ahead + lax.broadcasted_iota(jnp.int32, (rows, channels), 0)
        return jnp.where(place >= seq_len, place - seq_len, place)

    def convolve(b, carry):
        place = place_in(b, 0)
        conv = jnp.zeros((rows, channels), jnp.float32)
        for j in range(3):
            moved = gated[b, 6 + j : 6 + j + rows, :]
            conv = conv + jnp.where(place >= 2 - j, moved, 0.0) * taps[2 + j : 3 + j, :]
        total_a[b, :, 3 * channels : 4 * channels] = conv
        mixed[b] = (total_a[b, :, channels : 2 * channels] * conv).astype(jnp.bfloat16)
        return carry

    lax.fori_loop(0, 4, convolve, 0)

    def branch(i, carry):
        t, q = lax.div(i, planes // 2), lax.rem(i, planes // 2)
        left = mixed[pair(t)].reshape(2 * rows, channels)
        out = times_transposed(left, two_planes(0, q, channels, 2 * channels))
        out = out.reshape(2, rows, 2 * wide).astype(jnp.bfloat16)
        sent_a[pair(t), :, two_columns(q)] = out
        return carry

    lax.fori_loop(0, planes, branch, 0)
    part_start(sent_a, got_a, 0)
    gather_done(0)
    gather_done(1)
    keep_weights = pltpu.make_async_copy(w.at[pl.ds(0, 2)], kept_weights, keep_sem.at[1])
    keep_mixer = pltpu.make_async_copy(total_a, kept_mixer, keep_sem.at[2])
    keep_weights.start()
    keep_mixer.start()
    pass_on(2, 1)
    part_pass(sent_a, got_a, 0)
    for k in range(4, chunks):
        own_at_end(k)
    own_between(4)
    for t in range(2, planes):
        pass_on(2, t)
    own_between(5)
    keep_weights.wait()
    keep_mixer.wait()
    total_a[...] = jnp.zeros_like(total_a)
    total_b[...] = jnp.zeros_like(total_b)
    all_wait(e_all, 1)
    transposed(e_all, 1)
    part_wait(sent_a, got_a, 0)

    def second_norm(span):
        hidden = tokens[span, :].astype(jnp.float32) + summed(sent_a, got_a, span)
        hidden_one[span, :] = hidden
        n_two[at.block, span, :] = (hidden * scale_of(hidden) * gains[1:2, :]).astype(jnp.bfloat16)

    by_rows(second_norm)
    all_start(n_two, 2)
    part_done(sent_a, got_a, 0)
    pass_on(3, 1)
    all_pass(n_two, 2)
    for t in range(2, planes):
        pass_on(3, t)
    pass_on(4, 1)
    take_last(2)
    near_wait(n_two, 2)

    def cast(source, target):
        def run(b, carry):
            target[b] = source[b].astype(jnp.bfloat16)
            return carry

        lax.fori_loop(0, 4, run, 0)

    def feed_forward(k):
        def half(j, carry):
            t = lax.rem(at.x + j, 2)

            @pl.when(jnp.logical_and(k == 2, j == 1))
            def _():
                far_wait(n_two, 2)

            normed = n_two[pair(t)].reshape(2 * rows, width)
            both = dot(normed, whole(k, 0, 2 * step_cols))
            d_active = dot(
                e_all[pair(t)].reshape(2 * rows, width), whole(k, 2 * step_cols, 3 * step_cols)
            )
            gate, upper = both[:, :step_cols], both[:, step_cols:]
            sigma = jax.nn.sigmoid(gate)
            soft = gate * sigma
            here = pl.ds(pl.multiple_of(t * 2 * rows, 2 * rows), 2 * rows)
            active[here, :] = (soft * upper).astype(jnp.bfloat16)
            d_gate_up[here, step_cols:] = (d_active * soft).astype(jnp.bfloat16)
            d_gate_up[here, :step_cols] = (
                d_active * upper * sigma * (1.0 + gate * (1.0 - sigma))
            ).astype(jnp.bfloat16)

            def spread(q, inner):
                back = times_transposed(d_gate_up[here, :], two_planes(k, q, 0, 2 * step_cols))
                total_b[pair(t), :, two_columns(q)] += back.reshape(2, rows, 2 * wide)
                out = times_transposed(
                    active[here, :], two_planes(k, q, 2 * step_cols, 3 * step_cols)
                )
                total_a[pair(t), :, two_columns(q)] += out.reshape(2, rows, 2 * wide)
                return inner

            lax.fori_loop(0, planes // 2, spread, 0)
            return carry

        lax.fori_loop(0, 2, half, 0)

        @pl.when(k == chunks - 1)
        def _():
            cast(total_b, sent_a)
            part_start(sent_a, got_a, 2)

        gather_done(k)
        pl.when(k == 2)(lambda: transposed(n_two, 0))

        def grads(n, carry):
            span = pl.ds(pl.multiple_of(n * step_cols, step_cols), step_cols)
            weight_grad(0, d_gate_up[:, span], k, span)
            return carry

        lax.fori_loop(0, 2, grads, 0)
        weight_grad(1, active[...], k, pl.ds(2 * step_cols, step_cols))

    def one_part(i, carry):
        k = i + 2
        core_wait(k)
        feed_forward(k)
        core_start(i)
        pl.when(k + 2 < chunks)(lambda: pass_on(k + 2, 2))
        pl.when(k + 3 < chunks)(lambda: pass_on(k + 3, 1))
        pl.when(i == 0)(lambda: own_between(6))
        pl.when(i == 0)(lambda: own_between(7))
        pl.when(i == 1)(lambda: own_between(8))
        pl.when(k + 1 < chunks)(lambda: take_last(k + 1))
        first_hop(i)
        now = jnp.logical_and(i >= 3, i < parts - 1)
        pl.when(jnp.logical_and(between, now))(lambda: tick(i - 2))

        @pl.when(k + 1 < chunks)
        def _():
            for t in range(3, planes):
                pass_on(k + 1, t)

        return carry

    lax.fori_loop(0, parts, one_part, 0)

    restore_weights = pltpu.make_async_copy(kept_weights, w.at[pl.ds(0, 2)], keep_sem.at[1])
    restore_weights.start()

    cast(total_a, sent_b)
    restore_mixer = pltpu.make_async_copy(kept_mixer, total_a, keep_sem.at[2])
    restore_mixer.start()
    part_pass(sent_a, got_a, 2)
    pl.when(jnp.logical_not(between))(lambda: tick(3))
    tick(4)
    part_wait(sent_a, got_a, 2)

    def through_second(span):
        grad = back_through_norm(
            summed(sent_a, got_a, span), hidden_one[span, :], gains[1:2, :], 1
        )
        grad = e_all[at.block, span, :].astype(jnp.float32) + grad
        d_hidden[span, :] = grad
        f_all[at.block, span, :] = grad.astype(jnp.bfloat16)

    by_rows(through_second)
    all_done(n_two, 2)
    all_start(f_all, 3)
    part_done(sent_a, got_a, 2)
    all_pass(f_all, 3)
    part_start(sent_b, n_two, 1)
    sum_done(0)
    transposed(n_one, 2)
    all_done(n_one, 0)
    restore_weights.wait()
    restore_mixer.wait()
    tick(5)
    all_wait(f_all, 3)

    def into_mixer(t, carry):
        grad = f_all[pair(t)].reshape(2 * rows, width)
        d_mixed = dot(grad, whole(0, channels, 2 * channels)).reshape(2, rows, channels)
        conv = total_a[pair(t), :, 3 * channels : 4 * channels]
        c_part = total_a[pair(t), :, channels : 2 * channels]
        n_one[pair(t), :, 2 * channels : 3 * channels] = (d_mixed * conv).astype(jnp.bfloat16)
        d_conv[pair(t), 0:rows, :] = d_mixed * c_part
        return carry

    lax.fori_loop(0, 2, into_mixer, 0)
    head = d_conv.at[:, pl.ds(0, 8), :]
    halo_core(1, head).start()
    pl.when(at.gives_last)(lambda: halo_plane(1, head, at.last).start())

    def from_c(i, carry):
        t, q = lax.div(i, planes // 2), lax.rem(i, planes // 2)
        grad = n_one[pair(t), :, 2 * channels : 3 * channels].reshape(2 * rows, channels)
        out = times_transposed(grad, two_planes(0, q, 0, channels))
        total_b[pair(t), :, two_columns(q)] = out.reshape(2, rows, 2 * wide)
        return carry

    lax.fori_loop(0, planes, from_c, 0)
    sum_done(1)
    transposed(f_all, 3)

    d_c = n_one[:, :, 2 * channels : 3 * channels].reshape(4 * rows, channels)
    weight_grad(2, d_c, 0, pl.ds(0, channels))
    weight_grad(3, mixed[...].reshape(4 * rows, channels), 0, pl.ds(channels, channels))
    core_start(jnp.int32(parts))
    tick(6)
    halo_core(1, head).wait_recv()
    pl.when(at.gives_next)(lambda: halo_plane(1, head, at.next).wait_recv())
    for group in range(2):

        @pl.when(at.is_first)
        def _():
            d_conv[2 * group, rows : rows + 8, :] = halo[2, 2 * group]
            d_conv[2 * group + 1, rows : rows + 8, :] = halo[2, 2 * group + 1]

        @pl.when(at.is_last)
        def _():
            d_conv[2 * group, rows : rows + 8, :] = halo[2, 2 * group + 1]
            d_conv[2 * group + 1, rows : rows + 8, :] = halo[3, 2 * group]

    def convolve_back(b, carry):
        place = place_in(b, 0)
        d_gated = jnp.zeros((rows, channels), jnp.float32)
        for j in range(3):
            ahead = 2 - j
            moved = jnp.where(
                place_in(b, ahead) >= ahead, d_conv[b, ahead : ahead + rows, :], 0.0
            )
            d_gated = d_gated + moved * taps[2 + j : 3 + j, :]
            product = d_conv[b, 0:rows, :] * gated[b, 6 + j : 6 + j + rows, :]
            small[2 + j : 3 + j, channel_columns] += jnp.sum(
                jnp.where(place >= ahead, product, 0.0), axis=0, keepdims=True
            )
        x_part = total_a[b, :, 2 * channels : 3 * channels]
        n_one[b, :, 0:channels] = (d_gated * x_part).astype(jnp.bfloat16)
        b_part = total_a[b, :, 0:channels]
        n_one[b, :, channels : 2 * channels] = (d_gated * b_part).astype(jnp.bfloat16)
        return carry

    lax.fori_loop(0, 4, convolve_back, 0)
    first_hop(jnp.int32(parts))

    def d_normed(i, carry):
        t, q = lax.div(i, planes // 2), lax.rem(i, planes // 2)
        grad = n_one[pair(t), :, 0 : 2 * channels].reshape(2 * rows, 2 * channels)
        out = times_transposed(grad, two_planes(1, q, 0, 2 * channels))
        out = total_b[pair(t), :, two_columns(q)] + out.reshape(2, rows, 2 * wide)
        sent_a[pair(t), :, two_columns(q)] = out.astype(jnp.bfloat16)
        return carry

    lax.fori_loop(0, planes, d_normed, 0)
    part_start(sent_a, got_a, 3)

    def b_and_x_weight(n, carry):
        span = pl.ds(pl.multiple_of(n * channels, channels), channels)
        grad = n_one[:, :, span].reshape(4 * rows, channels)
        weight_grad(2, grad, 1, span)
        return carry

    lax.fori_loop(0, 2, b_and_x_weight, 0)
    core_start(jnp.int32(parts + 1))
    tick(7)
    part_pass(sent_a, got_a, 3)
    first_hop(jnp.int32(parts + 1))
    part_pass(sent_b, n_two, 1)
    tick(8)
    last_passes(9)
    part_wait(sent_a, got_a, 3)

    def through_first(span):
        hidden = tokens[span, :].astype(jnp.float32)
        grad = back_through_norm(summed(sent_a, got_a, span), hidden, gains[0:1, :], 0)
        sent_a[at.block, span, :] = (d_hidden[span, :] + grad).astype(jnp.bfloat16)

    by_rows(through_first)
    d_tokens_copy = pltpu.make_async_copy(sent_a.at[at.block], d_tokens, keep_sem.at[3])
    d_tokens_copy.start()

    def small_copy(i, to):
        return remote(small, small_in.at[i], small_send.at[i], small_recv.at[i], to)

    def small_plane(t):
        to = lax.rem(at.me + 4 * t, count)
        return remote(
            small, small_in.at[2 + t], small_send.at[2 + t], small_recv.at[2 + t], (to, at.x)
        )

    small_copy(0, at.core).start()
    for i, (here, following) in enumerate(
        ((at.core, at.beside), (at.beside, at.across), (at.across, None))
    ):
        small_copy(i, here).wait()
        small[...] += small_in[i]
        if following is not None:
            small_copy(i + 1, following).start()
    for t in range(1, planes):
        small_plane(t).start()
    last_ticks(9)
    part_wait(sent_b, n_two, 1)

    def last_out(span):
        total = hidden_one[span, :] + summed(sent_b, n_two, span)
        sent_b[at.block, span, :] = total.astype(jnp.bfloat16)

    by_rows(last_out)
    result_copy = pltpu.make_async_copy(sent_b.at[at.block], result, keep_sem.at[4])
    result_copy.start()
    for t in range(1, planes):
        small_plane(t).wait()
    for t in range(1, planes):
        small[...] += small_in[2 + t]

    d_tokens_copy.wait()
    result_copy.wait()
    part_done(sent_a, got_a, 3)
    all_done(e_all, 1)
    part_done(sent_b, n_two, 1)
    all_done(f_all, 3)
    halo_core(0, tail).wait_send()
    halo_core(1, head).wait_send()
    pl.when(at.gives_next)(lambda: halo_plane(0, tail, at.next).wait_send())
    pl.when(at.gives_last)(lambda: halo_plane(1, head, at.last).wait_send())
    for v in range(2, chunks):
        sum_done(v)


def one_kernel(planes, seq_len, weights, tokens, d_out, gains):
    chunks, _, share, cols = weights.shape
    parts = chunks - 2
    rows, width = tokens.shape
    channels = width // 4
    low, full = jnp.bfloat16, jnp.float32
    shape = jax.ShapeDtypeStruct
    vmem, anywhere = pl.BlockSpec(memory_space=pltpu.VMEM), pl.BlockSpec(memory_space=pl.ANY)
    dma = pltpu.SemaphoreType.DMA
    block = (4, rows, width)
    return pl.pallas_call(
        functools.partial(kernel, planes, parts, seq_len),
        out_shape=(
            shape((rows, width), low),
            shape((rows, width), low),
            shape((chunks, share, cols), low),
            shape((chunks, share, cols), low),
            shape((8, width), full),
            shape((2, planes, 2, 2, share, cols), low),
            shape(block, full),
        ),
        in_specs=[anywhere, vmem, anywhere, vmem],
        out_specs=[anywhere, anywhere, anywhere, anywhere, vmem, anywhere, anywhere],
        scratch_shapes=[
            pltpu.VMEM((chunks, planes, 2, 2, share, cols), low),
            pltpu.VMEM((2, planes, 2, share, cols), low),
            pltpu.VMEM((chunks, 2, share, cols), low),
            pltpu.VMEM(block, low),
            pltpu.VMEM(block, low),
            pltpu.VMEM(block, low),
            pltpu.VMEM(block, low),
            pltpu.VMEM(block, low),
            pltpu.VMEM(block, low),
            pltpu.VMEM(block, full),
            pltpu.VMEM(block, full),
            pltpu.VMEM((3, rows, width), low),
            pltpu.VMEM((4, rows + 8, channels), full),
            pltpu.VMEM((4, rows + 8, channels), full),
            pltpu.VMEM((4, rows, channels), low),
            pltpu.VMEM((4 * rows, PART), low),
            pltpu.VMEM((4 * rows, 2 * PART), low),
            pltpu.VMEM((rows, width), full),
            pltpu.VMEM((rows, width), full),
            pltpu.VMEM((4, 4, 8, channels), full),
            pltpu.VMEM((4 * planes,) + gains.shape, low),
            pltpu.VMEM((8, width), full),
            pltpu.VMEM((8, channels), full),
            pltpu.VMEM((2 + planes, 8, width), full),
            dma((4 * planes,)),
            dma((4 * planes,)),
            dma((2 + planes,)),
            dma((2 + planes,)),
            dma((chunks,)),
            dma((chunks,)),
            dma((chunks,)),
            dma((chunks, 2, planes)),
            dma((chunks, planes)),
            dma((chunks, planes)),
            dma((chunks, planes)),
            dma((chunks,)),
            dma((chunks,)),
            pltpu.SemaphoreType.REGULAR,
            dma((chunks, 2, planes)),
            dma((chunks, 2, planes)),
            pltpu.SemaphoreType.REGULAR((2,)),
            dma((chunks,)),
            dma((chunks,)),
            dma((chunks,)),
            dma((4, 6)),
            dma((4, 6)),
            dma((4, 6)),
            dma((4, 6)),
            dma((4,)),
            dma((4,)),
            dma((5,)),
        ],
        compiler_params=pltpu.CompilerParams(
            collective_id=0, has_side_effects=True, vmem_limit_bytes=64 * 1024 * 1024
        ),
    )(weights, tokens, d_out, gains)


def split_kernel(hidden, parts, gate, up, down, in_weight, out_weight, weights):
    channels = out_weight.shape[1] // 2
    left = parts * PART - hidden
    blank = jnp.zeros((gate.shape[0], left), jnp.bfloat16)
    for which, source in enumerate((gate, up, down)):
        here = pl.ds(which * PART, PART)
        for half in range(2):
            for part in range(parts):
                low = half * hidden + part * PART
                if part < parts - 1 or left == 0:
                    weights[2 + part, half, :, here] = source[:, low : low + PART]
                else:
                    last = source[:, low : low + PART - left]
                    weights[2 + part, half, :, here] = jnp.concatenate([last, blank], axis=1)
    for half in range(2):
        span = slice(half * channels, (half + 1) * channels)
        weights[0, half, :, 0:channels] = in_weight[1, :, span]
        weights[0, half, :, channels:] = out_weight[:, span]
        weights[1, half, :, 0:channels] = in_weight[0, :, span]
        weights[1, half, :, channels:] = in_weight[2, :, span]


def split(gate, up, down, in_weight, out_weight, step=48):
    share, columns = gate.shape
    hidden = columns // 2
    parts = -(-hidden // PART)
    by_rows = pl.BlockSpec((step, columns), lambda i: (i, 0))
    cols = 3 * PART
    return pl.pallas_call(
        functools.partial(split_kernel, hidden, parts),
        grid=(share // step,),
        out_shape=jax.ShapeDtypeStruct((parts + 2, 2, share, cols), jnp.bfloat16),
        in_specs=[
            by_rows,
            by_rows,
            by_rows,
            pl.BlockSpec((3, step, in_weight.shape[2]), lambda i: (0, i, 0)),
            pl.BlockSpec((step, out_weight.shape[1]), lambda i: (i, 0)),
        ],
        out_specs=pl.BlockSpec((parts + 2, 2, step, cols), lambda i: (0, 0, i, 0)),
    )(gate, up, down, in_weight, out_weight)


def join_kernel(hidden, parts, own, other, gate, up, down, in_weight, out_weight):
    channels = out_weight.shape[1] // 2
    side = lax.rem(lax.div(lax.axis_index("seq"), 2), 2)

    def put(half, source):
        for which, target in enumerate((gate, up, down)):
            pieces = [
                source[2 + part, :, which * PART : (which + 1) * PART].astype(jnp.float32)
                for part in range(parts)
            ]
            whole = jnp.concatenate(pieces, axis=1)[:, :hidden]
            target[:, half * hidden : (half + 1) * hidden] = whole
        span = slice(half * channels, (half + 1) * channels)
        in_weight[1, :, span] = source[0, :, 0:channels].astype(jnp.float32)
        out_weight[:, span] = source[0, :, channels:].astype(jnp.float32)
        in_weight[0, :, span] = source[1, :, 0:channels].astype(jnp.float32)
        in_weight[2, :, span] = source[1, :, channels:].astype(jnp.float32)

    @pl.when(side == 0)
    def _():
        put(0, own)
        put(1, other)

    @pl.when(side == 1)
    def _():
        put(0, other)
        put(1, own)


def join(own, other, hidden, channels, step=48):
    chunks, share, cols = own.shape
    parts = chunks - 2
    full = jnp.float32
    part = pl.BlockSpec((chunks, step, cols), lambda i: (0, i, 0))
    by_rows = pl.BlockSpec((step, 2 * hidden), lambda i: (i, 0))
    shape = jax.ShapeDtypeStruct
    return pl.pallas_call(
        functools.partial(join_kernel, hidden, parts),
        grid=(share // step,),
        out_shape=(
            shape((share, 2 * hidden), full),
            shape((share, 2 * hidden), full),
            shape((share, 2 * hidden), full),
            shape((3, share, 2 * channels), full),
            shape((share, 2 * channels), full),
        ),
        in_specs=[part, part],
        out_specs=(
            by_rows,
            by_rows,
            by_rows,
            pl.BlockSpec((3, step, 2 * channels), lambda i: (0, i, 0)),
            pl.BlockSpec((step, 2 * channels), lambda i: (i, 0)),
        ),
    )(own, other)


def on_device(
    tokens,
    norm1_gain,
    in_weight,
    conv_kernel,
    out_weight,
    norm2_gain,
    gate_weight,
    up_weight,
    down_weight,
    d_out,
):
    planes = lax.axis_size("seq") // 4
    here = lax.axis_index("seq")
    rows, width = tokens.shape[1:]
    share = gate_weight.shape[0]
    channels = in_weight.shape[2] // 2
    hidden = gate_weight.shape[1] // 2

    gains = jnp.concatenate([norm1_gain[None], norm2_gain[None], conv_kernel.T], axis=0)
    gains = jnp.pad(gains, ((0, 16 - gains.shape[0]), (0, 128 - share)))

    weights = split(
        gate_weight, up_weight, down_weight, jnp.swapaxes(in_weight, 0, 1), out_weight
    )
    result, d_tokens, own_grad, other_grad, small, _, _ = one_kernel(
        planes,
        lax.axis_size("seq") * rows // SEQS,
        weights,
        tokens[0],
        d_out[0],
        gains,
    )
    d_gate, d_up, d_down, d_in, d_branch = join(own_grad, other_grad, hidden, channels)
    sums = lax.dynamic_slice_in_dim(small, here * share, share, 1)
    return (
        result[None],
        d_tokens[None],
        sums[0],
        jnp.swapaxes(d_in, 0, 1),
        sums[2:5].T,
        d_branch,
        sums[1],
        d_gate,
        d_up,
        d_down,
    )


def fits(mesh):
    return mesh.shape["seq"] <= 16


def solution(mesh):
    return jax.shard_map(
        on_device if fits(mesh) else plain_on_device,
        mesh=mesh,
        in_specs=(
            P("fsdp", "seq", None),
            P("seq"),
            P("seq", None, "fsdp"),
            P("seq", None),
            P("seq", "fsdp"),
            P("seq"),
            P("seq", "fsdp"),
            P("seq", "fsdp"),
            P("seq", "fsdp"),
            P("fsdp", "seq", None),
        ),
        out_specs=(
            P("fsdp", "seq", None),
            P("fsdp", "seq", None),
            P("seq"),
            P("seq", None, "fsdp"),
            P("seq", None),
            P("seq", "fsdp"),
            P("seq"),
            P("seq", "fsdp"),
            P("seq", "fsdp"),
            P("seq", "fsdp"),
        ),
        check_vma=False,
    )
```
